32 devices in a mesh: pipe: 2 (over core), dp: 4 (over z), tensor: 4 (over y, x).
Axes of the slice: x: 2, y: 2, z: 4, core: 2. Of those that a mesh axis runs over, the one named last changes fastest.
Arguments:
- boundary: bfloat16 [2, 8, 128, 512], P('pipe', 'dp', 'tensor'), may hold values from -10 to 10
- lengths: int32 [8], P('dp'), may hold values from 32 to 128, as said below
- batch_of: int32 [8], P('dp'), may hold values from 0 to 1, as said below
- mats: bfloat16 [2, 8, 512, 512], P('pipe', None, 'dp', 'tensor'), may hold values from -0.25 to 0.25
- ffw: bfloat16 [2, 4, 512, 2048], P('pipe', None, 'dp', 'tensor'), may hold values from -0.25 to 0.25
- vec_model: bfloat16 [2, 14, 512], P('pipe', None, ('dp', 'tensor')), may hold values from -1 to 1
- vec_inner: bfloat16 [2, 39, 512], P('pipe', None, ('tensor', 'dp')), may hold values from -1 to 1
- vec_ff: bfloat16 [2, 2, 2048], P('pipe', None, ('tensor', 'dp')), may hold values from -1 to 1
Outputs:
- boundary_out: bfloat16 [2, 8, 128, 512], P('pipe', 'dp', 'tensor')
- mats_grad: float32 [2, 8, 512, 512], P('pipe', None, 'dp', 'tensor')
- ffw_grad: float32 [2, 4, 512, 2048], P('pipe', None, 'dp', 'tensor')
- vec_model_grad: float32 [2, 14, 512], P('pipe', None, ('dp', 'tensor'))
- vec_inner_grad: float32 [2, 39, 512], P('pipe', None, ('tensor', 'dp'))
- vec_ff_grad: float32 [2, 2, 2048], P('pipe', None, ('tensor', 'dp'))
The draws below stay inside these ranges and needn't reach their ends.
Inputs may be any that keep to these rules, and one draw needn't show every extreme that they name: `lengths`: some sequence has exactly 128 tokens and some exactly 32. `batch_of`: in each aligned block of 2 sequences (the sequences of one device) every micro-batch number stands exactly once.
All inputs are finite; a program needn't handle non-finite values.
Results may differ from the reference program's by a relative error of at most 0.03.
Values may be sent and summed in bfloat16 or wider, within the bound.
No kernel may reach another device: no remote copies, remote signals or barrier semaphores. Data moves between devices by JAX's collectives and lax.ppermute only.
A program may use at most 128 MiB of HBM per device.

```python
from functools import partial
import jax
import jax.numpy as jnp
from jax import lax

D = 512
HEADS = 8
HEAD_DIM = 64
FF = 2048
KSIZE = 31
MB = 2
LEN = 128
SEQS = 8


def draw_boundary(key, part):
    key = jax.random.fold_in(key, 11)
    noise_key, offset_key = jax.random.split(key)
    shape = (2, SEQS, LEN, D)
    noise = jax.random.truncated_normal(noise_key, -5.0, 5.0, shape, jnp.float32)
    offsets = jax.random.truncated_normal(offset_key, -3.0, 3.0, (SEQS, 1, D), jnp.float32)
    rising = 0.5 + jnp.arange(SEQS).astype(jnp.float32) / SEQS
    starts = noise[0] + offsets * rising[:, None, None]
    return jnp.stack([starts, noise[1]]).astype(jnp.bfloat16)


def draw_lengths(key, part):
    key = jax.random.fold_in(key, 12)
    pick_key, value_key = jax.random.split(key)
    counts = jax.random.randint(value_key, (SEQS,), LEN // 4, LEN + 1)
    chosen = jax.random.permutation(pick_key, SEQS)
    counts = counts.at[chosen[0]].set(LEN)
    counts = counts.at[chosen[1]].set(LEN // 4)
    return counts.astype(jnp.int32)


def draw_batch_of(key, part):
    key = jax.random.fold_in(key, 13)
    scores = jax.random.randint(key, (SEQS // MB, MB), 0, 1 << 20) * MB + jnp.arange(MB)[None, :]
    return jnp.argsort(scores, axis=1).reshape(SEQS).astype(jnp.int32)


def block_levels(key, shape, cuts, low, top_value):
    def one(dim, blocks):
        heights = jax.random.uniform(jax.random.fold_in(jax.random.fold_in(key, 6), dim), (blocks,), jnp.float32, low / len(cuts), top_value / len(cuts))
        return jnp.repeat(jnp.exp(heights), shape[dim] // blocks).reshape((-1,) + (1,) * (len(shape) - dim - 1))

    level = one(*cuts[0])
    for cut in cuts[1:]:
        level = level * one(*cut)
    return level


def bell_draw(own_key, extent, scale, bound, cuts=(), dtype=jnp.bfloat16):
    level = block_levels(own_key, extent, cuts, -0.22, 0.18) if cuts else 1.0
    array = jax.random.normal(own_key, extent, jnp.float32) * scale * level
    return jnp.minimum(jnp.maximum(array, -bound), bound).astype(dtype)


def setup_inputs(seed: int = 0) -> dict:
    key_list = jax.random.split(jax.random.key(seed), 9)
    boundary = draw_boundary(jax.random.fold_in(key_list[8], 71), 0)
    lengths = draw_lengths(jax.random.fold_in(key_list[8], 71), 0)
    batch_of = draw_batch_of(jax.random.fold_in(key_list[8], 71), 0)
    mats = bell_draw(key_list[3], (2, 8, D, D), D ** -0.5, 0.25, ((0, 2), (2, 4), (3, 4)))
    ffw = bell_draw(key_list[4], (2, 4, D, FF), D ** -0.5, 0.25, ((0, 2), (2, 4), (3, 4)))
    vec_model = bell_draw(key_list[5], (2, 14, D), 0.2, 1.0, ((0, 2), (2, 16)))
    vec_inner = bell_draw(key_list[6], (2, 8 + KSIZE, D), 0.2, 1.0, ((0, 2), (2, 16)))
    vec_ff = bell_draw(key_list[7], (2, 2, FF), 0.2, 1.0, ((0, 2), (2, 16)))
    return dict(boundary=boundary, lengths=lengths, batch_of=batch_of, mats=mats, ffw=ffw, vec_model=vec_model, vec_inner=vec_inner, vec_ff=vec_ff)


PRECISE = lax.Precision.HIGHEST
EPSILON = 1e-05
HUGE_NEG = -1000000000.0

@jax.custom_vjp
def low(v):
    return lax.optimization_barrier(v.astype(jnp.bfloat16)).astype(jnp.float32)

@jax.custom_vjp
def low_back(v):
    return v

def low_keep(v):
    return (low(v), None)

def low_pass(kept, grad):
    return (grad,)

def back_keep(v):
    return (v, None)

def back_low(kept, grad):
    return (low(grad),)
low.defvjp(low_keep, low_pass)
low_back.defvjp(back_keep, back_low)

def layer_norm(stream, gain, shift):
    centre = stream - lax.optimization_barrier(jnp.mean(stream, axis=-1, keepdims=True))
    spread = lax.optimization_barrier(jnp.mean(centre * centre, axis=-1, keepdims=True))
    return centre * lax.rsqrt(spread + EPSILON) * (1.0 + gain) + shift

def sinusoid(length, width):
    place = (length - 1 - jnp.arange(2 * length - 1)).astype(jnp.float32)
    index = jnp.arange(width // 2).astype(jnp.float32)
    rate = jnp.exp(index * (-2.0 * jnp.log(10000.0) / width))
    angle = place[:, None] * rate[None, :]
    return jnp.stack([jnp.sin(angle), jnp.cos(angle)], axis=-1).reshape(2 * length - 1, width)

def rel_shift(table):
    head_count, length, span = table.shape
    padded = jnp.pad(table, ((0, 0), (0, 0), (1, 0)))
    padded = padded.reshape(head_count, span + 1, length)[:, 1:]
    return padded.reshape(head_count, length, span)[:, :, :length]

def depthwise(mixed, taps):
    size = taps.shape[0]
    length = mixed.shape[-2]
    axis_time = mixed.ndim - 2
    widths = [(0, 0)] * axis_time + [(size // 2, size // 2), (0, 0)]
    padded = jnp.pad(mixed, widths)
    filtered = jnp.zeros_like(mixed)
    for tap_idx in range(size):
        filtered = filtered + taps[tap_idx] * lax.slice_in_dim(padded, tap_idx, tap_idx + length, axis=axis_time)
    return filtered

def project(values, weight):
    return jnp.einsum('bld,de->ble', values, weight, precision=PRECISE)

def project_back(values, weight):
    return jnp.einsum('ble,de->bld', values, weight, precision=PRECISE)

def feed_forward(stream, ff_mats, model_vec, hidden_vec, which, first_row):
    normed = low(layer_norm(stream, model_vec[first_row], model_vec[first_row + 1]))
    before = low_back(project(normed, ff_mats[2 * which]) + hidden_vec[which])
    active = low(jax.nn.silu(before))
    branch = low_back(project_back(active, ff_mats[2 * which + 1]) + model_vec[first_row + 2])
    return stream + 0.5 * branch

def one_sequence(pieces, rel_pos):
    query_u, query_v, key_rows, value_rows, key_mask = pieces
    direct = jnp.einsum('ihd,jhd->hij', query_u, key_rows, precision=PRECISE)
    relative = rel_shift(jnp.einsum('ihd,rhd->hir', query_v, rel_pos, precision=PRECISE))
    scores = low_back((direct + relative) * HEAD_DIM ** (-0.5))
    scores = jnp.where(key_mask[None, None, :] > 0.5, scores, HUGE_NEG)
    attn_probs = low(jax.nn.softmax(scores, axis=-1))
    context = jnp.einsum('hij,jhd->ihd', attn_probs, value_rows, precision=PRECISE)
    return low(low_back(context)).reshape(context.shape[0], -1)

def attend(stream, key_mask, rel_pos, matrices, model_vec, inner_vec):
    split_shape = (stream.shape[0], stream.shape[1], HEADS, HEAD_DIM)
    normed = low(layer_norm(stream, model_vec[3], model_vec[4]))
    query_rows = low_back(project(normed, matrices[0]) + inner_vec[0])
    query_u = low(query_rows + inner_vec[2]).reshape(split_shape)
    query_v = low(query_rows + inner_vec[3]).reshape(split_shape)
    key_rows = low(low_back(project(normed, matrices[1]))).reshape(split_shape)
    value_rows = low(low_back(project(normed, matrices[2]) + inner_vec[1])).reshape(split_shape)
    context = lax.map(jax.checkpoint(partial(one_sequence, rel_pos=rel_pos)), (query_u, query_v, key_rows, value_rows, key_mask))
    branch = low_back(project_back(context, matrices[3]) + model_vec[5])
    return stream + branch

def gated_unit(first_half, second_half, key_mask):
    return first_half * jax.nn.sigmoid(second_half) * key_mask[..., None]

def convolve(stream, key_mask, matrices, model_vec, inner_vec):
    normed = low(layer_norm(stream, model_vec[6], model_vec[7]))
    gate_in = low_back(project(normed, matrices[5]) + inner_vec[4])
    gate_sig = low_back(project(normed, matrices[6]) + inner_vec[5])
    mixed = gated_unit(gate_in, gate_sig, key_mask)
    filtered = depthwise(mixed, inner_vec[8:])
    inside = key_mask[..., None]
    token_count = jnp.sum(key_mask)
    chan_mean = lax.optimization_barrier(jnp.sum(inside * filtered, axis=(0, 1))) / token_count
    centre = filtered - chan_mean
    spread = lax.optimization_barrier(jnp.sum(inside * centre * centre, axis=(0, 1))) / token_count
    normal = centre * lax.rsqrt(spread + EPSILON) * (1.0 + inner_vec[6]) + inner_vec[7]
    active = low(jax.nn.silu(normal))
    branch = low_back(project_back(active, matrices[7]) + model_vec[8])
    return stream + branch

def conformer(stream, key_mask, rel_pos, matrices, ff_mats, model_vec, inner_vec, hidden_vec):
    stream = feed_forward(stream, ff_mats, model_vec, hidden_vec, 0, 0)
    stream = attend(stream, key_mask, rel_pos, matrices, model_vec, inner_vec)
    stream = convolve(stream, key_mask, matrices, model_vec, inner_vec)
    stream = feed_forward(stream, ff_mats, model_vec, hidden_vec, 1, 9)
    return layer_norm(stream, model_vec[12], model_vec[13])

def reference(boundary, lengths, batch_of, mats, ffw, vec_model, vec_inner, vec_ff):
    groups = SEQS // MB
    order = jnp.argsort(batch_of, stable=True).astype(jnp.int32)
    key_masks = (jnp.arange(LEN)[None, :] < lengths[order][:, None]).astype(jnp.float32).reshape(MB, groups, LEN)
    starts = boundary[0].astype(jnp.float32)[order].reshape(MB, groups, LEN, D)
    cotangent = boundary[1].astype(jnp.float32)[order].reshape(MB, groups, LEN, D)
    pos_table = low(sinusoid(LEN, D))

    def whole(begin_rows, matrices, ff_mats, model_vec, inner_vec, hidden_vec):
        positions = [low(jnp.dot(pos_table, matrices[section_idx, 4], precision=PRECISE)).reshape(2 * LEN - 1, HEADS, HEAD_DIM) for section_idx in range(2)]
        finals = []
        for micro_idx in range(MB):
            middle = conformer(begin_rows[micro_idx], key_masks[micro_idx], positions[0], matrices[0], ff_mats[0], model_vec[0], inner_vec[0], hidden_vec[0])
            middle = low(low_back(middle))
            finals.append(conformer(middle, key_masks[micro_idx], positions[1], matrices[1], ff_mats[1], model_vec[1], inner_vec[1], hidden_vec[1]))
        return jnp.stack(finals)
    finals, pullback = jax.vjp(whole, starts, mats.astype(jnp.float32), ffw.astype(jnp.float32), vec_model.astype(jnp.float32), vec_inner.astype(jnp.float32), vec_ff.astype(jnp.float32))
    d_starts, g_mats, g_ffw, g_model, g_inner, g_hidden = pullback(cotangent)
    outputs = jnp.zeros((SEQS, LEN, D), jnp.float32).at[order].set(finals.reshape(SEQS, LEN, D))
    d_inputs = jnp.zeros((SEQS, LEN, D), jnp.float32).at[order].set(d_starts.reshape(SEQS, LEN, D))
    return (jnp.stack([d_inputs, outputs]).astype(jnp.bfloat16), g_mats, g_ffw, g_model, g_inner, g_hidden)
```

```python
import functools

import jax
import jax.numpy as jnp
from jax import lax
from jax.experimental import pallas as pl
from jax.experimental.pallas import tpu as pltpu
from jax.sharding import PartitionSpec as P

HEAD_DIM = 64
MB = 2
EPSILON = 1e-05
HUGE_NEG = -1000000000.0
F32 = jnp.float32
BF16 = jnp.bfloat16
LANES = 128
VMEM_LIMIT = 56 * 1024 * 1024

ORDER_A = 0
ORDER_B = 1
ORDER_C = 2


def sinusoid(length, width):
    place = (length - 1 - jnp.arange(2 * length - 1)).astype(F32)
    index = jnp.arange(width // 2).astype(F32)
    rate = jnp.exp(index * (-2.0 * jnp.log(10000.0) / width))
    angle = place[:, None] * rate[None, :]
    return jnp.stack([jnp.sin(angle), jnp.cos(angle)], axis=-1).reshape(2 * length - 1, width)


def nn(a, b):
    return lax.dot_general(a, b, (((1,), (0,)), ((), ())), preferred_element_type=F32)


def nt(a, b):
    return lax.dot_general(a, b, (((1,), (1,)), ((), ())), preferred_element_type=F32)


def tn(a, b):
    return lax.dot_general(a, b, (((0,), (0,)), ((), ())), preferred_element_type=F32)


def ln_parts(v):
    centre = v - jnp.mean(v, axis=-1, keepdims=True)
    rstd = lax.rsqrt(jnp.mean(centre * centre, axis=-1, keepdims=True) + EPSILON)
    return centre * rstd, rstd


def ln(v, gain, shift):
    xhat, _ = ln_parts(v)
    return xhat * (1.0 + gain) + shift


def ln_back(v, gain, dy):
    xhat, rstd = ln_parts(v)
    g = dy * (1.0 + gain)
    dx = rstd * (
        g - jnp.mean(g, axis=-1, keepdims=True) - xhat * jnp.mean(g * xhat, axis=-1, keepdims=True)
    )
    return dx, rows_sum(dy * xhat), rows_sum(dy)


def rows_sum(v):
    return jnp.sum(v, axis=0, keepdims=True)


def sigmoid(v):
    return 1.0 / (1.0 + jnp.exp(-v))


def silu_slope(v):
    s = sigmoid(v)
    return s * (1.0 + v * (1.0 - s))


def bit_order(order, count):
    return [(order + k) % count for k in range(count)]


def slot_mask(slot, bits):
    out = 0
    for k, b in enumerate(bits):
        out |= ((slot >> k) & 1) << b
    return out


def start_weights(meta, own, oth, dst, sem, order, slots, tensor, half, which=None):
    bits = bit_order(order, slots.bit_length() - 1)
    me, core = meta[0], meta[1]
    rows, cols = own.shape[-2], own.shape[-1]
    for slot in range(slots):
        f = me ^ slot_mask(slot, bits)
        plane, t = f // tensor, lax.rem(f, tensor)
        col = pl.ds(pl.multiple_of(t * cols, cols), cols)
        for src, c in ((own, core), (oth, 1 - core)):
            row = pl.ds(pl.multiple_of((c * half + plane) * rows, rows), rows)
            s = src.at[slot] if which is None else src.at[slot, pl.ds(which[0], which[1])]
            pltpu.make_async_copy(s, dst.at[:, row, col], sem).start()


def wait_weights(dst, sem):
    pltpu.make_async_copy(dst, dst, sem).wait()


def head_mask(h):
    lane = lax.broadcasted_iota(jnp.int32, (1, LANES), 1)
    return (lane // HEAD_DIM) == h


def blk(i):
    return slice(i * LANES, (i + 1) * LANES)


def f1_kernel(dims, meta, x_ref, vm_ref, vi_ref, vf_ref, pos_ref, a_own, a_oth, b_own, b_oth,
              s2_ref, filt_ref, stat_ref, s1_ref, before_ref, qu_ref, qv_ref, k_ref, v_ref,
              rel_ref, probs_ref, ctx_ref, gi_ref, gs_ref,
              wa, wb, pad, sems):
    slots, tensor, half = dims
    start_weights(meta, a_own, a_oth, wa, sems.at[0], ORDER_A, slots, tensor, half)
    start_weights(meta, b_own, b_oth, wb, sems.at[1], ORDER_B, slots, tensor, half)
    length = meta[2]
    n_tok = x_ref.shape[0]
    vm = lambda r: vm_ref[r:r + 1, :]
    vi = lambda r: vi_ref[r:r + 1, :]
    x = x_ref[...].astype(F32)
    wait_weights(wa, sems.at[0])
    n0 = ln(x, vm(0), vm(1)).astype(BF16)
    before = nn(n0, wa[0]) + vf_ref[0:1, :]
    before_ref[...] = before
    active = (before * sigmoid(before)).astype(BF16)
    s1 = x + 0.5 * (nt(active, wa[1]) + vm(2))
    s1_ref[...] = s1
    wait_weights(wb, sems.at[1])
    rel_ref[...] = nn(pos_ref[...], wb[4]).astype(BF16)
    n1 = ln(s1, vm(3), vm(4)).astype(BF16)
    q = nn(n1, wb[0]) + vi(0)
    qu_ref[...] = (q + vi(2)).astype(BF16)
    qv_ref[...] = (q + vi(3)).astype(BF16)
    k_ref[...] = nn(n1, wb[1]).astype(BF16)
    v_ref[...] = (nn(n1, wb[2]) + vi(1)).astype(BF16)
    keep = lax.broadcasted_iota(jnp.int32, (1, n_tok), 1) < length
    for i in range(qu_ref.shape[1] // LANES):
        qub, qvb, kb, vb = (r[:, blk(i)] for r in (qu_ref, qv_ref, k_ref, v_ref))
        rb = rel_ref[:, blk(i)]
        halves = []
        for h in range(2):
            mask = head_mask(h)
            direct = nt(jnp.where(mask, qub, 0), kb)
            table = nt(jnp.where(mask, qvb, 0), rb)
            shifted = pltpu.roll(table, n_tok + 1, 1, stride=1, stride_axis=0)[:, :n_tok]
            scores = jnp.where(keep, (direct + shifted) * HEAD_DIM ** (-0.5), HUGE_NEG)
            e = jnp.exp(scores - jnp.max(scores, axis=-1, keepdims=True))
            probs = e / jnp.sum(e, axis=-1, keepdims=True)
            probs_ref[2 * i + h] = probs
            halves.append(nn(probs.astype(BF16), vb))
        ctx_ref[:, blk(i)] = jnp.where(head_mask(0), halves[0], halves[1]).astype(BF16)
    s2 = s1 + nt(ctx_ref[...], wb[3]) + vm(5)
    s2_ref[...] = s2
    n2 = ln(s2, vm(6), vm(7)).astype(BF16)
    gi = nn(n2, wb[5]) + vi(4)
    gs = nn(n2, wb[6]) + vi(5)
    gi_ref[...] = gi
    gs_ref[...] = gs
    inside = (lax.broadcasted_iota(jnp.int32, (n_tok, 1), 0) < length).astype(F32)
    mixed = gi * sigmoid(gs) * inside
    taps = vi_ref.shape[0] - 9
    pad_store(pad, mixed)
    run_taps(pad, vi_ref, [8 + k for k in range(taps)], filt_ref)
    f = filt_ref[...]
    count = length.astype(F32)
    total = rows_sum(inside * f)
    centre = (f - total / count) * inside
    stat_ref[0:1, :] = total
    stat_ref[1:2, :] = rows_sum(centre * centre)
    stat_ref[2:3, :] = jnp.full_like(total, 1.0) * count
    stat_ref[3:8, :] = jnp.zeros((5, total.shape[1]), F32)


def pad_store(pad, value):
    rows = value.shape[0]
    pad[0:16, :] = jnp.zeros((16, value.shape[1]), F32)
    pad[16:16 + rows, :] = value
    pad[16 + rows:32 + rows, :] = jnp.zeros((16, value.shape[1]), F32)


def run_taps(pad, vi_ref, rows, out_ref):
    n_tok = out_ref.shape[0]
    wide = n_tok + 8
    for i in range(out_ref.shape[1] // LANES):
        total = None
        for s in range(8):
            part = None
            for q in range(4):
                e = 8 * q + s - 1
                if 0 <= e < len(rows):
                    term = vi_ref[rows[e]:rows[e] + 1, blk(i)] * pad[8 * q:8 * q + wide, blk(i)]
                    part = term if part is None else part + term
            moved = part[s:s + n_tok]
            total = moved if total is None else total + moved
        out_ref[:, blk(i)] = total


def bn_combine(stats_ref):
    groups = stats_ref.shape[0]
    total = sum(stats_ref[g, 0:1, :] for g in range(groups))
    count = sum(stats_ref[g, 2:3, :] for g in range(groups))
    mean = total / count
    m2 = 0.0
    for g in range(groups):
        n_g = stats_ref[g, 2:3, :]
        off = stats_ref[g, 0:1, :] / n_g - mean
        m2 = m2 + stats_ref[g, 1:2, :] + n_g * off * off
    return mean, lax.rsqrt(m2 / count + EPSILON), count


def f2_kernel(dims, meta, s2_ref, filt_ref, stats_ref, vm_ref, vi_ref, vf_ref, b_own, b_oth,
              c_own, c_oth, out_ref, s3_ref, before_ref, s4_ref, bn_ref, wct, wc, sems):
    slots, tensor, half = dims
    start_weights(meta, b_own, b_oth, wct, sems.at[0], ORDER_B, slots, tensor, half, (7, 1))
    start_weights(meta, c_own, c_oth, wc, sems.at[1], ORDER_C, slots, tensor, half)
    vm = lambda r: vm_ref[r:r + 1, :]
    vi = lambda r: vi_ref[r:r + 1, :]
    mean, inv, count = bn_combine(stats_ref)
    bn_ref[0:1, :] = mean
    bn_ref[1:2, :] = inv
    bn_ref[2:3, :] = count
    bn_ref[3:8, :] = jnp.zeros((5, mean.shape[1]), F32)
    normal = (filt_ref[...] - mean) * inv * (1.0 + vi(6)) + vi(7)
    active = (normal * sigmoid(normal)).astype(BF16)
    wait_weights(wct, sems.at[0])
    s3 = s2_ref[...] + nt(active, wct[0]) + vm(8)
    s3_ref[...] = s3
    n3 = ln(s3, vm(9), vm(10)).astype(BF16)
    wait_weights(wc, sems.at[1])
    before = nn(n3, wc[0]) + vf_ref[1:2, :]
    before_ref[...] = before
    act = (before * sigmoid(before)).astype(BF16)
    s4 = s3 + 0.5 * (nt(act, wc[1]) + vm(11))
    s4_ref[...] = s4
    out_ref[...] = ln(s4, vm(12), vm(13)).astype(BF16)


def b1_kernel(dims, meta, g_ref, s4_ref, s3_ref, before_ref, filt_ref, bn_ref, vm_ref, vi_ref,
              b_own, b_oth, c_own, c_oth,
              ds3_ref, dnorm_ref, sum_ref, n3_ref, db_ref, dl_ref, a_ref, dlc_ref, ac_ref,
              gm_ref, gi_ref, gf_ref, wct, wc, sems):
    slots, tensor, half = dims
    start_weights(meta, c_own, c_oth, wc, sems.at[1], ORDER_C, slots, tensor, half)
    start_weights(meta, b_own, b_oth, wct, sems.at[0], ORDER_B, slots, tensor, half, (7, 1))
    vm = lambda r: vm_ref[r:r + 1, :]
    vi = lambda r: vi_ref[r:r + 1, :]
    ds4, gain4, shift4 = ln_back(s4_ref[...], vm(12), g_ref[...].astype(F32))
    delta = (0.5 * ds4).astype(BF16)
    dl_ref[...] = delta
    s3 = s3_ref[...]
    n3_ref[...] = ln(s3, vm(9), vm(10)).astype(BF16)
    before = before_ref[...]
    a_ref[...] = (before * sigmoid(before)).astype(BF16)
    wait_weights(wc, sems.at[1])
    db = (nn(delta, wc[1]) * silu_slope(before)).astype(BF16)
    db_ref[...] = db
    dn = nt(db, wc[0])
    dx, gain3, shift3 = ln_back(s3, vm(9), dn)
    ds3 = ds4 + dx
    ds3_ref[...] = ds3
    dlc = ds3.astype(BF16)
    dlc_ref[...] = dlc
    xhat = (filt_ref[...] - bn_ref[0:1, :]) * bn_ref[1:2, :]
    normal = xhat * (1.0 + vi(6)) + vi(7)
    ac_ref[...] = (normal * sigmoid(normal)).astype(BF16)
    wait_weights(wct, sems.at[0])
    dnorm = nn(dlc, wct[0]) * silu_slope(normal)
    dnorm_ref[...] = dnorm
    u6 = rows_sum(dnorm * xhat)
    u7 = rows_sum(dnorm)
    sum_ref[0:1, :] = u7 * (1.0 + vi(6))
    sum_ref[1:2, :] = u6 * (1.0 + vi(6))
    sum_ref[2:8, :] = jnp.zeros((6, u6.shape[1]), F32)
    gm_ref[0:1, :] = rows_sum(dlc.astype(F32))
    gm_ref[1:2, :] = gain3
    gm_ref[2:3, :] = shift3
    gm_ref[3:4, :] = rows_sum(delta.astype(F32))
    gm_ref[4:5, :] = gain4
    gm_ref[5:6, :] = shift4
    gm_ref[6:8, :] = jnp.zeros((2, u6.shape[1]), F32)
    gi_ref[0:1, :] = u6
    gi_ref[1:2, :] = u7
    gi_ref[2:8, :] = jnp.zeros((6, u6.shape[1]), F32)
    gf_ref[...] = rows_sum(db.astype(F32))


def b2_kernel(dims, meta, ds3_ref, dnorm_ref, sums_ref, filt_ref, bn_ref, gin_ref, gsig_ref,
              s2_ref, s1_ref, x_ref, before_ref, qu_ref, qv_ref, k_ref, v_ref, rel_ref,
              probs_ref, vm_ref, vi_ref, a_own, a_oth, b_own, b_oth,
              dx_ref, n2_ref, dgi_ref, dgs_ref, dla_ref, n1_ref, dq_ref, dk_ref, dv_ref,
              drel_ref, n0_ref, db_ref, dl_ref, a_ref, gm_ref, gi_ref, gf_ref,
              wa, wb, pad_m, pad_d, dmix, sems):
    slots, tensor, half = dims
    start_weights(meta, b_own, b_oth, wb, sems.at[1], ORDER_B, slots, tensor, half)
    start_weights(meta, a_own, a_oth, wa, sems.at[0], ORDER_A, slots, tensor, half)
    length = meta[2]
    n_tok, width = ds3_ref.shape
    vm = lambda r: vm_ref[r:r + 1, :]
    vi = lambda r: vi_ref[r:r + 1, :]
    groups = sums_ref.shape[0]
    plain = sum(sums_ref[g, 0:1, :] for g in range(groups))
    tilted = sum(sums_ref[g, 1:2, :] for g in range(groups))
    inv = bn_ref[1:2, :]
    xhat = (filt_ref[...] - bn_ref[0:1, :]) * inv
    inside = (lax.broadcasted_iota(jnp.int32, (n_tok, 1), 0) < length).astype(F32)
    dfilt = inv * (
        dnorm_ref[...] * (1.0 + vi(6)) - inside / bn_ref[2:3, :] * (plain + xhat * tilted)
    )
    gin = gin_ref[...]
    sig = sigmoid(gsig_ref[...])
    taps = vi_ref.shape[0] - 9
    pad_store(pad_m, gin * sig * inside)
    pad_store(pad_d, dfilt)
    run_taps(pad_d, vi_ref, [8 + taps - 1 - e for e in range(taps)], dmix)
    wide = n_tok + 8
    for i in range(width // LANES):
        for s in range(8):
            moved = pad_d[16 - s:16 - s + wide, blk(i)]
            for q in range(4):
                e = 8 * q + s - 1
                if 0 <= e < taps:
                    gi_ref[6 + e:7 + e, blk(i)] = rows_sum(
                        moved * pad_m[8 * q:8 * q + wide, blk(i)]
                    )
    dm = dmix[...] * inside
    dgi = (dm * sig).astype(BF16)
    dgs = (dm * gin * sig * (1.0 - sig)).astype(BF16)
    dgi_ref[...] = dgi
    dgs_ref[...] = dgs
    wait_weights(wb, sems.at[1])
    s2 = s2_ref[...]
    n2_ref[...] = ln(s2, vm(6), vm(7)).astype(BF16)
    dx, gain, shift = ln_back(s2, vm(6), nt(dgi, wb[5]) + nt(dgs, wb[6]))
    gm_ref[6:7, :] = gain
    gm_ref[7:8, :] = shift
    ds2 = ds3_ref[...] + dx
    dla = ds2.astype(BF16)
    dla_ref[...] = dla
    dctx = nn(dla, wb[3]).astype(BF16)
    row = lax.broadcasted_iota(jnp.int32, (n_tok, n_tok), 0)
    col = lax.broadcasted_iota(jnp.int32, (n_tok, n_tok), 1)
    flip = (row + col == n_tok - 1).astype(F32).astype(BF16)
    for i in range(width // LANES):
        qub, qvb, kb, vb = (r[:, blk(i)] for r in (qu_ref, qv_ref, k_ref, v_ref))
        rb = rel_ref[:, blk(i)]
        dcb = dctx[:, blk(i)]
        got = []
        for h in range(2):
            mask = head_mask(h)
            probs = probs_ref[2 * i + h]
            dprobs = nt(jnp.where(mask, dcb, 0), vb)
            dvh = tn(probs.astype(BF16), dcb)
            ds = probs * (dprobs - jnp.sum(probs * dprobs, axis=-1, keepdims=True))
            ds = (ds.astype(BF16).astype(F32) * HEAD_DIM ** (-0.5)).astype(BF16)
            turned = jnp.concatenate([nn(flip, ds), jnp.zeros((n_tok, n_tok), F32)], axis=1)
            turned = pltpu.roll(turned, 0, 1, stride=1, stride_axis=0).astype(BF16)
            dr = nn(flip, turned).astype(BF16)
            got.append((nn(ds, kb), nn(dr, rb), tn(ds, qub), dvh, tn(dr, qvb)))
        first = head_mask(0)
        dqu, dqv, dk, dv, drel = (jnp.where(first, a, b) for a, b in zip(*got))
        dq = (dqu + dqv).astype(BF16)
        dvb = dv.astype(BF16)
        dq_ref[:, blk(i)] = dq
        dk_ref[:, blk(i)] = dk.astype(BF16)
        dv_ref[:, blk(i)] = dvb
        drel_ref[:, blk(i)] = drel.astype(BF16)
        gi_ref[0:1, blk(i)] = rows_sum(dq.astype(F32))
        gi_ref[1:2, blk(i)] = rows_sum(dvb.astype(F32))
        gi_ref[2:3, blk(i)] = rows_sum(dqu)
        gi_ref[3:4, blk(i)] = rows_sum(dqv)
    gi_ref[4:5, :] = rows_sum(dgi.astype(F32))
    gi_ref[5:6, :] = rows_sum(dgs.astype(F32))
    gi_ref[6 + taps:40, :] = jnp.zeros((40 - 6 - taps, width), F32)
    s1 = s1_ref[...]
    n1_ref[...] = ln(s1, vm(3), vm(4)).astype(BF16)
    dn = nt(dq_ref[...], wb[0]) + nt(dk_ref[...], wb[1]) + nt(dv_ref[...], wb[2])
    dx, gain, shift = ln_back(s1, vm(3), dn)
    gm_ref[3:4, :] = gain
    gm_ref[4:5, :] = shift
    gm_ref[5:6, :] = rows_sum(dla.astype(F32))
    ds1 = ds2 + dx
    delta = (0.5 * ds1).astype(BF16)
    dl_ref[...] = delta
    before = before_ref[...]
    a_ref[...] = (before * sigmoid(before)).astype(BF16)
    wait_weights(wa, sems.at[0])
    db = (nn(delta, wa[1]) * silu_slope(before)).astype(BF16)
    db_ref[...] = db
    x = x_ref[...].astype(F32)
    n0_ref[...] = ln(x, vm(0), vm(1)).astype(BF16)
    dx, gain, shift = ln_back(x, vm(0), nt(db, wa[0]))
    gm_ref[0:1, :] = gain
    gm_ref[1:2, :] = shift
    gm_ref[2:3, :] = rows_sum(delta.astype(F32))
    gf_ref[...] = rows_sum(db.astype(F32))
    dx_ref[...] = (ds1 + dx).astype(BF16)


def w_kernel(dims, order, count, meta, *refs):
    slots, tensor, half = dims
    pairs, out = refs[:2 * count], refs[2 * count]
    bits = bit_order(order, slots.bit_length() - 1)
    me, core = meta[0], meta[1]
    rows, cols = out.shape[-2], out.shape[-1]
    mine = half * rows
    for i in range(count):
        left, right = pairs[2 * i], pairs[2 * i + 1]
        part = left[:, pl.ds(pl.multiple_of(core * mine, mine), mine)]
        grad = tn(part, right[...])
        for f in range(slots):
            rel = me ^ f
            slot = sum((lax.shift_right_logical(rel, b) & 1) << k for k, b in enumerate(bits))
            plane, t = f // tensor, f % tensor
            out[slot, i] = grad[plane * rows:(plane + 1) * rows, t * cols:(t + 1) * cols].astype(BF16)


def vmem(*shape):
    return pl.BlockSpec(memory_space=pltpu.VMEM)


def call(kernel, ins, outs, scratch=(), any_from=None, flops=0, name=None):
    specs = [pl.BlockSpec(memory_space=pltpu.SMEM)]
    for i in range(1, len(ins)):
        away = any_from is not None and i >= any_from
        specs.append(pl.BlockSpec(memory_space=pl.ANY if away else pltpu.VMEM))
    nbytes = sum(a.size * a.dtype.itemsize for a in ins)
    return pl.pallas_call(
        kernel,
        out_shape=[jax.ShapeDtypeStruct(s, d) for s, d in outs],
        in_specs=specs,
        out_specs=[pl.BlockSpec(memory_space=pltpu.VMEM) for _ in outs],
        scratch_shapes=list(scratch),
        compiler_params=pltpu.CompilerParams(vmem_limit_bytes=VMEM_LIMIT),
        cost_estimate=pl.CostEstimate(flops=flops, bytes_accessed=nbytes, transcendentals=0),
        name=name,
    )(*ins)


def permute(value, pairs):
    return lax.ppermute(value, ("pipe", "dp", "tensor"), pairs)


def per_device(n, tensor, boundary, lengths, batch_of, mats, ffw, vec_model, vec_inner, vec_ff):
    half = n // 2
    slots = half * tensor
    nbits = slots.bit_length() - 1
    dims = (slots, tensor, half)
    core = lax.axis_index("pipe")
    d = lax.axis_index("dp")
    t = lax.axis_index("tensor")
    upper = d // half
    plane = lax.rem(d, half)
    me = plane * tensor + t
    is_upper = upper == 1

    def flat(c, dd, tt):
        return (c * n + dd) * tensor + tt

    everyone = [(c, dd, tt) for c in range(2) for dd in range(n) for tt in range(tensor)]

    def home(c, dd, tt):
        u = dd // half
        return (c, dd, tt) if c == u else (1 - c, dd + half if u == 0 else dd - half, tt)

    swap_pairs = [(flat(*e), flat(*home(*e))) for e in everyone]
    core_pairs = [(flat(c, dd, tt), flat(1 - c, dd, tt)) for c, dd, tt in everyone]

    def bit_pairs(b):
        out = []
        for c, dd, tt in everyone:
            f = ((dd % half) * tensor + tt) ^ (1 << b)
            out.append((flat(c, dd, tt), flat(c, dd // half * half + f // tensor, f % tensor)))
        return out

    def gather(block, order):
        held = permute(block, swap_pairs)[None]
        for b in bit_order(order, nbits):
            held = jnp.concatenate([held, permute(held, bit_pairs(b))], axis=0)
        return held, permute(held, core_pairs)

    def natural(value, lead):
        shape = value.shape
        value = value.reshape((2,) * nbits + shape[1:])
        for b in range(nbits):
            on = lax.shift_right_logical(me, b) & 1
            value = jnp.where(on == 1, jnp.flip(value, nbits - 1 - b), value)
        return value.reshape(shape)

    def by_core(own, oth):
        return jnp.where(core == 0, jnp.stack([own, oth]), jnp.stack([oth, own]))

    ends = boundary[0]
    rows_here, width = ends.shape[1], ends.shape[2]
    length_all = rows_here * tensor
    per_vec = [vec_model.shape[1] * vec_model.shape[2], vec_inner.shape[1] * vec_inner.shape[2],
               vec_ff.shape[1] * vec_ff.shape[2]]
    rows_vec = -(-(sum(per_vec) + MB) // width)
    rows_vec = -(-rows_vec // 16) * 16
    first_is = batch_of[0] == 0
    ordered = jnp.where(first_is, ends, ends[::-1]).reshape(MB * rows_here, width)
    len_ordered = jnp.where(first_is, lengths, lengths[::-1]).astype(BF16)
    vec = jnp.concatenate([vec_model[0].reshape(-1), vec_inner[0].reshape(-1),
                           vec_ff[0].reshape(-1), len_ordered])
    vec = jnp.pad(vec, (0, rows_vec * width - vec.size)).reshape(rows_vec, width)
    v_own, v_oth = gather(jnp.concatenate([ordered, vec], axis=0), 0)
    a_own, a_oth = gather(ffw[0, 0:2], ORDER_A)
    b_own, b_oth = gather(mats[0], ORDER_B)
    c_own, c_oth = gather(ffw[0, 2:4], ORDER_C)

    everything = by_core(natural(v_own, 0), natural(v_oth, 0))
    everything = everything.reshape(n, tensor, MB * rows_here + rows_vec, width)
    vecs = everything[:, :, MB * rows_here:].reshape(n, tensor, rows_vec * width)
    cut = [0, per_vec[0], per_vec[0] + per_vec[1], sum(per_vec)]
    vm = vecs[:, :, cut[0]:cut[1]].reshape(n, tensor, vec_model.shape[1], -1)
    vm = vm.transpose(2, 0, 1, 3).reshape(vec_model.shape[1], width).astype(F32)
    vi = vecs[:, :, cut[1]:cut[2]].reshape(n, tensor, vec_inner.shape[1], -1)
    vi = vi.transpose(2, 1, 0, 3).reshape(vec_inner.shape[1], width).astype(F32)
    vi = jnp.pad(vi, ((0, 1), (0, 0)))
    vf = vecs[:, :, cut[2]:cut[3]].reshape(n, tensor, vec_ff.shape[1], -1)
    vf = vf.transpose(2, 1, 0, 3).reshape(vec_ff.shape[1], -1).astype(F32)
    side, micro = lax.rem(t, 2), t // 2
    source = side * half + plane
    mine = lax.dynamic_index_in_dim(everything, source, 0, keepdims=False)
    tokens = mine[:, :MB * rows_here].reshape(tensor, MB, rows_here, width)
    x0 = lax.dynamic_index_in_dim(tokens, micro, 1, keepdims=False).reshape(length_all, width)
    my_lengths = vecs[:, 0, cut[3]:cut[3] + MB]
    my_length = lax.dynamic_index_in_dim(my_lengths, source, 0, keepdims=False)
    my_length = lax.dynamic_index_in_dim(my_length, micro, 0, keepdims=False).astype(jnp.int32)
    meta = jnp.stack([me, core, my_length, upper]).astype(jnp.int32)
    pos = jnp.pad(sinusoid(length_all, width), ((0, 1), (0, 0))).astype(BF16)

    hidden = vf.shape[1]
    rows, fcols, mcols = ffw.shape[2], ffw.shape[3], mats.shape[3]
    heads = width // HEAD_DIM
    L, D, H = length_all, width, hidden
    wa_s = pltpu.VMEM((2, D, H), BF16)
    wb_s = pltpu.VMEM((8, D, D), BF16)
    wct_s = pltpu.VMEM((1, D, D), BF16)
    sems = pltpu.SemaphoreType.DMA((2,))
    pad_s = pltpu.VMEM((L + 32, D), F32)
    mat_flops = 2 * L * D * D

    def f1(x):
        return call(
            functools.partial(f1_kernel, dims),
            [meta, x, vm, vi, vf, pos, a_own, a_oth, b_own, b_oth],
            [((L, D), F32), ((L, D), F32), ((8, D), F32), ((L, D), F32), ((L, H), F32)]
            + [((L, D), BF16)] * 4
            + [((2 * L, D), BF16), ((heads, L, L), F32), ((L, D), BF16), ((L, D), F32), ((L, D), F32)],
            [wa_s, wb_s, pad_s, sems], 6, 15 * mat_flops, "layer_front",
        )

    def f2(s2, filt, stats):
        return call(
            functools.partial(f2_kernel, dims),
            [meta, s2, filt, stats, vm, vi, vf, b_own, b_oth, c_own, c_oth],
            [((L, D), BF16), ((L, D), F32), ((L, H), F32), ((L, D), F32), ((8, D), F32)],
            [wct_s, wa_s, sems], 7, 9 * mat_flops, "layer_rear",
        )

    def b1(g, s4, s3, before, filt, bn):
        return call(
            functools.partial(b1_kernel, dims),
            [meta, g, s4, s3, before, filt, bn, vm, vi, b_own, b_oth, c_own, c_oth],
            [((L, D), F32), ((L, D), F32), ((8, D), F32), ((L, D), BF16), ((L, H), BF16),
             ((L, D), BF16), ((L, H), BF16), ((L, D), BF16), ((L, D), BF16),
             ((8, D), F32), ((8, D), F32), ((1, H), F32)],
            [wct_s, wa_s, sems], 9, 9 * mat_flops, "back_rear",
        )

    def b2(ds3, dnorm, sums, filt, bn, gin, gsig, s2, s1, x, before, qu, qv, k, v, rel, probs):
        return call(
            functools.partial(b2_kernel, dims),
            [meta, ds3, dnorm, sums, filt, bn, gin, gsig, s2, s1, x, before, qu, qv, k, v, rel,
             probs, vm, vi, a_own, a_oth, b_own, b_oth],
            [((L, D), BF16)] * 9 + [((2 * L, D), BF16), ((L, D), BF16), ((L, H), BF16),
             ((L, D), BF16), ((L, H), BF16), ((8, D), F32), ((40, D), F32), ((1, H), F32)],
            [wa_s, wb_s, pad_s, pad_s, pltpu.VMEM((L, D), F32), sems], 20, 20 * mat_flops,
            "back_front",
        )

    def w(order, pairs, cols):
        flat_pairs = [a for pair in pairs for a in pair]
        return call(
            functools.partial(w_kernel, dims, order, len(pairs)),
            [meta] + flat_pairs,
            [((slots, len(pairs), rows, cols), BF16)],
            (), None, 4 * mat_flops, "weight_grads",
        )[0]

    norm_bits = [0] + list(range(tensor.bit_length() - 1, nbits))

    def norm_group(value):
        held = value[None]
        for b in norm_bits:
            held = jnp.concatenate([held, permute(held, bit_pairs(b))], axis=0)
        return held

    up_pairs = [(flat(c, dd, tt), flat(c, dd + half, tt)) for c, dd, tt in everyone if dd < half]
    down_pairs = [(b, a) for a, b in up_pairs]

    def forward(x):
        front = f1(x)
        stats = norm_group(front[2])
        rear = f2(front[0], front[1], stats)
        return front, rear

    front, rear = forward(x0)
    middle = permute(rear[0], up_pairs)
    x1 = jnp.where(is_upper, middle, x0)
    front, rear = forward(x1)
    (s2, filt, _, s1, before0, qu, qv, k, v, rel, probs, ctx, gin, gsig) = front
    made, s3, before1, s4, bn = rear

    def backward(g):
        part1 = b1(g, s4, s3, before1, filt, bn)
        sums = norm_group(part1[2])
        part2 = b2(part1[0], part1[1], sums, filt, bn, gin, gsig, s2, s1, x1, before0, qu, qv, k,
                   v, rel, probs)
        return part1, part2

    _, part2 = backward(x0)
    d_middle = permute(part2[0], down_pairs)
    part1, part2 = backward(jnp.where(is_upper, x0, d_middle))
    (_, _, _, n3, db1, dl3, a1, dlc, ac, gm1, gi1, gf1) = part1
    (dx, n2, dgi, dgs, dla, n1, dq, dk, dv, drel, n0, db0, dl0, a0, gm2, gi2, gf2) = part2

    def scatter(value, order):
        bits = bit_order(order, nbits)
        for b in reversed(bits):
            keep = value.shape[0] // 2
            got = permute(value[keep:], bit_pairs(b))
            value = (value[:keep].astype(F32) + got.astype(F32)).astype(value.dtype)
        return permute(value[0], swap_pairs)

    grad_c = scatter(w(ORDER_C, [(n3, db1), (dl3, a1)], fcols), ORDER_C)
    pos_pair = jnp.pad(pos, ((0, 0), (0, 0)))
    grad_b = scatter(
        w(ORDER_B, [(n1, dq), (n1, dk), (n1, dv), (dla, ctx), (pos_pair, drel), (n2, dgi),
                    (n2, dgs), (dlc, ac)], mcols), ORDER_B)
    grad_a = scatter(w(ORDER_A, [(n0, db0), (dl0, a0)], fcols), ORDER_A)

    gm = jnp.concatenate([gm2[0:8], gm1[0:6]], axis=0)
    gi = jnp.concatenate([gi2[0:6], gi1[0:2], gi2[6:6 + vec_inner.shape[1] - 8]], axis=0)
    gf = jnp.concatenate([gf2, gf1], axis=0)
    gm = gm.reshape(gm.shape[0], n, tensor, -1).transpose(1, 2, 0, 3).reshape(n, tensor, -1)
    gi = gi.reshape(gi.shape[0], tensor, n, -1).transpose(2, 1, 0, 3).reshape(n, tensor, -1)
    gf = gf.reshape(gf.shape[0], tensor, n, -1).transpose(2, 1, 0, 3).reshape(n, tensor, -1)
    gv = jnp.concatenate([gm, gi, gf], axis=2)
    gv = jnp.pad(gv, ((0, 0), (0, 0), (0, rows_vec * width - gv.shape[2])))
    gv = lax.dynamic_slice_in_dim(gv, core * half, half, 0).reshape(slots, rows_vec, width)
    gv = scatter(natural(gv, 0), 0).reshape(-1)

    stream = jnp.where(is_upper, made, dx).reshape(tensor, rows_here, width)
    got = [None] * MB
    for j in range(tensor):
        sent = lax.dynamic_index_in_dim(stream, t ^ j, 0, keepdims=False)
        if j:
            pairs = [(flat(tt & 1, dd, tt), flat(tt & 1, dd, tt ^ j))
                     for c, dd, tt in everyone if c == 0]
            sent = permute(sent, pairs)
        got[j >> 1] = sent if got[j >> 1] is None else jnp.where(
            lax.rem(t ^ j, 2) == core, sent, got[j >> 1])
    pair = jnp.stack(got)
    pair = jnp.where(micro == 0, pair, pair[::-1])
    pair = permute(pair, swap_pairs)
    ends_out = jnp.where(first_is, pair, pair[::-1])[None]

    return (
        ends_out,
        grad_b.astype(F32)[None],
        jnp.concatenate([grad_a, grad_c], axis=0).astype(F32)[None],
        gv[cut[0]:cut[1]].reshape(vec_model.shape),
        gv[cut[1]:cut[2]].reshape(vec_inner.shape),
        gv[cut[2]:cut[3]].reshape(vec_ff.shape),
    )


def solution(mesh):
    return jax.shard_map(
        functools.partial(per_device, mesh.shape["dp"], mesh.shape["tensor"]),
        mesh=mesh,
        in_specs=(
            P("pipe", "dp", "tensor", None),
            P("dp"),
            P("dp"),
            P("pipe", None, "dp", "tensor"),
            P("pipe", None, "dp", "tensor"),
            P("pipe", None, ("dp", "tensor")),
            P("pipe", None, ("tensor", "dp")),
            P("pipe", None, ("tensor", "dp")),
        ),
        out_specs=(
            P("pipe", "dp", "tensor", None),
            P("pipe", None, "dp", "tensor"),
            P("pipe", None, "dp", "tensor"),
            P("pipe", None, ("dp", "tensor")),
            P("pipe", None, ("tensor", "dp")),
            P("pipe", None, ("tensor", "dp")),
        ),
        check_vma=False,
    )
```

```python
import functools

import jax
import jax.numpy as jnp
import numpy as np
from jax import lax
from jax.experimental import pallas as pl
from jax.experimental.pallas import tpu as pltpu
from jax.sharding import PartitionSpec as P

HEAD_DIM = 64
MB = 2
EPSILON = 1e-05
HUGE_NEG = -1000000000.0
F32 = jnp.float32
BF16 = jnp.bfloat16
LANES = 128
VMEM_LIMIT = 56 * 1024 * 1024

ORDER_A = 0
ORDER_B = 1
ORDER_C = 2


def sinusoid(length, width):
    place = (length - 1 - np.arange(2 * length - 1)).astype(np.float32)
    index = np.arange(width // 2).astype(np.float32)
    rate = np.exp(index * np.float32(-2.0 * np.log(10000.0) / width)).astype(np.float32)
    angle = (place[:, None] * rate[None, :]).astype(np.float64)
    table = np.stack([np.sin(angle), np.cos(angle)], axis=-1).reshape(2 * length - 1, width)
    return np.pad(table, ((0, 1), (0, 0))).astype(np.float32)


def nn(a, b):
    return lax.dot_general(a, b, (((1,), (0,)), ((), ())), preferred_element_type=F32)


def nt(a, b):
    return lax.dot_general(a, b, (((1,), (1,)), ((), ())), preferred_element_type=F32)


def tn(a, b):
    return lax.dot_general(a, b, (((0,), (0,)), ((), ())), preferred_element_type=F32)


def ln_parts(v):
    centre = v - jnp.mean(v, axis=-1, keepdims=True)
    rstd = lax.rsqrt(jnp.mean(centre * centre, axis=-1, keepdims=True) + EPSILON)
    return centre * rstd, rstd


def ln(v, gain, shift):
    xhat, _ = ln_parts(v)
    return xhat * (1.0 + gain) + shift


def ln_back(v, gain, dy):
    xhat, rstd = ln_parts(v)
    g = dy * (1.0 + gain)
    dx = rstd * (
        g - jnp.mean(g, axis=-1, keepdims=True) - xhat * jnp.mean(g * xhat, axis=-1, keepdims=True)
    )
    return dx, rows_sum(dy * xhat), rows_sum(dy)


def rows_sum(v):
    return jnp.sum(v, axis=0, keepdims=True)


def sigmoid(v):
    return 1.0 / (1.0 + jnp.exp(-v))


def silu_slope(v):
    s = sigmoid(v)
    return s * (1.0 + v * (1.0 - s))


def bit_order(order, count):
    return [(order + k) % count for k in range(count)]


def slot_mask(slot, bits):
    out = 0
    for k, b in enumerate(bits):
        out |= ((slot >> k) & 1) << b
    return out


def owners(meta, order, dims):
    slots, tensor, half = dims
    bits = bit_order(order, slots.bit_length() - 1)
    me, core = meta[0], meta[1]
    out = []
    for slot in range(slots):
        f = me ^ slot_mask(slot, bits)
        plane, t = f // tensor, lax.rem(f, tensor)
        hi, at = divmod(slot, slots // 2)
        out.append((hi, at, core * half + plane, t))
        out.append((2 + hi, at, (1 - core) * half + plane, t))
    return out


def start_a(meta, srcs, dst, sem, order, dims):
    cols = srcs[0].shape[-1]
    rows = dst.shape[1] // (2 * dims[2])
    for which, at, d, t in owners(meta, order, dims):
        col = pl.ds(pl.multiple_of(t * cols, cols), cols)
        row = pl.ds(pl.multiple_of(d * rows, rows), rows)
        for k in range(2):
            pltpu.make_async_copy(
                srcs[which].at[at, pl.ds(k * rows, rows)], dst.at[k, row, col], sem).start()


def start_b(meta, srcs, dst, sem, order, dims, which_mats):
    rows, cols = srcs[0].shape[-2:]
    for which, at, d, t in owners(meta, order, dims):
        col = pl.ds(pl.multiple_of(t * cols, cols), cols)
        row = pl.ds(pl.multiple_of(d * rows, rows), rows)
        pltpu.make_async_copy(
            srcs[which].at[at, pl.ds(*which_mats)], dst.at[:, row, col], sem).start()


def wait_weights(dst, sem):
    pltpu.make_async_copy(dst, dst, sem).wait()


def head_mask(h):
    lane = lax.broadcasted_iota(jnp.int32, (1, LANES), 1)
    return (lane // HEAD_DIM) == h


def blk(i):
    return slice(i * LANES, (i + 1) * LANES)


VEC_MODEL, VEC_INNER, VEC_FF, VEC_ROWS = 0, 16, 56, 64


def lane_offsets(d, t, dims, width, hidden):
    slots, tensor, half = dims
    n = 2 * half
    w_small, w_ff = width // (n * tensor), hidden // (n * tensor)
    return (d * tensor + t) * w_small, (t * n + d) * w_small, (t * n + d) * w_ff


def prep_kernel(dims, rows, meta, *refs):
    srcs, (vm_ref, vi_ref, vf_ref, held, sem) = refs[:4], refs[4:]
    where = owners(meta, ORDER_A, dims)
    for i, (which, at, d, t) in enumerate(where):
        pltpu.make_async_copy(srcs[which].at[at, pl.ds(2 * rows, 16)], held.at[i], sem).start()
    wait_weights(held, sem)
    width, hidden = vm_ref.shape[1], vf_ref.shape[1]
    totals = None
    for i, (which, at, d, t) in enumerate(where):
        got = held[i].astype(F32)
        pieces = [got[:, blk(k)] for k in range(4)]
        model, inner, ff = pieces[0], jnp.concatenate(pieces[1:3] + [pieces[3][0:8]], axis=0), pieces[3][8:16]
        offs = lane_offsets(d, t, dims, width, hidden)
        placed = []
        for value, off, full in ((model, offs[0], width), (inner, offs[1], width), (ff, offs[2], hidden)):
            value = jnp.concatenate([value, jnp.zeros((value.shape[0], full - LANES), F32)], axis=1)
            placed.append(pltpu.roll(value, off, 1))
        totals = placed if totals is None else [a + b for a, b in zip(totals, placed)]
    vm_ref[...], vi_ref[...], vf_ref[...] = totals


def f1_kernel(dims, meta, xa_ref, xb_ref, vm_ref, vi_ref, vf_ref, pos_ref, a0, a1, a2, a3,
              b0, b1, b2, b3, s2_ref, filt_ref, stat_ref, s1_ref, before_ref, qu_ref, qv_ref, k_ref, v_ref,
              rel_ref, probs_ref, ctx_ref, gi_ref, gs_ref,
              wa, wb, pad, sems):
    start_a(meta, (a0, a1, a2, a3), wa, sems.at[0], ORDER_A, dims)
    start_b(meta, (b0, b1, b2, b3), wb, sems.at[1], ORDER_B, dims, (0, 8))
    length = meta[2]
    n_tok = xa_ref.shape[0]
    vm = lambda r: vm_ref[r:r + 1, :]
    vi = lambda r: vi_ref[r:r + 1, :]
    x = jnp.where(meta[3] == 1, xb_ref[...].astype(F32), xa_ref[...].astype(F32))
    wait_weights(wa, sems.at[0])
    n0 = ln(x, vm(0), vm(1)).astype(BF16)
    before = nn(n0, wa[0]) + vf_ref[0:1, :]
    before_ref[...] = before
    active = (before * sigmoid(before)).astype(BF16)
    s1 = x + 0.5 * (nt(active, wa[1]) + vm(2))
    s1_ref[...] = s1
    wait_weights(wb, sems.at[1])
    rel_ref[...] = nn(pos_ref[...], wb[4]).astype(BF16)
    n1 = ln(s1, vm(3), vm(4)).astype(BF16)
    q = nn(n1, wb[0]) + vi(0)
    qu_ref[...] = (q + vi(2)).astype(BF16)
    qv_ref[...] = (q + vi(3)).astype(BF16)
    k_ref[...] = nn(n1, wb[1]).astype(BF16)
    v_ref[...] = (nn(n1, wb[2]) + vi(1)).astype(BF16)
    keep = lax.broadcasted_iota(jnp.int32, (1, n_tok), 1) < length
    for i in range(qu_ref.shape[1] // LANES):
        qub, qvb, kb, vb = (r[:, blk(i)] for r in (qu_ref, qv_ref, k_ref, v_ref))
        rb = rel_ref[:, blk(i)]
        halves = []
        for h in range(2):
            mask = head_mask(h)
            direct = nt(jnp.where(mask, qub, 0), kb)
            table = nt(jnp.where(mask, qvb, 0), rb)
            shifted = pltpu.roll(table, n_tok + 1, 1, stride=1, stride_axis=0)[:, :n_tok]
            scores = jnp.where(keep, (direct + shifted) * HEAD_DIM ** (-0.5), HUGE_NEG)
            e = jnp.exp(scores - jnp.max(scores, axis=-1, keepdims=True))
            probs = e / jnp.sum(e, axis=-1, keepdims=True)
            probs_ref[2 * i + h] = probs
            halves.append(nn(probs.astype(BF16), vb))
        ctx_ref[:, blk(i)] = jnp.where(head_mask(0), halves[0], halves[1]).astype(BF16)
    s2 = s1 + nt(ctx_ref[...], wb[3]) + vm(5)
    s2_ref[...] = s2
    n2 = ln(s2, vm(6), vm(7)).astype(BF16)
    gi = nn(n2, wb[5]) + vi(4)
    gs = nn(n2, wb[6]) + vi(5)
    gi_ref[...] = gi
    gs_ref[...] = gs
    inside = (lax.broadcasted_iota(jnp.int32, (n_tok, 1), 0) < length).astype(F32)
    mixed = gi * sigmoid(gs) * inside
    taps = vi_ref.shape[0] - 9
    pad_store(pad, mixed)
    run_taps(pad, vi_ref, [8 + k for k in range(taps)], filt_ref)
    f = filt_ref[...]
    count = length.astype(F32)
    total = rows_sum(inside * f)
    centre = (f - total / count) * inside
    stat_ref[0:1, :] = total
    stat_ref[1:2, :] = rows_sum(centre * centre)
    stat_ref[2:3, :] = jnp.full_like(total, 1.0) * count
    stat_ref[3:8, :] = jnp.zeros((5, total.shape[1]), F32)


def pad_store(pad, value):
    rows = value.shape[0]
    pad[0:16, :] = jnp.zeros((16, value.shape[1]), F32)
    pad[16:16 + rows, :] = value
    pad[16 + rows:32 + rows, :] = jnp.zeros((16, value.shape[1]), F32)


def run_taps(pad, vi_ref, rows, out_ref):
    n_tok = out_ref.shape[0]
    wide = n_tok + 8
    for i in range(out_ref.shape[1] // LANES):
        total = None
        for s in range(8):
            part = None
            for q in range(4):
                e = 8 * q + s - 1
                if 0 <= e < len(rows):
                    term = vi_ref[rows[e]:rows[e] + 1, blk(i)] * pad[8 * q:8 * q + wide, blk(i)]
                    part = term if part is None else part + term
            moved = part[s:s + n_tok]
            total = moved if total is None else total + moved
        out_ref[:, blk(i)] = total


def each_group(refs):
    return [(r, g) for r in refs for g in range(r.shape[0])]


def bn_combine(refs):
    groups = each_group(refs)
    total = sum(r[g, 0:1, :] for r, g in groups)
    count = sum(r[g, 2:3, :] for r, g in groups)
    mean = total / count
    m2 = 0.0
    for r, g in groups:
        n_g = r[g, 2:3, :]
        off = r[g, 0:1, :] / n_g - mean
        m2 = m2 + r[g, 1:2, :] + n_g * off * off
    return mean, lax.rsqrt(m2 / count + EPSILON), count


def f2_kernel(dims, groups, meta, s2_ref, filt_ref, *refs):
    stats, refs = refs[:groups], refs[groups:]
    vm_ref, vi_ref, vf_ref, b0, b1, b2, b3, c0, c1, c2, c3 = refs[:11]
    out_ref, s3_ref, before_ref, s4_ref, bn_ref, wct, wc, sems = refs[11:]
    start_b(meta, (b0, b1, b2, b3), wct, sems.at[0], ORDER_B, dims, (7, 1))
    start_a(meta, (c0, c1, c2, c3), wc, sems.at[1], ORDER_C, dims)
    vm = lambda r: vm_ref[r:r + 1, :]
    vi = lambda r: vi_ref[r:r + 1, :]
    mean, inv, count = bn_combine(stats)
    bn_ref[0:1, :] = mean
    bn_ref[1:2, :] = inv
    bn_ref[2:3, :] = count
    bn_ref[3:8, :] = jnp.zeros((5, mean.shape[1]), F32)
    normal = (filt_ref[...] - mean) * inv * (1.0 + vi(6)) + vi(7)
    active = (normal * sigmoid(normal)).astype(BF16)
    wait_weights(wct, sems.at[0])
    s3 = s2_ref[...] + nt(active, wct[0]) + vm(8)
    s3_ref[...] = s3
    n3 = ln(s3, vm(9), vm(10)).astype(BF16)
    wait_weights(wc, sems.at[1])
    before = nn(n3, wc[0]) + vf_ref[1:2, :]
    before_ref[...] = before
    act = (before * sigmoid(before)).astype(BF16)
    s4 = s3 + 0.5 * (nt(act, wc[1]) + vm(11))
    s4_ref[...] = s4
    out_ref[...] = ln(s4, vm(12), vm(13)).astype(BF16)


def b1_kernel(dims, meta, ga_ref, gb_ref, s4_ref, s3_ref, before_ref, filt_ref, bn_ref, vm_ref,
              vi_ref, b0, b1, b2, b3, c0, c1, c2, c3,
              ds3_ref, dnorm_ref, sum_ref, n3_ref, db_ref, dl_ref, a_ref, dlc_ref, ac_ref,
              gm_ref, gi_ref, gf_ref, wct, wc, sems):
    start_a(meta, (c0, c1, c2, c3), wc, sems.at[1], ORDER_C, dims)
    start_b(meta, (b0, b1, b2, b3), wct, sems.at[0], ORDER_B, dims, (7, 1))
    vm = lambda r: vm_ref[r:r + 1, :]
    vi = lambda r: vi_ref[r:r + 1, :]
    g = jnp.where(meta[3] == 1, ga_ref[...].astype(F32), gb_ref[...].astype(F32))
    ds4, gain4, shift4 = ln_back(s4_ref[...], vm(12), g)
    delta = (0.5 * ds4).astype(BF16)
    dl_ref[...] = delta
    s3 = s3_ref[...]
    n3_ref[...] = ln(s3, vm(9), vm(10)).astype(BF16)
    before = before_ref[...]
    a_ref[...] = (before * sigmoid(before)).astype(BF16)
    wait_weights(wc, sems.at[1])
    db = (nn(delta, wc[1]) * silu_slope(before)).astype(BF16)
    db_ref[...] = db
    dn = nt(db, wc[0])
    dx, gain3, shift3 = ln_back(s3, vm(9), dn)
    ds3 = ds4 + dx
    ds3_ref[...] = ds3
    dlc = ds3.astype(BF16)
    dlc_ref[...] = dlc
    xhat = (filt_ref[...] - bn_ref[0:1, :]) * bn_ref[1:2, :]
    normal = xhat * (1.0 + vi(6)) + vi(7)
    ac_ref[...] = (normal * sigmoid(normal)).astype(BF16)
    wait_weights(wct, sems.at[0])
    dnorm = nn(dlc, wct[0]) * silu_slope(normal)
    dnorm_ref[...] = dnorm
    u6 = rows_sum(dnorm * xhat)
    u7 = rows_sum(dnorm)
    sum_ref[0:1, :] = u7 * (1.0 + vi(6))
    sum_ref[1:2, :] = u6 * (1.0 + vi(6))
    sum_ref[2:8, :] = jnp.zeros((6, u6.shape[1]), F32)
    gm_ref[0:1, :] = rows_sum(dlc.astype(F32))
    gm_ref[1:2, :] = gain3
    gm_ref[2:3, :] = shift3
    gm_ref[3:4, :] = rows_sum(delta.astype(F32))
    gm_ref[4:5, :] = gain4
    gm_ref[5:6, :] = shift4
    gm_ref[6:8, :] = jnp.zeros((2, u6.shape[1]), F32)
    gi_ref[0:1, :] = u6
    gi_ref[1:2, :] = u7
    gi_ref[2:8, :] = jnp.zeros((6, u6.shape[1]), F32)
    gf_ref[...] = rows_sum(db.astype(F32))


def b2_kernel(dims, groups, meta, ds3_ref, dnorm_ref, *refs):
    sums, refs = refs[:groups], refs[groups:]
    (filt_ref, bn_ref, gin_ref, gsig_ref, s2_ref, s1_ref, qu_ref, qv_ref, k_ref, v_ref, rel_ref,
     probs_ref, gm1_ref, gi1_ref, vm_ref, vi_ref, b0, b1, b2, b3) = refs[:20]
    (ds1_ref, n2_ref, dgi_ref, dgs_ref, dla_ref, n1_ref, dq_ref, dk_ref, dv_ref, drel_ref,
     gm_ref, gi_ref, wb, pad_m, pad_d, dmix, sem) = refs[20:]
    start_b(meta, (b0, b1, b2, b3), wb, sem, ORDER_B, dims, (0, 8))
    length = meta[2]
    n_tok, width = ds3_ref.shape
    vm = lambda r: vm_ref[r:r + 1, :]
    vi = lambda r: vi_ref[r:r + 1, :]
    plain = sum(r[g, 0:1, :] for r, g in each_group(sums))
    tilted = sum(r[g, 1:2, :] for r, g in each_group(sums))
    inv = bn_ref[1:2, :]
    xhat = (filt_ref[...] - bn_ref[0:1, :]) * inv
    inside = (lax.broadcasted_iota(jnp.int32, (n_tok, 1), 0) < length).astype(F32)
    dfilt = inv * (
        dnorm_ref[...] * (1.0 + vi(6)) - inside / bn_ref[2:3, :] * (plain + xhat * tilted)
    )
    gin = gin_ref[...]
    sig = sigmoid(gsig_ref[...])
    taps = vi_ref.shape[0] - 9
    pad_store(pad_m, gin * sig * inside)
    pad_store(pad_d, dfilt)
    run_taps(pad_d, vi_ref, [8 + taps - 1 - e for e in range(taps)], dmix)
    wide = n_tok + 8
    for i in range(width // LANES):
        for s in range(8):
            moved = pad_d[16 - s:16 - s + wide, blk(i)]
            for q in range(4):
                e = 8 * q + s - 1
                if 0 <= e < taps:
                    gi_ref[8 + e:9 + e, blk(i)] = rows_sum(
                        moved * pad_m[8 * q:8 * q + wide, blk(i)]
                    )
    dm = dmix[...] * inside
    dgi = (dm * sig).astype(BF16)
    dgs = (dm * gin * sig * (1.0 - sig)).astype(BF16)
    dgi_ref[...] = dgi
    dgs_ref[...] = dgs
    wait_weights(wb, sem)
    s2 = s2_ref[...]
    n2_ref[...] = ln(s2, vm(6), vm(7)).astype(BF16)
    dx, gain, shift = ln_back(s2, vm(6), nt(dgi, wb[5]) + nt(dgs, wb[6]))
    gm_ref[6:7, :] = gain
    gm_ref[7:8, :] = shift
    ds2 = ds3_ref[...] + dx
    dla = ds2.astype(BF16)
    dla_ref[...] = dla
    dctx = nn(dla, wb[3]).astype(BF16)
    row = lax.broadcasted_iota(jnp.int32, (n_tok, n_tok), 0)
    col = lax.broadcasted_iota(jnp.int32, (n_tok, n_tok), 1)
    flip = (row + col == n_tok - 1).astype(F32).astype(BF16)
    for i in range(width // LANES):
        qub, qvb, kb, vb = (r[:, blk(i)] for r in (qu_ref, qv_ref, k_ref, v_ref))
        rb = rel_ref[:, blk(i)]
        dcb = dctx[:, blk(i)]
        got = []
        for h in range(2):
            mask = head_mask(h)
            probs = probs_ref[2 * i + h]
            dprobs = nt(jnp.where(mask, dcb, 0), vb)
            dvh = tn(probs.astype(BF16), dcb)
            ds = probs * (dprobs - jnp.sum(probs * dprobs, axis=-1, keepdims=True))
            ds = (ds.astype(BF16).astype(F32) * HEAD_DIM ** (-0.5)).astype(BF16)
            turned = jnp.concatenate([nn(flip, ds), jnp.zeros((n_tok, n_tok), F32)], axis=1)
            turned = pltpu.roll(turned, 0, 1, stride=1, stride_axis=0).astype(BF16)
            dr = nn(flip, turned).astype(BF16)
            got.append((nn(ds, kb), nn(dr, rb), tn(ds, qub), dvh, tn(dr, qvb)))
        first = head_mask(0)
        dqu, dqv, dk, dv, drel = (jnp.where(first, a, b) for a, b in zip(*got))
        dq = (dqu + dqv).astype(BF16)
        dvb = dv.astype(BF16)
        dq_ref[:, blk(i)] = dq
        dk_ref[:, blk(i)] = dk.astype(BF16)
        dv_ref[:, blk(i)] = dvb
        drel_ref[:, blk(i)] = drel.astype(BF16)
        gi_ref[0:1, blk(i)] = rows_sum(dq.astype(F32))
        gi_ref[1:2, blk(i)] = rows_sum(dvb.astype(F32))
        gi_ref[2:3, blk(i)] = rows_sum(dqu)
        gi_ref[3:4, blk(i)] = rows_sum(dqv)
    gi_ref[4:5, :] = rows_sum(dgi.astype(F32))
    gi_ref[5:6, :] = rows_sum(dgs.astype(F32))
    gi_ref[6:8, :] = gi1_ref[0:2, :]
    gi_ref[8 + taps:40, :] = jnp.zeros((40 - 8 - taps, width), F32)
    gm_ref[0:3, :] = jnp.zeros((3, width), F32)
    gm_ref[8:16, :] = gm1_ref[...]
    s1 = s1_ref[...]
    n1_ref[...] = ln(s1, vm(3), vm(4)).astype(BF16)
    dn = nt(dq_ref[...], wb[0]) + nt(dk_ref[...], wb[1]) + nt(dv_ref[...], wb[2])
    dx, gain, shift = ln_back(s1, vm(3), dn)
    gm_ref[3:4, :] = gain
    gm_ref[4:5, :] = shift
    gm_ref[5:6, :] = rows_sum(dla.astype(F32))
    ds1_ref[...] = ds2 + dx


def b3_kernel(dims, meta, ds1_ref, xa_ref, xb_ref, before_ref, vm_ref, a0, a1, a2, a3,
              dx_ref, n0_ref, db_ref, dl_ref, a_ref, gm_ref, gf_ref, wa, sem):
    start_a(meta, (a0, a1, a2, a3), wa, sem, ORDER_A, dims)
    vm = lambda r: vm_ref[r:r + 1, :]
    ds1 = ds1_ref[...]
    delta = (0.5 * ds1).astype(BF16)
    dl_ref[...] = delta
    before = before_ref[...]
    a_ref[...] = (before * sigmoid(before)).astype(BF16)
    slope = silu_slope(before)
    x = jnp.where(meta[3] == 1, xb_ref[...].astype(F32), xa_ref[...].astype(F32))
    n0_ref[...] = ln(x, vm(0), vm(1)).astype(BF16)
    wait_weights(wa, sem)
    db = (nn(delta, wa[1]) * slope).astype(BF16)
    db_ref[...] = db
    dx, gain, shift = ln_back(x, vm(0), nt(db, wa[0]))
    gm_ref[0:1, :] = gain
    gm_ref[1:2, :] = shift
    gm_ref[2:3, :] = rows_sum(delta.astype(F32))
    gm_ref[3:8, :] = jnp.zeros((5, gain.shape[1]), F32)
    gf_ref[...] = rows_sum(db.astype(F32))
    dx_ref[...] = (ds1 + dx).astype(BF16)


def pieces_of(slots):
    out, top = [], slots
    while top > 1:
        out.append(range(top // 2, top))
        top //= 2
    return out + [range(0, 1)]


def w_kernel(dims, order, count, vectors, meta, *refs):
    slots, tensor, half = dims
    ins, refs = refs[:2 * count], refs[2 * count:]
    vecs, refs = refs[:vectors], refs[vectors:]
    outs, grad = refs[:-1], refs[-1]
    bits = bit_order(order, slots.bit_length() - 1)
    me, core = meta[0], meta[1]
    flat_rows = len(outs[0].shape) == 3
    cols = outs[0].shape[-1]
    rows = ins[0].shape[1] // (2 * half)
    mine = half * rows
    for i in range(count):
        part = ins[2 * i][:, pl.ds(pl.multiple_of(core * mine, mine), mine)]
        grad[i] = tn(part, ins[2 * i + 1][...])
    for out, piece in zip(outs, pieces_of(slots)):
        for at, slot in enumerate(piece):
            f = me ^ slot_mask(slot, bits)
            plane, t = f // tensor, lax.rem(f, tensor)
            row = pl.ds(pl.multiple_of(plane * rows, rows), rows)
            col = pl.ds(pl.multiple_of(t * cols, cols), cols)
            for i in range(count):
                block = grad[i, row, col].astype(BF16)
                if flat_rows:
                    out[at, i * rows:(i + 1) * rows, :] = block
                else:
                    out[at, i] = block
            if vectors:
                gm2_ref, gm0_ref, gi_ref, gf0_ref, gf1_ref = vecs
                width, hidden = gm2_ref.shape[1], gf0_ref.shape[1]
                offs = lane_offsets(core * half + plane, t, dims, width, hidden)
                model = gm2_ref[...] + jnp.concatenate(
                    [gm0_ref[...], jnp.zeros((8, width), F32)], axis=0)
                ff = jnp.concatenate(
                    [gf0_ref[...], gf1_ref[...], jnp.zeros((6, hidden), F32)], axis=0)
                moved = [
                    pltpu.roll(v, v.shape[1] - off, 1)[:, :LANES]
                    for v, off in ((model, offs[0]), (gi_ref[...], offs[1]), (ff, offs[2]))
                ]
                tail = jnp.concatenate([moved[1][32:40], moved[2]], axis=0)
                out[at, count * rows:count * rows + 16, :] = jnp.concatenate(
                    [moved[0], moved[1][0:16], moved[1][16:32], tail], axis=1).astype(BF16)


def vmem(*shape):
    return pl.BlockSpec(memory_space=pltpu.VMEM)


def call(kernel, ins, outs, scratch=(), any_from=None, flops=0, name=None):
    specs = [pl.BlockSpec(memory_space=pltpu.SMEM)]
    for i in range(1, len(ins)):
        away = any_from is not None and i >= any_from
        specs.append(pl.BlockSpec(memory_space=pl.ANY if away else pltpu.VMEM))
    nbytes = sum(a.size * a.dtype.itemsize for a in ins)
    return pl.pallas_call(
        kernel,
        out_shape=[jax.ShapeDtypeStruct(s, d) for s, d in outs],
        in_specs=specs,
        out_specs=[pl.BlockSpec(memory_space=pltpu.VMEM) for _ in outs],
        scratch_shapes=list(scratch),
        compiler_params=pltpu.CompilerParams(vmem_limit_bytes=VMEM_LIMIT),
        cost_estimate=pl.CostEstimate(flops=flops, bytes_accessed=nbytes, transcendentals=0),
        name=name,
    )(*ins)


def permute(value, pairs):
    return lax.ppermute(value, ("pipe", "dp", "tensor"), pairs)


def per_device(n, tensor, boundary, lengths, batch_of, mats, ffw, vec_model, vec_inner, vec_ff):
    half = n // 2
    slots = half * tensor
    nbits = slots.bit_length() - 1
    dims = (slots, tensor, half)
    core = lax.axis_index("pipe")
    d = lax.axis_index("dp")
    t = lax.axis_index("tensor")
    upper = d // half
    plane = lax.rem(d, half)
    me = plane * tensor + t
    is_upper = upper == 1

    def flat(c, dd, tt):
        return (c * n + dd) * tensor + tt

    everyone = [(c, dd, tt) for c in range(2) for dd in range(n) for tt in range(tensor)]

    def home(c, dd, tt):
        u = dd // half
        return (c, dd, tt) if c == u else (1 - c, dd + half if u == 0 else dd - half, tt)

    swap_pairs = [(flat(*e), flat(*home(*e))) for e in everyone]
    core_pairs = [(flat(c, dd, tt), flat(1 - c, dd, tt)) for c, dd, tt in everyone]

    def bit_pairs(b):
        out = []
        for c, dd, tt in everyone:
            f = ((dd % half) * tensor + tt) ^ (1 << b)
            out.append((flat(c, dd, tt), flat(c, dd // half * half + f // tensor, f % tensor)))
        return out

    def gather(block, order):
        held = permute(block, swap_pairs)[None]
        order = bit_order(order, nbits)
        for b in order[:-1]:
            held = jnp.concatenate([held, permute(held, bit_pairs(b))], axis=0)
        far = permute(held, bit_pairs(order[-1]))
        return [held, far, permute(held, core_pairs), permute(far, core_pairs)]

    ends = boundary[0]
    rows_here, width = ends.shape[1], ends.shape[2]
    length_all = rows_here * tensor
    side, micro = lax.rem(t, 2), t // 2
    first_is = batch_of[0] == 0

    there, back = [], []
    for k in range(2):
        pairs = []
        for h in range(2):
            for dd in range(n):
                for tt in range(tensor):
                    s = dd // half
                    j = (s ^ (tt & 1)) + 2 * k
                    pairs.append((flat(h, dd, tt), flat(j & 1, h * half + dd % half, tt ^ j)))
        there.append(pairs)
        back.append([(b, a) for a, b in pairs])

    ordered = jnp.where(first_is, ends, ends[::-1])
    len_ordered = jnp.where(first_is, lengths, lengths[::-1]).astype(BF16)
    parcels = jnp.concatenate(
        [ordered, jnp.broadcast_to(len_ordered[:, None, None], (MB, 16, width))], axis=1)
    sends = jnp.where(micro == 0, parcels, parcels[::-1])
    arrived = jnp.stack([permute(sends[k], there[k]) for k in range(2)])
    others = permute(arrived, core_pairs)
    both = jnp.where(core == 0, jnp.stack([arrived, others], 1), jnp.stack([others, arrived], 1))
    both = jnp.where(lax.rem(t, 2) == 0, both, both[:, ::-1])
    both = jnp.where(micro == 0, both, both[::-1])
    x0 = both[:, :, :rows_here].reshape(length_all, width)
    my_length = both[0, 0, rows_here, 0].astype(jnp.int32)
    meta = jnp.stack([me, core, my_length, upper]).astype(jnp.int32)
    pos = jnp.asarray(sinusoid(length_all, width)).astype(BF16)

    def lanes(v):
        return jnp.pad(v[0], ((0, 0), (0, LANES - v.shape[2])))

    vec = jnp.concatenate([
        jnp.pad(lanes(vec_model), ((0, VEC_INNER - vec_model.shape[1]), (0, 0))),
        jnp.pad(lanes(vec_inner), ((0, VEC_FF - VEC_INNER - vec_inner.shape[1]), (0, 0))),
        jnp.pad(lanes(vec_ff), ((0, VEC_ROWS - VEC_FF - vec_ff.shape[1]), (0, 0)))], axis=0)
    vec = vec.reshape(4, 16, LANES).transpose(1, 0, 2).reshape(16, 4 * LANES)
    rows, fcols, mcols = ffw.shape[2], ffw.shape[3], mats.shape[3]
    a_all = gather(jnp.concatenate([ffw[0, 0:2].reshape(2 * rows, fcols), vec], axis=0), ORDER_A)
    b_all = gather(mats[0], ORDER_B)
    c_all = gather(ffw[0, 2:4].reshape(2 * rows, fcols), ORDER_C)

    hidden = fcols * tensor
    heads = width // HEAD_DIM
    L, D, H = length_all, width, hidden
    wa_s = pltpu.VMEM((2, D, H), BF16)
    wb_s = pltpu.VMEM((8, D, D), BF16)
    wct_s = pltpu.VMEM((1, D, D), BF16)
    sem_s = pltpu.SemaphoreType.DMA
    sems = pltpu.SemaphoreType.DMA((2,))
    pad_s = pltpu.VMEM((L + 32, D), F32)
    mat_flops = 2 * L * D * D

    vm, vi, vf = call(
        functools.partial(prep_kernel, dims, rows), [meta] + a_all,
        [((16, D), F32), ((40, D), F32), ((8, H), F32)],
        [pltpu.VMEM((2 * slots, 16, 4 * LANES), BF16), sem_s], 1, 0, "vectors",
    )

    def f1(xa, xb):
        return call(
            functools.partial(f1_kernel, dims),
            [meta, xa, xb, vm, vi, vf, pos] + a_all + b_all,
            [((L, D), F32), ((L, D), F32), ((8, D), F32), ((L, D), F32), ((L, H), F32)]
            + [((L, D), BF16)] * 4
            + [((2 * L, D), BF16), ((heads, L, L), F32), ((L, D), BF16), ((L, D), F32), ((L, D), F32)],
            [wa_s, wb_s, pad_s, sems], 7, 15 * mat_flops, "layer_front",
        )

    def f2(s2, filt, stats):
        return call(
            functools.partial(f2_kernel, dims, len(stats)),
            [meta, s2, filt] + stats + [vm, vi, vf] + b_all + c_all,
            [((L, D), BF16), ((L, D), F32), ((L, H), F32), ((L, D), F32), ((8, D), F32)],
            [wct_s, wa_s, sems], 6 + len(stats), 9 * mat_flops, "layer_rear",
        )

    def b1(ga, gb, s4, s3, before, filt, bn):
        return call(
            functools.partial(b1_kernel, dims),
            [meta, ga, gb, s4, s3, before, filt, bn, vm, vi] + b_all + c_all,
            [((L, D), F32), ((L, D), F32), ((8, D), F32), ((L, D), BF16), ((L, H), BF16),
             ((L, D), BF16), ((L, H), BF16), ((L, D), BF16), ((L, D), BF16),
             ((8, D), F32), ((8, D), F32), ((1, H), F32)],
            [wct_s, wa_s, sems], 10, 9 * mat_flops, "back_rear",
        )

    def b2(ds3, dnorm, sums, *rest):
        ins = [meta, ds3, dnorm] + sums + list(rest) + [vm, vi]
        return call(
            functools.partial(b2_kernel, dims, len(sums)), ins + b_all,
            [((L, D), F32)] + [((L, D), BF16)] * 8
            + [((2 * L, D), BF16), ((16, D), F32), ((40, D), F32)],
            [wb_s, pad_s, pad_s, pltpu.VMEM((L, D), F32), sem_s], len(ins), 16 * mat_flops,
            "back_front",
        )

    def b3(ds1, xa, xb, before):
        return call(
            functools.partial(b3_kernel, dims), [meta, ds1, xa, xb, before, vm] + a_all,
            [((L, D), BF16), ((L, D), BF16), ((L, H), BF16), ((L, D), BF16), ((L, H), BF16),
             ((8, D), F32), ((1, H), F32)],
            [wa_s, sem_s], 6, 8 * mat_flops, "back_first",
        )

    def w(order, pairs, cols, is_ff, vecs=()):
        count = len(pairs)
        if is_ff:
            shape = (count * rows + (16 if vecs else 0), cols)
        else:
            shape = (count, rows, cols)
        return call(
            functools.partial(w_kernel, dims, order, count, len(vecs)),
            [meta] + [a for pair in pairs for a in pair] + list(vecs),
            [((len(p),) + shape, BF16) for p in pieces_of(slots)],
            [pltpu.VMEM((count, half * rows, cols * tensor), F32)], None, 4 * mat_flops,
            "weight_grads",
        )

    norm_bits = [0] + list(range(tensor.bit_length() - 1, nbits))

    def mask_pairs(mask):
        out = []
        for c, dd, tt in everyone:
            f = ((dd % half) * tensor + tt) ^ mask
            out.append((flat(c, dd, tt), flat(c, dd // half * half + f // tensor, f % tensor)))
        return out

    def norm_group(value):
        held = value[None]
        for first in range(0, len(norm_bits), 2):
            masks = [0]
            for b in norm_bits[first:first + 2]:
                masks = masks + [m ^ (1 << b) for m in masks]
            parts = [held] + [permute(held, mask_pairs(m)) for m in masks[1:]]
            if first + 2 < len(norm_bits):
                held = jnp.concatenate(parts, axis=0)
        return parts

    up_pairs = [(flat(c, dd, tt), flat(c, dd + half, tt)) for c, dd, tt in everyone if dd < half]
    down_pairs = [(b, a) for a, b in up_pairs]

    def forward(xa, xb):
        front = f1(xa, xb)
        stats = norm_group(front[2])
        return front, f2(front[0], front[1], stats)

    front, rear = forward(x0, x0)
    middle = permute(rear[0], up_pairs)
    front, rear = forward(x0, middle)
    (s2, filt, _, s1, before0, qu, qv, k, v, rel, probs, ctx, gin, gsig) = front
    made, s3, before1, s4, bn = rear

    def backward(gb):
        part1 = b1(x0, gb, s4, s3, before1, filt, bn)
        sums = norm_group(part1[2])
        part2 = b2(part1[0], part1[1], sums, filt, bn, gin, gsig, s2, s1, qu, qv, k, v, rel, probs,
                   part1[9], part1[10])
        return part1, part2

    part1, part2 = backward(x0)
    d_middle = permute(b3(part2[0], x0, middle, before0)[0], down_pairs)
    part1, part2 = backward(d_middle)
    (_, _, _, n3, db1, dl3, a1, dlc, ac, _, _, gf1) = part1
    (ds1, n2, dgi, dgs, dla, n1, dq, dk, dv, drel, gm2, gi2) = part2

    def scatter(sent, order):
        got = []
        for piece, b in zip(sent[:-1], reversed(bit_order(order, nbits))):
            size = piece.shape[0]
            for g in got:
                piece = piece.astype(F32) + g[size:2 * size].astype(F32)
            got.append(permute(piece.astype(BF16), bit_pairs(b)))
        total = sent[-1][0].astype(F32)
        for g in got:
            total = total + g[0].astype(F32)
        return permute(total.astype(BF16), swap_pairs)

    grad_c = scatter(w(ORDER_C, [(n3, db1), (dl3, a1)], fcols, True), ORDER_C)
    pieces_b = list(w(ORDER_B, [(n1, dq), (n1, dk), (n1, dv), (dla, ctx), (pos, drel), (n2, dgi),
                                (n2, dgs), (dlc, ac)], mcols, False))
    ds1, pieces_b[0] = lax.optimization_barrier((ds1, pieces_b[0]))
    dx, n0, db0, dl0, a0, gm0, gf0 = b3(ds1, x0, middle, before0)
    grad_b = scatter(pieces_b, ORDER_B)
    grad_a = scatter(w(ORDER_A, [(n0, db0), (dl0, a0)], fcols, True, (gm2, gm0, gi2, gf0, gf1)),
                     ORDER_A)

    stream = jnp.where(is_upper, made, dx).reshape(tensor, rows_here, width)
    pair = jnp.stack([
        permute(lax.dynamic_index_in_dim(stream, t ^ (core + 2 * k), 0, keepdims=False), back[k])
        for k in range(2)])
    pair = jnp.where(micro == 0, pair, pair[::-1])
    ends_out = jnp.where(first_is, pair, pair[::-1])[None]

    grad_a = grad_a.astype(F32)
    gv = grad_a[2 * rows:]
    small = vec_model.shape[2]
    gvi = jnp.concatenate([gv[:, LANES:LANES + small], gv[:, 2 * LANES:2 * LANES + small],
                           gv[:8, 3 * LANES:3 * LANES + small]], axis=0)
    grad_f = jnp.concatenate([grad_a[:2 * rows].reshape(2, rows, fcols),
                              grad_c.astype(F32).reshape(2, rows, fcols)], axis=0)
    return (
        ends_out,
        grad_b.astype(F32)[None],
        grad_f[None],
        gv[:vec_model.shape[1], :small][None],
        gvi[:vec_inner.shape[1]][None],
        gv[8:8 + vec_ff.shape[1], 3 * LANES:3 * LANES + vec_ff.shape[2]][None],
    )


def solution(mesh):
    return jax.shard_map(
        functools.partial(per_device, mesh.shape["dp"], mesh.shape["tensor"]),
        mesh=mesh,
        in_specs=(
            P("pipe", "dp", "tensor", None),
            P("dp"),
            P("dp"),
            P("pipe", None, "dp", "tensor"),
            P("pipe", None, "dp", "tensor"),
            P("pipe", None, ("dp", "tensor")),
            P("pipe", None, ("tensor", "dp")),
            P("pipe", None, ("tensor", "dp")),
        ),
        out_specs=(
            P("pipe", "dp", "tensor", None),
            P("pipe", None, "dp", "tensor"),
            P("pipe", None, "dp", "tensor"),
            P("pipe", None, ("dp", "tensor")),
            P("pipe", None, ("tensor", "dp")),
            P("pipe", None, ("tensor", "dp")),
        ),
        check_vma=False,
    )
```

```python
import functools

import jax
import jax.numpy as jnp
import numpy as np
from jax import lax
from jax.experimental import pallas as pl
from jax.experimental.pallas import tpu as pltpu
from jax.sharding import PartitionSpec as P

HEAD_DIM = 64
MB = 2
EPSILON = 1e-05
HUGE_NEG = -1000000000.0
F32 = jnp.float32
BF16 = jnp.bfloat16
LANES = 128
VMEM_LIMIT = 56 * 1024 * 1024

ORDER_A = 0
ORDER_B = 1
ORDER_C = 2
PARTS_A = 4
PARTS_B = 4
PARTS_C = 4


def sinusoid(length, width):
    place = (length - 1 - np.arange(2 * length - 1)).astype(np.float32)
    index = np.arange(width // 2).astype(np.float32)
    rate = np.exp(index * np.float32(-2.0 * np.log(10000.0) / width)).astype(np.float32)
    angle = (place[:, None] * rate[None, :]).astype(np.float64)
    table = np.stack([np.sin(angle), np.cos(angle)], axis=-1).reshape(2 * length - 1, width)
    return np.pad(table, ((0, 1), (0, 0))).astype(np.float32)


def nn(a, b):
    return lax.dot_general(a, b, (((1,), (0,)), ((), ())), preferred_element_type=F32)


def nt(a, b):
    return lax.dot_general(a, b, (((1,), (1,)), ((), ())), preferred_element_type=F32)


def tn(a, b):
    return lax.dot_general(a, b, (((0,), (0,)), ((), ())), preferred_element_type=F32)


def ln_parts(v):
    centre = v - jnp.mean(v, axis=-1, keepdims=True)
    rstd = lax.rsqrt(jnp.mean(centre * centre, axis=-1, keepdims=True) + EPSILON)
    return centre * rstd, rstd


def ln(v, gain, shift):
    xhat, _ = ln_parts(v)
    return xhat * (1.0 + gain) + shift


def ln_back(v, gain, dy):
    xhat, rstd = ln_parts(v)
    g = dy * (1.0 + gain)
    dx = rstd * (
        g - jnp.mean(g, axis=-1, keepdims=True) - xhat * jnp.mean(g * xhat, axis=-1, keepdims=True)
    )
    return dx, rows_sum(dy * xhat), rows_sum(dy)


def rows_sum(v):
    return jnp.sum(v, axis=0, keepdims=True)


def sigmoid(v):
    return 1.0 / (1.0 + jnp.exp(-v))


def silu_slope(v):
    s = sigmoid(v)
    return s * (1.0 + v * (1.0 - s))


def bit_order(order, count):
    return [(order + k) % count for k in range(count)]


def slot_mask(slot, bits):
    out = 0
    for k, b in enumerate(bits):
        out |= ((slot >> k) & 1) << b
    return out


def owners(meta, srcs, order, dims):
    slots, tensor, half = dims
    bits = bit_order(order, slots.bit_length() - 1)
    me, core = meta[0], meta[1]
    out, own = [], len(srcs) // 2
    for side in range(2):
        slot = 0
        for src in srcs[side * own:(side + 1) * own]:
            for at in range(src.shape[0]):
                f = me ^ slot_mask(slot, bits)
                plane, t = f // tensor, lax.rem(f, tensor)
                out.append((src, at, (core if side == 0 else 1 - core) * half + plane, t))
                slot += 1
    return out


def start_a(meta, srcs, dst, sem, order, dims):
    cols = srcs[0].shape[-1]
    rows = dst.shape[1] // (2 * dims[2])
    for which, at, d, t in owners(meta, srcs, order, dims):
        col = pl.ds(pl.multiple_of(t * cols, cols), cols)
        row = pl.ds(pl.multiple_of(d * rows, rows), rows)
        for k in range(2):
            pltpu.make_async_copy(
                which.at[at, pl.ds(k * rows, rows)], dst.at[k, row, col], sem).start()


def start_b(meta, srcs, dst, sem, order, dims, which_mats):
    rows, cols = srcs[0].shape[-2:]
    for which, at, d, t in owners(meta, srcs, order, dims):
        col = pl.ds(pl.multiple_of(t * cols, cols), cols)
        row = pl.ds(pl.multiple_of(d * rows, rows), rows)
        pltpu.make_async_copy(
            which.at[at, pl.ds(*which_mats)], dst.at[:, row, col], sem).start()


def wait_weights(dst, sem):
    pltpu.make_async_copy(dst, dst, sem).wait()


def head_mask(h):
    lane = lax.broadcasted_iota(jnp.int32, (1, LANES), 1)
    return (lane // HEAD_DIM) == h


def blk(i):
    return slice(i * LANES, (i + 1) * LANES)


VEC_MODEL, VEC_INNER, VEC_FF, VEC_ROWS = 0, 16, 56, 64


def lane_offsets(d, t, dims, width, hidden):
    slots, tensor, half = dims
    n = 2 * half
    w_small, w_ff = width // (n * tensor), hidden // (n * tensor)
    return (d * tensor + t) * w_small, (t * n + d) * w_small, (t * n + d) * w_ff


def prep_kernel(dims, rows, meta, *refs):
    srcs, (vm_ref, vi_ref, vf_ref, held, sem) = refs[:PARTS_A], refs[PARTS_A:]
    where = owners(meta, srcs, ORDER_A, dims)
    for i, (which, at, d, t) in enumerate(where):
        pltpu.make_async_copy(which.at[at, pl.ds(2 * rows, 16)], held.at[i], sem).start()
    wait_weights(held, sem)
    width, hidden = vm_ref.shape[1], vf_ref.shape[1]
    totals = None
    for i, (which, at, d, t) in enumerate(where):
        got = held[i].astype(F32)
        pieces = [got[:, blk(k)] for k in range(4)]
        model, inner, ff = pieces[0], jnp.concatenate(pieces[1:3] + [pieces[3][0:8]], axis=0), pieces[3][8:16]
        offs = lane_offsets(d, t, dims, width, hidden)
        placed = []
        for value, off, full in ((model, offs[0], width), (inner, offs[1], width), (ff, offs[2], hidden)):
            value = jnp.concatenate([value, jnp.zeros((value.shape[0], full - LANES), F32)], axis=1)
            placed.append(pltpu.roll(value, off, 1))
        totals = placed if totals is None else [a + b for a, b in zip(totals, placed)]
    vm_ref[...], vi_ref[...], vf_ref[...] = totals


def f1_kernel(dims, meta, xa_ref, xb_ref, vm_ref, vi_ref, vf_ref, pos_ref, *refs):
    part_a, part_b, refs = refs[:PARTS_A], refs[PARTS_A:PARTS_A + PARTS_B], refs[PARTS_A + PARTS_B:]
    (s2_ref, filt_ref, stat_ref, s1_ref, before_ref, act_ref, qu_ref, qv_ref, k_ref, v_ref,
     rel_ref, probs_ref, ctx_ref, gi_ref, gs_ref, wa, wb, pad, sems) = refs
    start_a(meta, part_a, wa, sems.at[0], ORDER_A, dims)
    start_b(meta, part_b, wb, sems.at[1], ORDER_B, dims, (0, 8))
    length = meta[2]
    n_tok = xa_ref.shape[0]
    vm = lambda r: vm_ref[r:r + 1, :]
    vi = lambda r: vi_ref[r:r + 1, :]
    x = jnp.where(meta[3] == 1, xb_ref[...].astype(F32), xa_ref[...].astype(F32))
    wait_weights(wa, sems.at[0])
    n0 = ln(x, vm(0), vm(1)).astype(BF16)
    before = nn(n0, wa[0]) + vf_ref[0:1, :]
    before_ref[...] = before
    active = (before * sigmoid(before)).astype(BF16)
    act_ref[...] = active
    s1 = x + 0.5 * (nt(active, wa[1]) + vm(2))
    s1_ref[...] = s1
    wait_weights(wb, sems.at[1])
    rel_ref[...] = nn(pos_ref[...], wb[4]).astype(BF16)
    n1 = ln(s1, vm(3), vm(4)).astype(BF16)
    q = nn(n1, wb[0]) + vi(0)
    qu_ref[...] = (q + vi(2)).astype(BF16)
    qv_ref[...] = (q + vi(3)).astype(BF16)
    k_ref[...] = nn(n1, wb[1]).astype(BF16)
    v_ref[...] = (nn(n1, wb[2]) + vi(1)).astype(BF16)
    keep = lax.broadcasted_iota(jnp.int32, (1, n_tok), 1) < length
    for i in range(qu_ref.shape[1] // LANES):
        qub, qvb, kb, vb = (r[:, blk(i)] for r in (qu_ref, qv_ref, k_ref, v_ref))
        rb = rel_ref[:, blk(i)]
        halves = []
        for h in range(2):
            mask = head_mask(h)
            direct = nt(jnp.where(mask, qub, 0), kb)
            table = nt(jnp.where(mask, qvb, 0), rb)
            shifted = pltpu.roll(table, n_tok + 1, 1, stride=1, stride_axis=0)[:, :n_tok]
            scores = jnp.where(keep, (direct + shifted) * HEAD_DIM ** (-0.5), HUGE_NEG)
            e = jnp.exp(scores - jnp.max(scores, axis=-1, keepdims=True))
            probs = e / jnp.sum(e, axis=-1, keepdims=True)
            probs_ref[2 * i + h] = probs
            halves.append(nn(probs.astype(BF16), vb))
        ctx_ref[:, blk(i)] = jnp.where(head_mask(0), halves[0], halves[1]).astype(BF16)
    s2 = s1 + nt(ctx_ref[...], wb[3]) + vm(5)
    s2_ref[...] = s2
    n2 = ln(s2, vm(6), vm(7)).astype(BF16)
    gi = nn(n2, wb[5]) + vi(4)
    gs = nn(n2, wb[6]) + vi(5)
    gi_ref[...] = gi
    gs_ref[...] = gs
    inside = (lax.broadcasted_iota(jnp.int32, (n_tok, 1), 0) < length).astype(F32)
    mixed = gi * sigmoid(gs) * inside
    taps = vi_ref.shape[0] - 9
    pad_store(pad, mixed)
    run_taps(pad, vi_ref, [8 + k for k in range(taps)], filt_ref)
    f = filt_ref[...]
    count = length.astype(F32)
    total = rows_sum(inside * f)
    centre = (f - total / count) * inside
    stat_ref[0:1, :] = total
    stat_ref[1:2, :] = rows_sum(centre * centre)
    stat_ref[2:3, :] = jnp.full_like(total, 1.0) * count
    stat_ref[3:8, :] = jnp.zeros((5, total.shape[1]), F32)


def pad_store(pad, value):
    rows = value.shape[0]
    pad[0:16, :] = jnp.zeros((16, value.shape[1]), F32)
    pad[16:16 + rows, :] = value
    pad[16 + rows:32 + rows, :] = jnp.zeros((16, value.shape[1]), F32)


def run_taps(pad, vi_ref, rows, out_ref):
    n_tok = out_ref.shape[0]
    wide = n_tok + 8
    for i in range(out_ref.shape[1] // LANES):
        total = None
        for s in range(8):
            part = None
            for q in range(4):
                e = 8 * q + s - 1
                if 0 <= e < len(rows):
                    term = vi_ref[rows[e]:rows[e] + 1, blk(i)] * pad[8 * q:8 * q + wide, blk(i)]
                    part = term if part is None else part + term
            moved = part[s:s + n_tok]
            total = moved if total is None else total + moved
        out_ref[:, blk(i)] = total


def each_group(refs):
    return [(r, g) for r in refs for g in range(r.shape[0])]


def bn_combine(refs):
    groups = each_group(refs)
    total = sum(r[g, 0:1, :] for r, g in groups)
    count = sum(r[g, 2:3, :] for r, g in groups)
    mean = total / count
    m2 = 0.0
    for r, g in groups:
        n_g = r[g, 2:3, :]
        off = r[g, 0:1, :] / n_g - mean
        m2 = m2 + r[g, 1:2, :] + n_g * off * off
    return mean, lax.rsqrt(m2 / count + EPSILON), count


def f2_kernel(dims, groups, meta, s2_ref, filt_ref, *refs):
    stats, refs = refs[:groups], refs[groups:]
    vm_ref, vi_ref, vf_ref = refs[:3]
    part_b, part_c, refs = refs[3:3 + PARTS_B], refs[3 + PARTS_B:3 + PARTS_B + PARTS_C], refs[3 + PARTS_B + PARTS_C:]
    out_ref, s3_ref, before_ref, s4_ref, bn_ref, wct, wc, sems = refs
    start_b(meta, part_b, wct, sems.at[0], ORDER_B, dims, (7, 1))
    start_a(meta, part_c, wc, sems.at[1], ORDER_C, dims)
    vm = lambda r: vm_ref[r:r + 1, :]
    vi = lambda r: vi_ref[r:r + 1, :]
    mean, inv, count = bn_combine(stats)
    bn_ref[0:1, :] = mean
    bn_ref[1:2, :] = inv
    bn_ref[2:3, :] = count
    bn_ref[3:8, :] = jnp.zeros((5, mean.shape[1]), F32)
    normal = (filt_ref[...] - mean) * inv * (1.0 + vi(6)) + vi(7)
    active = (normal * sigmoid(normal)).astype(BF16)
    wait_weights(wct, sems.at[0])
    s3 = s2_ref[...] + nt(active, wct[0]) + vm(8)
    s3_ref[...] = s3
    n3 = ln(s3, vm(9), vm(10)).astype(BF16)
    wait_weights(wc, sems.at[1])
    before = nn(n3, wc[0]) + vf_ref[1:2, :]
    before_ref[...] = before
    act = (before * sigmoid(before)).astype(BF16)
    s4 = s3 + 0.5 * (nt(act, wc[1]) + vm(11))
    s4_ref[...] = s4
    out_ref[...] = ln(s4, vm(12), vm(13)).astype(BF16)


def b1_kernel(dims, fresh, meta, ga_ref, gb_ref, s4_ref, s3_ref, before_ref, filt_ref, bn_ref,
              vm_ref, vi_ref, *refs):
    part_b, part_c, refs = refs[:PARTS_B], refs[PARTS_B:PARTS_B + PARTS_C], refs[PARTS_B + PARTS_C:]
    (ds3_ref, dnorm_ref, sum_ref, n3_ref, db_ref, dl_ref, a_ref, dlc_ref, ac_ref,
     gm_ref, gi_ref, gf_ref, wct, wc, sems) = refs
    if fresh:
        start_a(meta, part_c, wc, sems.at[1], ORDER_C, dims)
        start_b(meta, part_b, wct, sems.at[0], ORDER_B, dims, (7, 1))
    vm = lambda r: vm_ref[r:r + 1, :]
    vi = lambda r: vi_ref[r:r + 1, :]
    g = jnp.where(meta[3] == 1, ga_ref[...].astype(F32), gb_ref[...].astype(F32))
    ds4, gain4, shift4 = ln_back(s4_ref[...], vm(12), g)
    delta = (0.5 * ds4).astype(BF16)
    dl_ref[...] = delta
    s3 = s3_ref[...]
    n3_ref[...] = ln(s3, vm(9), vm(10)).astype(BF16)
    before = before_ref[...]
    a_ref[...] = (before * sigmoid(before)).astype(BF16)
    if fresh:
        wait_weights(wc, sems.at[1])
    db = (nn(delta, wc[1]) * silu_slope(before)).astype(BF16)
    db_ref[...] = db
    dn = nt(db, wc[0])
    dx, gain3, shift3 = ln_back(s3, vm(9), dn)
    ds3 = ds4 + dx
    ds3_ref[...] = ds3
    dlc = ds3.astype(BF16)
    dlc_ref[...] = dlc
    xhat = (filt_ref[...] - bn_ref[0:1, :]) * bn_ref[1:2, :]
    normal = xhat * (1.0 + vi(6)) + vi(7)
    ac_ref[...] = (normal * sigmoid(normal)).astype(BF16)
    if fresh:
        wait_weights(wct, sems.at[0])
    dnorm = nn(dlc, wct[0]) * silu_slope(normal)
    dnorm_ref[...] = dnorm
    u6 = rows_sum(dnorm * xhat)
    u7 = rows_sum(dnorm)
    sum_ref[0:1, :] = u7 * (1.0 + vi(6))
    sum_ref[1:2, :] = u6 * (1.0 + vi(6))
    sum_ref[2:8, :] = jnp.zeros((6, u6.shape[1]), F32)
    gm_ref[0:1, :] = rows_sum(dlc.astype(F32))
    gm_ref[1:2, :] = gain3
    gm_ref[2:3, :] = shift3
    gm_ref[3:4, :] = rows_sum(delta.astype(F32))
    gm_ref[4:5, :] = gain4
    gm_ref[5:6, :] = shift4
    gm_ref[6:8, :] = jnp.zeros((2, u6.shape[1]), F32)
    gi_ref[0:1, :] = u6
    gi_ref[1:2, :] = u7
    gi_ref[2:8, :] = jnp.zeros((6, u6.shape[1]), F32)
    gf_ref[...] = rows_sum(db.astype(F32))


def turn_kernel(dims, groups, meta, ga_ref, s2_ref, filt_ref, *refs):
    stats, refs = refs[:groups], refs[groups:]
    n_in = 3 + PARTS_B + PARTS_C
    vm_ref, vi_ref, vf_ref, *weights = refs[:n_in]
    refs = refs[n_in:]
    ahead, behind, (wct, wc, sems) = refs[:5], refs[5:17], refs[17:]
    f2_kernel(dims, groups, meta, s2_ref, filt_ref, *stats, vm_ref, vi_ref, vf_ref, *weights,
              *ahead, wct, wc, sems)
    _, s3_ref, before_ref, s4_ref, bn_ref = ahead
    b1_kernel(dims, False, meta, ga_ref, ga_ref, s4_ref, s3_ref, before_ref, filt_ref, bn_ref,
              vm_ref, vi_ref, *weights, *behind, wct, wc, sems)


def b2_kernel(dims, groups, meta, ds3_ref, dnorm_ref, *refs):
    sums, refs = refs[:groups], refs[groups:]
    (filt_ref, bn_ref, gin_ref, gsig_ref, s2_ref, s1_ref, qu_ref, qv_ref, k_ref, v_ref, rel_ref,
     probs_ref, gm1_ref, gi1_ref, vm_ref, vi_ref) = refs[:16]
    part_b, refs = refs[16:16 + PARTS_B], refs[16 + PARTS_B:]
    (ds1_ref, n2_ref, dgi_ref, dgs_ref, dla_ref, n1_ref, dq_ref, dk_ref, dv_ref, drel_ref,
     dl_ref, gm_ref, gi_ref, wb, pad_m, pad_d, dmix, sem) = refs
    start_b(meta, part_b, wb, sem, ORDER_B, dims, (0, 8))
    length = meta[2]
    n_tok, width = ds3_ref.shape
    vm = lambda r: vm_ref[r:r + 1, :]
    vi = lambda r: vi_ref[r:r + 1, :]
    plain = sum(r[g, 0:1, :] for r, g in each_group(sums))
    tilted = sum(r[g, 1:2, :] for r, g in each_group(sums))
    inv = bn_ref[1:2, :]
    xhat = (filt_ref[...] - bn_ref[0:1, :]) * inv
    inside = (lax.broadcasted_iota(jnp.int32, (n_tok, 1), 0) < length).astype(F32)
    dfilt = inv * (
        dnorm_ref[...] * (1.0 + vi(6)) - inside / bn_ref[2:3, :] * (plain + xhat * tilted)
    )
    gin = gin_ref[...]
    sig = sigmoid(gsig_ref[...])
    taps = vi_ref.shape[0] - 9
    pad_store(pad_m, gin * sig * inside)
    pad_store(pad_d, dfilt)
    run_taps(pad_d, vi_ref, [8 + taps - 1 - e for e in range(taps)], dmix)
    wide = n_tok + 8
    for i in range(width // LANES):
        for s in range(8):
            moved = pad_d[16 - s:16 - s + wide, blk(i)]
            for q in range(4):
                e = 8 * q + s - 1
                if 0 <= e < taps:
                    gi_ref[8 + e:9 + e, blk(i)] = rows_sum(
                        moved * pad_m[8 * q:8 * q + wide, blk(i)]
                    )
    dm = dmix[...] * inside
    dgi = (dm * sig).astype(BF16)
    dgs = (dm * gin * sig * (1.0 - sig)).astype(BF16)
    dgi_ref[...] = dgi
    dgs_ref[...] = dgs
    wait_weights(wb, sem)
    s2 = s2_ref[...]
    n2_ref[...] = ln(s2, vm(6), vm(7)).astype(BF16)
    dx, gain, shift = ln_back(s2, vm(6), nt(dgi, wb[5]) + nt(dgs, wb[6]))
    gm_ref[6:7, :] = gain
    gm_ref[7:8, :] = shift
    ds2 = ds3_ref[...] + dx
    dla = ds2.astype(BF16)
    dla_ref[...] = dla
    dctx = nn(dla, wb[3]).astype(BF16)
    row = lax.broadcasted_iota(jnp.int32, (n_tok, n_tok), 0)
    col = lax.broadcasted_iota(jnp.int32, (n_tok, n_tok), 1)
    flip = (row + col == n_tok - 1).astype(F32).astype(BF16)
    for i in range(width // LANES):
        qub, qvb, kb, vb = (r[:, blk(i)] for r in (qu_ref, qv_ref, k_ref, v_ref))
        rb = rel_ref[:, blk(i)]
        dcb = dctx[:, blk(i)]
        got = []
        for h in range(2):
            mask = head_mask(h)
            probs = probs_ref[2 * i + h]
            dprobs = nt(jnp.where(mask, dcb, 0), vb)
            dvh = tn(probs.astype(BF16), dcb)
            ds = probs * (dprobs - jnp.sum(probs * dprobs, axis=-1, keepdims=True))
            ds = (ds.astype(BF16).astype(F32) * HEAD_DIM ** (-0.5)).astype(BF16)
            turned = jnp.concatenate([nn(flip, ds), jnp.zeros((n_tok, n_tok), F32)], axis=1)
            turned = pltpu.roll(turned, 0, 1, stride=1, stride_axis=0).astype(BF16)
            dr = nn(flip, turned).astype(BF16)
            got.append((nn(ds, kb), nn(dr, rb), tn(ds, qub), dvh, tn(dr, qvb)))
        first = head_mask(0)
        dqu, dqv, dk, dv, drel = (jnp.where(first, a, b) for a, b in zip(*got))
        dq = (dqu + dqv).astype(BF16)
        dvb = dv.astype(BF16)
        dq_ref[:, blk(i)] = dq
        dk_ref[:, blk(i)] = dk.astype(BF16)
        dv_ref[:, blk(i)] = dvb
        drel_ref[:, blk(i)] = drel.astype(BF16)
        gi_ref[0:1, blk(i)] = rows_sum(dq.astype(F32))
        gi_ref[1:2, blk(i)] = rows_sum(dvb.astype(F32))
        gi_ref[2:3, blk(i)] = rows_sum(dqu)
        gi_ref[3:4, blk(i)] = rows_sum(dqv)
    gi_ref[4:5, :] = rows_sum(dgi.astype(F32))
    gi_ref[5:6, :] = rows_sum(dgs.astype(F32))
    gi_ref[6:8, :] = gi1_ref[0:2, :]
    gi_ref[8 + taps:40, :] = jnp.zeros((40 - 8 - taps, width), F32)
    gm_ref[0:3, :] = jnp.zeros((3, width), F32)
    gm_ref[8:16, :] = gm1_ref[...]
    s1 = s1_ref[...]
    n1_ref[...] = ln(s1, vm(3), vm(4)).astype(BF16)
    dn = nt(dq_ref[...], wb[0]) + nt(dk_ref[...], wb[1]) + nt(dv_ref[...], wb[2])
    dx, gain, shift = ln_back(s1, vm(3), dn)
    gm_ref[3:4, :] = gain
    gm_ref[4:5, :] = shift
    gm_ref[5:6, :] = rows_sum(dla.astype(F32))
    ds1 = ds2 + dx
    ds1_ref[...] = ds1
    dl_ref[...] = (0.5 * ds1).astype(BF16)


def b3_kernel(dims, fresh, meta, ds1_ref, xa_ref, xb_ref, before_ref, vm_ref, *refs):
    part_a, (dx_ref, n0_ref, db_ref, gm_ref, gf_ref, wa, sem) = refs[:PARTS_A], refs[PARTS_A:]
    if fresh:
        start_a(meta, part_a, wa, sem, ORDER_A, dims)
    vm = lambda r: vm_ref[r:r + 1, :]
    ds1 = ds1_ref[...]
    delta = (0.5 * ds1).astype(BF16)
    before = before_ref[...]
    slope = silu_slope(before)
    x = jnp.where(meta[3] == 1, xb_ref[...].astype(F32), xa_ref[...].astype(F32))
    n0_ref[...] = ln(x, vm(0), vm(1)).astype(BF16)
    wait_weights(wa, sem)
    db = (nn(delta, wa[1]) * slope).astype(BF16)
    db_ref[...] = db
    dx, gain, shift = ln_back(x, vm(0), nt(db, wa[0]))
    gm_ref[0:1, :] = gain
    gm_ref[1:2, :] = shift
    gm_ref[2:3, :] = rows_sum(delta.astype(F32))
    gm_ref[3:8, :] = jnp.zeros((5, gain.shape[1]), F32)
    gf_ref[...] = rows_sum(db.astype(F32))
    dx_ref[...] = (ds1 + dx).astype(BF16)


def back_kernel(dims, groups, meta, *refs):
    n_in = 2 + groups + 16 + PARTS_B
    ins, refs = refs[:n_in], refs[n_in:]
    (xa_ref, xb_ref, before_ref), part_a, refs = refs[:3], refs[3:3 + PARTS_A], refs[3 + PARTS_A:]
    mid, last, scratch, (wa, sem_a) = refs[:13], refs[13:18], refs[18:23], refs[23:]
    start_a(meta, part_a, wa, sem_a, ORDER_A, dims)
    b2_kernel(dims, groups, meta, *ins, *mid, *scratch)
    b3_kernel(dims, False, meta, mid[0], xa_ref, xb_ref, before_ref, ins[groups + 16], *part_a,
              *last, wa, sem_a)


def pieces_of(slots):
    out, top = [], slots
    while top > 1:
        out.append(range(top // 2, top))
        top //= 2
    return out + [range(0, 1)]


def w_kernel(dims, order, count, vectors, meta, *refs):
    slots, tensor, half = dims
    ins, refs = refs[:2 * count], refs[2 * count:]
    vecs, refs = refs[:vectors], refs[vectors:]
    outs, grad = refs[:-1], refs[-1]
    bits = bit_order(order, slots.bit_length() - 1)
    me, core = meta[0], meta[1]
    flat_rows = len(outs[0].shape) == 3
    cols = outs[0].shape[-1]
    rows = ins[0].shape[1] // (2 * half)
    mine = half * rows
    for i in range(count):
        part = ins[2 * i][:, pl.ds(pl.multiple_of(core * mine, mine), mine)]
        grad[i] = tn(part, ins[2 * i + 1][...])
    for out, piece in zip(outs, pieces_of(slots)):
        for at, slot in enumerate(piece):
            f = me ^ slot_mask(slot, bits)
            plane, t = f // tensor, lax.rem(f, tensor)
            row = pl.ds(pl.multiple_of(plane * rows, rows), rows)
            col = pl.ds(pl.multiple_of(t * cols, cols), cols)
            for i in range(count):
                block = grad[i, row, col].astype(BF16)
                if flat_rows:
                    out[at, i * rows:(i + 1) * rows, :] = block
                else:
                    out[at, i] = block
            if vectors:
                gm2_ref, gm0_ref, gi_ref, gf0_ref, gf1_ref = vecs
                width, hidden = gm2_ref.shape[1], gf0_ref.shape[1]
                offs = lane_offsets(core * half + plane, t, dims, width, hidden)
                model = gm2_ref[...] + jnp.concatenate(
                    [gm0_ref[...], jnp.zeros((8, width), F32)], axis=0)
                ff = jnp.concatenate(
                    [gf0_ref[...], gf1_ref[...], jnp.zeros((6, hidden), F32)], axis=0)
                moved = [
                    pltpu.roll(v, v.shape[1] - off, 1)[:, :LANES]
                    for v, off in ((model, offs[0]), (gi_ref[...], offs[1]), (ff, offs[2]))
                ]
                tail = jnp.concatenate([moved[1][32:40], moved[2]], axis=0)
                out[at, count * rows:count * rows + 16, :] = jnp.concatenate(
                    [moved[0], moved[1][0:16], moved[1][16:32], tail], axis=1).astype(BF16)


def vmem(*shape):
    return pl.BlockSpec(memory_space=pltpu.VMEM)


def call(kernel, ins, outs, scratch=(), any_from=None, flops=0, name=None):
    specs = [pl.BlockSpec(memory_space=pltpu.SMEM)]
    for i in range(1, len(ins)):
        away = i in any_from if isinstance(any_from, list) else any_from is not None and i >= any_from
        specs.append(pl.BlockSpec(memory_space=pl.ANY if away else pltpu.VMEM))
    nbytes = sum(a.size * a.dtype.itemsize for a in ins)
    return pl.pallas_call(
        kernel,
        out_shape=[jax.ShapeDtypeStruct(s, d) for s, d in outs],
        in_specs=specs,
        out_specs=[pl.BlockSpec(memory_space=pltpu.VMEM) for _ in outs],
        scratch_shapes=list(scratch),
        compiler_params=pltpu.CompilerParams(vmem_limit_bytes=VMEM_LIMIT),
        cost_estimate=pl.CostEstimate(flops=flops, bytes_accessed=nbytes, transcendentals=0),
        name=name,
    )(*ins)


def permute(value, pairs):
    return lax.ppermute(value, ("pipe", "dp", "tensor"), pairs)


def per_device(n, tensor, boundary, lengths, batch_of, mats, ffw, vec_model, vec_inner, vec_ff):
    half = n // 2
    slots = half * tensor
    nbits = slots.bit_length() - 1
    dims = (slots, tensor, half)
    core = lax.axis_index("pipe")
    d = lax.axis_index("dp")
    t = lax.axis_index("tensor")
    upper = d // half
    plane = lax.rem(d, half)
    me = plane * tensor + t
    is_upper = upper == 1

    def flat(c, dd, tt):
        return (c * n + dd) * tensor + tt

    everyone = [(c, dd, tt) for c in range(2) for dd in range(n) for tt in range(tensor)]

    def home(c, dd, tt):
        u = dd // half
        return (c, dd, tt) if c == u else (1 - c, dd + half if u == 0 else dd - half, tt)

    swap_pairs = [(flat(*e), flat(*home(*e))) for e in everyone]
    core_pairs = [(flat(c, dd, tt), flat(1 - c, dd, tt)) for c, dd, tt in everyone]

    def bit_pairs(b):
        out = []
        for c, dd, tt in everyone:
            f = ((dd % half) * tensor + tt) ^ (1 << b)
            out.append((flat(c, dd, tt), flat(c, dd // half * half + f // tensor, f % tensor)))
        return out

    def spread(held, bits):
        for b in bits:
            held = jnp.concatenate([held, permute(held, bit_pairs(b))], axis=0)
        return held

    def both_cores(pieces):
        return pieces + [permute(p, core_pairs) for p in pieces]

    def gather(block, order):
        bits = bit_order(order, nbits)
        held = spread(permute(block, swap_pairs)[None], bits[:-1])
        return both_cores([held, permute(held, bit_pairs(bits[-1]))])

    rows, fcols, mcols = ffw.shape[2], ffw.shape[3], mats.shape[3]
    ends = boundary[0]
    rows_here, width = ends.shape[1], ends.shape[2]
    length_all = rows_here * tensor
    side, micro = lax.rem(t, 2), t // 2
    first_is = batch_of[0] == 0

    there, back = [], []
    for k in range(2):
        pairs = []
        for h in range(2):
            for dd in range(n):
                for tt in range(tensor):
                    s = dd // half
                    j = (s ^ (tt & 1)) + 2 * k
                    pairs.append((flat(h, dd, tt), flat(j & 1, h * half + dd % half, tt ^ j)))
        there.append(pairs)
        back.append([(b, a) for a, b in pairs])

    def lanes(v):
        return jnp.pad(v[0], ((0, 0), (0, LANES - v.shape[2])))

    vec = jnp.concatenate([
        jnp.pad(lanes(vec_model), ((0, VEC_INNER - vec_model.shape[1]), (0, 0))),
        jnp.pad(lanes(vec_inner), ((0, VEC_FF - VEC_INNER - vec_inner.shape[1]), (0, 0))),
        jnp.pad(lanes(vec_ff), ((0, VEC_ROWS - VEC_FF - vec_ff.shape[1]), (0, 0)))], axis=0)
    vec = vec.reshape(4, 16, LANES).transpose(1, 0, 2).reshape(16, 4 * LANES)
    ordered = jnp.where(first_is, ends, ends[::-1])
    len_ordered = jnp.where(first_is, lengths, lengths[::-1]).astype(BF16)
    parcels = jnp.concatenate(
        [ordered, jnp.broadcast_to(len_ordered[:, None, None], (MB, 16, width))], axis=1)
    sends = jnp.where(micro == 0, parcels, parcels[::-1])
    arrived = jnp.stack([permute(sends[k], there[k]) for k in range(2)])
    others = permute(arrived, core_pairs)
    both = jnp.where(core == 0, jnp.stack([arrived, others], 1), jnp.stack([others, arrived], 1))
    both = jnp.where(lax.rem(t, 2) == 0, both, both[:, ::-1])
    both = jnp.where(micro == 0, both, both[::-1])
    x0 = both[:, :, :rows_here].reshape(length_all, width)
    my_length = both[0, 0, rows_here, 0].astype(jnp.int32)
    meta = jnp.stack([me, core, my_length, upper]).astype(jnp.int32)
    pos = jnp.asarray(sinusoid(length_all, width)).astype(BF16)

    a_all = gather(jnp.concatenate([ffw[0, 0:2].reshape(2 * rows, fcols), vec], axis=0), ORDER_A)
    b_all = gather(mats[0], ORDER_B)
    c_all = gather(ffw[0, 2:4].reshape(2 * rows, fcols), ORDER_C)

    hidden = fcols * tensor
    heads = width // HEAD_DIM
    L, D, H = length_all, width, hidden
    wa_s = pltpu.VMEM((2, D, H), BF16)
    wb_s = pltpu.VMEM((8, D, D), BF16)
    wct_s = pltpu.VMEM((1, D, D), BF16)
    sem_s = pltpu.SemaphoreType.DMA
    sems = pltpu.SemaphoreType.DMA((2,))
    pad_s = pltpu.VMEM((L + 32, D), F32)
    mat_flops = 2 * L * D * D

    vm, vi, vf = call(
        functools.partial(prep_kernel, dims, rows), [meta] + a_all,
        [((16, D), F32), ((40, D), F32), ((8, H), F32)],
        [pltpu.VMEM((2 * slots, 16, 4 * LANES), BF16), sem_s], 1, 0, "vectors",
    )

    def f1(xa, xb):
        return call(
            functools.partial(f1_kernel, dims),
            [meta, xa, xb, vm, vi, vf, pos] + a_all + b_all,
            [((L, D), F32), ((L, D), F32), ((8, D), F32), ((L, D), F32), ((L, H), F32),
             ((L, H), BF16)] + [((L, D), BF16)] * 4
            + [((2 * L, D), BF16), ((heads, L, L), F32), ((L, D), BF16), ((L, D), F32), ((L, D), F32)],
            [wa_s, wb_s, pad_s, sems], 7, 15 * mat_flops, "layer_front",
        )

    rear_out = [((L, D), BF16), ((L, D), F32), ((L, H), F32), ((L, D), F32), ((8, D), F32)]
    back_rear_out = [
        ((L, D), F32), ((L, D), F32), ((8, D), F32), ((L, D), BF16), ((L, H), BF16),
        ((L, D), BF16), ((L, H), BF16), ((L, D), BF16), ((L, D), BF16),
        ((8, D), F32), ((8, D), F32), ((1, H), F32)]
    back_front_out = ([((L, D), F32)] + [((L, D), BF16)] * 8
                      + [((2 * L, D), BF16), ((L, D), BF16), ((16, D), F32), ((40, D), F32)])
    back_first_out = [((L, D), BF16), ((L, D), BF16), ((L, H), BF16), ((8, D), F32), ((1, H), F32)]
    front_scratch = [wb_s, pad_s, pad_s, pltpu.VMEM((L, D), F32), sem_s]

    def f2(s2, filt, stats):
        ins = [meta, s2, filt] + stats + [vm, vi, vf]
        return call(
            functools.partial(f2_kernel, dims, len(stats)), ins + b_all + c_all, rear_out,
            [wct_s, wa_s, sems], len(ins), 9 * mat_flops, "layer_rear",
        )

    def turn(ga, s2, filt, stats):
        ins = [meta, ga, s2, filt] + stats + [vm, vi, vf]
        out = call(
            functools.partial(turn_kernel, dims, len(stats)), ins + b_all + c_all,
            rear_out + back_rear_out, [wct_s, wa_s, sems], len(ins), 18 * mat_flops, "layer_turn",
        )
        return out[:5], out[5:]

    def b1(ga, gb, s4, s3, before, filt, bn):
        return call(
            functools.partial(b1_kernel, dims, True),
            [meta, ga, gb, s4, s3, before, filt, bn, vm, vi] + b_all + c_all, back_rear_out,
            [wct_s, wa_s, sems], 10, 9 * mat_flops, "back_rear",
        )

    def b2(ds3, dnorm, sums, *rest):
        ins = [meta, ds3, dnorm] + sums + list(rest) + [vm, vi]
        return call(
            functools.partial(b2_kernel, dims, len(sums)), ins + b_all, back_front_out,
            front_scratch, len(ins), 16 * mat_flops, "back_front",
        )

    def b3(ds1, xa, xb, before):
        return call(
            functools.partial(b3_kernel, dims, True), [meta, ds1, xa, xb, before, vm] + a_all,
            back_first_out, [wa_s, sem_s], 6, 8 * mat_flops, "back_first",
        )

    def back_whole(ds3, dnorm, sums, rest, xa, xb, before):
        ins = [meta, ds3, dnorm] + sums + list(rest) + [vm, vi]
        away = list(range(len(ins), len(ins) + PARTS_B))
        whole = ins + b_all + [xa, xb, before] + a_all
        away += list(range(len(whole) - PARTS_A, len(whole)))
        return call(
            functools.partial(back_kernel, dims, len(sums)), whole,
            back_front_out + back_first_out, front_scratch + [wa_s, sem_s], away, 24 * mat_flops,
            "back_whole",
        )[len(back_front_out)]

    def w(order, pairs, cols, is_ff, vecs=()):
        count = len(pairs)
        if is_ff:
            shape = (count * rows + (16 if vecs else 0), cols)
        else:
            shape = (count, rows, cols)
        return call(
            functools.partial(w_kernel, dims, order, count, len(vecs)),
            [meta] + [a for pair in pairs for a in pair] + list(vecs),
            [((len(p),) + shape, BF16) for p in pieces_of(slots)],
            [pltpu.VMEM((count, half * rows, cols * tensor), F32)], None, 4 * mat_flops,
            "weight_grads",
        )

    norm_bits = [0] + list(range(tensor.bit_length() - 1, nbits))

    def mask_pairs(mask):
        out = []
        for c, dd, tt in everyone:
            f = ((dd % half) * tensor + tt) ^ mask
            out.append((flat(c, dd, tt), flat(c, dd // half * half + f // tensor, f % tensor)))
        return out

    def norm_group(value):
        held = value[None]
        for first in range(0, len(norm_bits), 2):
            masks = [0]
            for b in norm_bits[first:first + 2]:
                masks = masks + [m ^ (1 << b) for m in masks]
            parts = [held] + [permute(held, mask_pairs(m)) for m in masks[1:]]
            if first + 2 < len(norm_bits):
                held = jnp.concatenate(parts, axis=0)
        return parts

    up_pairs = [(flat(c, dd, tt), flat(c, dd + half, tt)) for c, dd, tt in everyone if dd < half]
    down_pairs = [(b, a) for a, b in up_pairs]

    def forward(xa, xb):
        front = f1(xa, xb)
        stats = norm_group(front[2])
        return front, f2(front[0], front[1], stats)

    _, rear = forward(x0, x0)
    middle = permute(rear[0], up_pairs)
    front = f1(x0, middle)
    (s2, filt, stats, s1, before0, a0, qu, qv, k, v, rel, probs, ctx, gin, gsig) = front
    rear, part1 = turn(x0, s2, filt, norm_group(stats))
    made, s3, before1, s4, bn = rear

    def rest(part):
        return [filt, bn, gin, gsig, s2, s1, qu, qv, k, v, rel, probs, part[9], part[10]]

    dx = back_whole(part1[0], part1[1], norm_group(part1[2]), rest(part1), x0, middle, before0)
    d_middle = permute(dx, down_pairs)
    part1 = b1(x0, d_middle, s4, s3, before1, filt, bn)
    sums = norm_group(part1[2])
    (_, _, _, n3, db1, dl3, a1, dlc, ac, _, _, gf1) = part1

    def round_of(sent, got, order):
        done = len(got)
        total = sent[done].astype(F32)
        size = total.shape[0]
        last = done == nbits
        for g in got:
            total = total + (g[0:1] if last else g[size:2 * size]).astype(F32)
        if last:
            return permute(total[0].astype(BF16), swap_pairs)
        bit = list(reversed(bit_order(order, nbits)))[done]
        return got + [permute(total.astype(BF16), bit_pairs(bit))]

    def scatter(sent, got, order):
        while len(got) <= nbits:
            more = round_of(sent, got, order)
            if len(got) == nbits:
                return more
            got = more

    pieces_c = w(2, [(n3, db1), (dl3, a1)], fcols, True)
    got_c = round_of(pieces_c, [], 2)
    part2 = b2(part1[0], part1[1], sums, *rest(part1))
    (ds1, n2, dgi, dgs, dla, n1, dq, dk, dv, drel, dl0, gm2, gi2) = part2
    got_c[0], n1 = lax.optimization_barrier((got_c[0], n1))
    got_c = round_of(pieces_c, got_c, 2)
    pieces_b = list(w(0, [(n1, dq), (n1, dk), (n1, dv), (dla, ctx), (pos, drel), (n2, dgi),
                          (n2, dgs), (dlc, ac)], mcols, False))
    got_b = round_of(pieces_b, [], 0)
    ds1, pieces_b[1] = lax.optimization_barrier((ds1, pieces_b[1]))
    dx, n0, db0, gm0, gf0 = b3(ds1, x0, middle, before0)
    got_c[1], n0 = lax.optimization_barrier((got_c[1], n0))
    got_c = round_of(pieces_c, got_c, 2)
    pieces_a = w(1, [(n0, db0), (dl0, a0)], fcols, True, (gm2, gm0, gi2, gf0, gf1))
    got_a = round_of(pieces_a, [], 1)
    got_c[2], got_a[0] = lax.optimization_barrier((got_c[2], got_a[0]))
    grad_c = scatter(pieces_c, got_c, 2)
    grad_b = scatter(pieces_b, got_b, 0)
    grad_a = scatter(pieces_a, got_a, 1)

    stream = jnp.where(is_upper, made, dx).reshape(tensor, rows_here, width)
    pair = jnp.stack([
        permute(lax.dynamic_index_in_dim(stream, t ^ (core + 2 * k), 0, keepdims=False), back[k])
        for k in range(2)])
    pair = jnp.where(micro == 0, pair, pair[::-1])
    ends_out = jnp.where(first_is, pair, pair[::-1])[None]

    grad_a = grad_a.astype(F32)
    gv = grad_a[2 * rows:]
    small = vec_model.shape[2]
    gvi = jnp.concatenate([gv[:, LANES:LANES + small], gv[:, 2 * LANES:2 * LANES + small],
                           gv[:8, 3 * LANES:3 * LANES + small]], axis=0)
    grad_f = jnp.concatenate([grad_a[:2 * rows].reshape(2, rows, fcols),
                              grad_c.astype(F32).reshape(2, rows, fcols)], axis=0)
    grad_m = grad_b.astype(F32)
    return (
        ends_out,
        grad_m[None],
        grad_f[None],
        gv[:vec_model.shape[1], :small][None],
        gvi[:vec_inner.shape[1]][None],
        gv[8:8 + vec_ff.shape[1], 3 * LANES:3 * LANES + vec_ff.shape[2]][None],
    )


def solution(mesh):
    return jax.shard_map(
        functools.partial(per_device, mesh.shape["dp"], mesh.shape["tensor"]),
        mesh=mesh,
        in_specs=(
            P("pipe", "dp", "tensor", None),
            P("dp"),
            P("dp"),
            P("pipe", None, "dp", "tensor"),
            P("pipe", None, "dp", "tensor"),
            P("pipe", None, ("dp", "tensor")),
            P("pipe", None, ("tensor", "dp")),
            P("pipe", None, ("tensor", "dp")),
        ),
        out_specs=(
            P("pipe", "dp", "tensor", None),
            P("pipe", None, "dp", "tensor"),
            P("pipe", None, "dp", "tensor"),
            P("pipe", None, ("dp", "tensor")),
            P("pipe", None, ("tensor", "dp")),
            P("pipe", None, ("tensor", "dp")),
        ),
        check_vma=False,
    )
```

```python
import functools

import jax
import jax.numpy as jnp
import numpy as np
from jax import lax
from jax.experimental import pallas as pl
from jax.experimental.pallas import tpu as pltpu
from jax.sharding import PartitionSpec as P

HEAD_DIM = 64
MB = 2
EPSILON = 1e-05
HUGE_NEG = -1000000000.0
F32 = jnp.float32
BF16 = jnp.bfloat16
LANES = 128
VMEM_LIMIT = 28 * 1024 * 1024

ORDER_A = 0
ORDER_B = 1
ORDER_C = 2
PARTS_A = 4
PARTS_B = 4
PARTS_C = 4


def sinusoid(length, width):
    place = (length - 1 - np.arange(2 * length - 1)).astype(np.float32)
    index = np.arange(width // 2).astype(np.float32)
    rate = np.exp(index * np.float32(-2.0 * np.log(10000.0) / width)).astype(np.float32)
    angle = (place[:, None] * rate[None, :]).astype(np.float64)
    table = np.stack([np.sin(angle), np.cos(angle)], axis=-1).reshape(2 * length - 1, width)
    return np.pad(table, ((0, 1), (0, 0))).astype(np.float32)


def nn(a, b):
    return lax.dot_general(a, b, (((1,), (0,)), ((), ())), preferred_element_type=F32)


def nt(a, b):
    return lax.dot_general(a, b, (((1,), (1,)), ((), ())), preferred_element_type=F32)


def tn(a, b):
    return lax.dot_general(a, b, (((0,), (0,)), ((), ())), preferred_element_type=F32)


def ln_parts(v):
    centre = v - jnp.mean(v, axis=-1, keepdims=True)
    rstd = lax.rsqrt(jnp.mean(centre * centre, axis=-1, keepdims=True) + EPSILON)
    return centre * rstd, rstd


def ln(v, gain, shift):
    xhat, _ = ln_parts(v)
    return xhat * (1.0 + gain) + shift


def ln_back(v, gain, dy):
    xhat, rstd = ln_parts(v)
    g = dy * (1.0 + gain)
    dx = rstd * (
        g - jnp.mean(g, axis=-1, keepdims=True) - xhat * jnp.mean(g * xhat, axis=-1, keepdims=True)
    )
    return dx, rows_sum(dy * xhat), rows_sum(dy)


def rows_sum(v):
    return jnp.sum(v, axis=0, keepdims=True)


def sigmoid(v):
    return 1.0 / (1.0 + jnp.exp(-v))


def silu_slope(v):
    s = sigmoid(v)
    return s * (1.0 + v * (1.0 - s))


def bit_order(order, count):
    return [(order + k) % count for k in range(count)]


def slot_mask(slot, bits):
    out = 0
    for k, b in enumerate(bits):
        out |= ((slot >> k) & 1) << b
    return out


def owners(meta, srcs, order, dims):
    slots, tensor, half = dims
    bits = bit_order(order, slots.bit_length() - 1)
    me, core = meta[0], meta[1]
    out, own = [], len(srcs) // 2
    for side in range(2):
        slot = 0
        for src in srcs[side * own:(side + 1) * own]:
            for at in range(src.shape[0]):
                f = me ^ slot_mask(slot, bits)
                plane, t = f // tensor, lax.rem(f, tensor)
                out.append((src, at, (core if side == 0 else 1 - core) * half + plane, t))
                slot += 1
    return out


def start_a(meta, srcs, dst, sem, order, dims):
    cols = srcs[0].shape[-1]
    rows = dst.shape[1] // (2 * dims[2])
    for which, at, d, t in owners(meta, srcs, order, dims):
        col = pl.ds(pl.multiple_of(t * cols, cols), cols)
        row = pl.ds(pl.multiple_of(d * rows, rows), rows)
        for k in range(2):
            pltpu.make_async_copy(
                which.at[at, pl.ds(k * rows, rows)], dst.at[k, row, col], sem).start()


def start_b(meta, srcs, dst, sem, order, dims, which_mats):
    rows, cols = srcs[0].shape[-2:]
    for which, at, d, t in owners(meta, srcs, order, dims):
        col = pl.ds(pl.multiple_of(t * cols, cols), cols)
        row = pl.ds(pl.multiple_of(d * rows, rows), rows)
        pltpu.make_async_copy(
            which.at[at, pl.ds(*which_mats)], dst.at[:, row, col], sem).start()


def wait_weights(dst, sem):
    pltpu.make_async_copy(dst, dst, sem).wait()


def head_mask(h):
    lane = lax.broadcasted_iota(jnp.int32, (1, LANES), 1)
    return (lane // HEAD_DIM) == h


def blk(i):
    return slice(i * LANES, (i + 1) * LANES)


VEC_MODEL, VEC_INNER, VEC_FF, VEC_ROWS = 0, 16, 56, 64


def lane_offsets(d, t, dims, width, hidden):
    slots, tensor, half = dims
    n = 2 * half
    w_small, w_ff = width // (n * tensor), hidden // (n * tensor)
    return (d * tensor + t) * w_small, (t * n + d) * w_small, (t * n + d) * w_ff


def prep_kernel(dims, rows, meta, *refs):
    srcs, (vm_ref, vi_ref, vf_ref, held, sem) = refs[:PARTS_A], refs[PARTS_A:]
    where = owners(meta, srcs, ORDER_A, dims)
    for i, (which, at, d, t) in enumerate(where):
        pltpu.make_async_copy(which.at[at, pl.ds(2 * rows, 16)], held.at[i], sem).start()
    wait_weights(held, sem)
    width, hidden = vm_ref.shape[1], vf_ref.shape[1]
    totals = None
    for i, (which, at, d, t) in enumerate(where):
        got = held[i].astype(F32)
        pieces = [got[:, blk(k)] for k in range(4)]
        model, inner, ff = pieces[0], jnp.concatenate(pieces[1:3] + [pieces[3][0:8]], axis=0), pieces[3][8:16]
        offs = lane_offsets(d, t, dims, width, hidden)
        placed = []
        for value, off, full in ((model, offs[0], width), (inner, offs[1], width), (ff, offs[2], hidden)):
            value = jnp.concatenate([value, jnp.zeros((value.shape[0], full - LANES), F32)], axis=1)
            placed.append(pltpu.roll(value, off, 1))
        totals = placed if totals is None else [a + b for a, b in zip(totals, placed)]
    vm_ref[...], vi_ref[...], vf_ref[...] = totals


def f1_kernel(dims, meta, xa_ref, xb_ref, vm_ref, vi_ref, vf_ref, pos_ref, *refs):
    part_a, part_b, refs = refs[:PARTS_A], refs[PARTS_A:PARTS_A + PARTS_B], refs[PARTS_A + PARTS_B:]
    (s2_ref, filt_ref, stat_ref, s1_ref, before_ref, act_ref, qu_ref, qv_ref, k_ref, v_ref,
     rel_ref, probs_ref, ctx_ref, gi_ref, gs_ref, wa, wb, pad, sems) = refs
    start_a(meta, part_a, wa, sems.at[0], ORDER_A, dims)
    start_b(meta, part_b, wb, sems.at[1], ORDER_B, dims, (0, 8))
    length = meta[2]
    n_tok = xa_ref.shape[0]
    vm = lambda r: vm_ref[r:r + 1, :]
    vi = lambda r: vi_ref[r:r + 1, :]
    x = jnp.where(meta[3] == 1, xb_ref[...].astype(F32), xa_ref[...].astype(F32))
    wait_weights(wa, sems.at[0])
    n0 = ln(x, vm(0), vm(1)).astype(BF16)
    before = nn(n0, wa[0]) + vf_ref[0:1, :]
    before_ref[...] = before
    active = (before * sigmoid(before)).astype(BF16)
    act_ref[...] = active
    s1 = x + 0.5 * (nt(active, wa[1]) + vm(2))
    s1_ref[...] = s1
    wait_weights(wb, sems.at[1])
    rel_ref[...] = nn(pos_ref[...], wb[4]).astype(BF16)
    n1 = ln(s1, vm(3), vm(4)).astype(BF16)
    q = nn(n1, wb[0]) + vi(0)
    qu_ref[...] = (q + vi(2)).astype(BF16)
    qv_ref[...] = (q + vi(3)).astype(BF16)
    k_ref[...] = nn(n1, wb[1]).astype(BF16)
    v_ref[...] = (nn(n1, wb[2]) + vi(1)).astype(BF16)
    keep = lax.broadcasted_iota(jnp.int32, (1, n_tok), 1) < length
    for i in range(qu_ref.shape[1] // LANES):
        qub, qvb, kb, vb = (r[:, blk(i)] for r in (qu_ref, qv_ref, k_ref, v_ref))
        rb = rel_ref[:, blk(i)]
        halves = []
        for h in range(2):
            mask = head_mask(h)
            direct = nt(jnp.where(mask, qub, 0), kb)
            table = nt(jnp.where(mask, qvb, 0), rb)
            shifted = pltpu.roll(table, n_tok + 1, 1, stride=1, stride_axis=0)[:, :n_tok]
            scores = jnp.where(keep, (direct + shifted) * HEAD_DIM ** (-0.5), HUGE_NEG)
            e = jnp.exp(scores - jnp.max(scores, axis=-1, keepdims=True))
            probs = e / jnp.sum(e, axis=-1, keepdims=True)
            probs_ref[2 * i + h] = probs
            halves.append(nn(probs.astype(BF16), vb))
        ctx_ref[:, blk(i)] = jnp.where(head_mask(0), halves[0], halves[1]).astype(BF16)
    s2 = s1 + nt(ctx_ref[...], wb[3]) + vm(5)
    s2_ref[...] = s2
    n2 = ln(s2, vm(6), vm(7)).astype(BF16)
    gi = nn(n2, wb[5]) + vi(4)
    gs = nn(n2, wb[6]) + vi(5)
    gi_ref[...] = gi
    gs_ref[...] = gs
    inside = (lax.broadcasted_iota(jnp.int32, (n_tok, 1), 0) < length).astype(F32)
    mixed = gi * sigmoid(gs) * inside
    taps = vi_ref.shape[0] - 9
    pad_store(pad, mixed)
    run_taps(pad, vi_ref, [8 + k for k in range(taps)], filt_ref)
    f = filt_ref[...]
    count = length.astype(F32)
    total = rows_sum(inside * f)
    centre = (f - total / count) * inside
    stat_ref[0:1, :] = total
    stat_ref[1:2, :] = rows_sum(centre * centre)
    stat_ref[2:3, :] = jnp.full_like(total, 1.0) * count
    stat_ref[3:8, :] = jnp.zeros((5, total.shape[1]), F32)


def pad_store(pad, value):
    rows = value.shape[0]
    pad[0:16, :] = jnp.zeros((16, value.shape[1]), F32)
    pad[16:16 + rows, :] = value
    pad[16 + rows:32 + rows, :] = jnp.zeros((16, value.shape[1]), F32)


def run_taps(pad, vi_ref, rows, out_ref):
    n_tok = out_ref.shape[0]
    wide = n_tok + 8
    for i in range(out_ref.shape[1] // LANES):
        total = None
        for s in range(8):
            part = None
            for q in range(4):
                e = 8 * q + s - 1
                if 0 <= e < len(rows):
                    term = vi_ref[rows[e]:rows[e] + 1, blk(i)] * pad[8 * q:8 * q + wide, blk(i)]
                    part = term if part is None else part + term
            moved = part[s:s + n_tok]
            total = moved if total is None else total + moved
        out_ref[:, blk(i)] = total


def each_group(refs):
    return [(r, g) for r in refs for g in range(r.shape[0])]


def bn_combine(refs):
    groups = each_group(refs)
    total = sum(r[g, 0:1, :] for r, g in groups)
    count = sum(r[g, 2:3, :] for r, g in groups)
    mean = total / count
    m2 = 0.0
    for r, g in groups:
        n_g = r[g, 2:3, :]
        off = r[g, 0:1, :] / n_g - mean
        m2 = m2 + r[g, 1:2, :] + n_g * off * off
    return mean, lax.rsqrt(m2 / count + EPSILON), count


def f2_kernel(dims, groups, meta, s2_ref, filt_ref, *refs):
    stats, refs = refs[:groups], refs[groups:]
    vm_ref, vi_ref, vf_ref = refs[:3]
    part_b, part_c, refs = refs[3:3 + PARTS_B], refs[3 + PARTS_B:3 + PARTS_B + PARTS_C], refs[3 + PARTS_B + PARTS_C:]
    out_ref, s3_ref, before_ref, s4_ref, bn_ref, wct, wc, sems = refs
    start_b(meta, part_b, wct, sems.at[0], ORDER_B, dims, (7, 1))
    start_a(meta, part_c, wc, sems.at[1], ORDER_C, dims)
    vm = lambda r: vm_ref[r:r + 1, :]
    vi = lambda r: vi_ref[r:r + 1, :]
    mean, inv, count = bn_combine(stats)
    bn_ref[0:1, :] = mean
    bn_ref[1:2, :] = inv
    bn_ref[2:3, :] = count
    bn_ref[3:8, :] = jnp.zeros((5, mean.shape[1]), F32)
    normal = (filt_ref[...] - mean) * inv * (1.0 + vi(6)) + vi(7)
    active = (normal * sigmoid(normal)).astype(BF16)
    wait_weights(wct, sems.at[0])
    s3 = s2_ref[...] + nt(active, wct[0]) + vm(8)
    s3_ref[...] = s3
    n3 = ln(s3, vm(9), vm(10)).astype(BF16)
    wait_weights(wc, sems.at[1])
    before = nn(n3, wc[0]) + vf_ref[1:2, :]
    before_ref[...] = before
    act = (before * sigmoid(before)).astype(BF16)
    s4 = s3 + 0.5 * (nt(act, wc[1]) + vm(11))
    s4_ref[...] = s4
    out_ref[...] = ln(s4, vm(12), vm(13)).astype(BF16)


def b1_kernel(dims, fresh, meta, ga_ref, gb_ref, s4_ref, s3_ref, before_ref, filt_ref, bn_ref,
              vm_ref, vi_ref, *refs):
    part_b, part_c, refs = refs[:PARTS_B], refs[PARTS_B:PARTS_B + PARTS_C], refs[PARTS_B + PARTS_C:]
    (ds3_ref, dnorm_ref, sum_ref, n3_ref, db_ref, dl_ref, a_ref, dlc_ref, ac_ref,
     gm_ref, gi_ref, gf_ref, wct, wc, sems) = refs
    if fresh:
        start_a(meta, part_c, wc, sems.at[1], ORDER_C, dims)
        start_b(meta, part_b, wct, sems.at[0], ORDER_B, dims, (7, 1))
    vm = lambda r: vm_ref[r:r + 1, :]
    vi = lambda r: vi_ref[r:r + 1, :]
    g = jnp.where(meta[3] == 1, ga_ref[...].astype(F32), gb_ref[...].astype(F32))
    ds4, gain4, shift4 = ln_back(s4_ref[...], vm(12), g)
    delta = (0.5 * ds4).astype(BF16)
    dl_ref[...] = delta
    s3 = s3_ref[...]
    n3_ref[...] = ln(s3, vm(9), vm(10)).astype(BF16)
    before = before_ref[...]
    a_ref[...] = (before * sigmoid(before)).astype(BF16)
    if fresh:
        wait_weights(wc, sems.at[1])
    db = (nn(delta, wc[1]) * silu_slope(before)).astype(BF16)
    db_ref[...] = db
    dn = nt(db, wc[0])
    dx, gain3, shift3 = ln_back(s3, vm(9), dn)
    ds3 = ds4 + dx
    ds3_ref[...] = ds3
    dlc = ds3.astype(BF16)
    dlc_ref[...] = dlc
    xhat = (filt_ref[...] - bn_ref[0:1, :]) * bn_ref[1:2, :]
    normal = xhat * (1.0 + vi(6)) + vi(7)
    ac_ref[...] = (normal * sigmoid(normal)).astype(BF16)
    if fresh:
        wait_weights(wct, sems.at[0])
    dnorm = nn(dlc, wct[0]) * silu_slope(normal)
    dnorm_ref[...] = dnorm
    u6 = rows_sum(dnorm * xhat)
    u7 = rows_sum(dnorm)
    sum_ref[0:1, :] = u7 * (1.0 + vi(6))
    sum_ref[1:2, :] = u6 * (1.0 + vi(6))
    sum_ref[2:8, :] = jnp.zeros((6, u6.shape[1]), F32)
    gm_ref[0:1, :] = rows_sum(dlc.astype(F32))
    gm_ref[1:2, :] = gain3
    gm_ref[2:3, :] = shift3
    gm_ref[3:4, :] = rows_sum(delta.astype(F32))
    gm_ref[4:5, :] = gain4
    gm_ref[5:6, :] = shift4
    gm_ref[6:8, :] = jnp.zeros((2, u6.shape[1]), F32)
    gi_ref[0:1, :] = u6
    gi_ref[1:2, :] = u7
    gi_ref[2:8, :] = jnp.zeros((6, u6.shape[1]), F32)
    gf_ref[...] = rows_sum(db.astype(F32))


def turn_kernel(dims, groups, meta, ga_ref, s2_ref, filt_ref, *refs):
    stats, refs = refs[:groups], refs[groups:]
    n_in = 3 + PARTS_B + PARTS_C
    vm_ref, vi_ref, vf_ref, *weights = refs[:n_in]
    refs = refs[n_in:]
    ahead, behind, (wct, wc, sems) = refs[:5], refs[5:17], refs[17:]
    f2_kernel(dims, groups, meta, s2_ref, filt_ref, *stats, vm_ref, vi_ref, vf_ref, *weights,
              *ahead, wct, wc, sems)
    _, s3_ref, before_ref, s4_ref, bn_ref = ahead
    b1_kernel(dims, False, meta, ga_ref, ga_ref, s4_ref, s3_ref, before_ref, filt_ref, bn_ref,
              vm_ref, vi_ref, *weights, *behind, wct, wc, sems)


def b2_kernel(dims, groups, meta, ds3_ref, dnorm_ref, *refs):
    sums, refs = refs[:groups], refs[groups:]
    (filt_ref, bn_ref, gin_ref, gsig_ref, s2_ref, s1_ref, qu_ref, qv_ref, k_ref, v_ref, rel_ref,
     probs_ref, gm1_ref, gi1_ref, vm_ref, vi_ref) = refs[:16]
    part_b, refs = refs[16:16 + PARTS_B], refs[16 + PARTS_B:]
    (ds1_ref, n2_ref, dgi_ref, dgs_ref, dla_ref, n1_ref, dq_ref, dk_ref, dv_ref, drel_ref,
     dl_ref, gm_ref, gi_ref, wb, pad_m, pad_d, dmix, sem) = refs
    start_b(meta, part_b, wb, sem, ORDER_B, dims, (0, 8))
    length = meta[2]
    n_tok, width = ds3_ref.shape
    vm = lambda r: vm_ref[r:r + 1, :]
    vi = lambda r: vi_ref[r:r + 1, :]
    plain = sum(r[g, 0:1, :] for r, g in each_group(sums))
    tilted = sum(r[g, 1:2, :] for r, g in each_group(sums))
    inv = bn_ref[1:2, :]
    xhat = (filt_ref[...] - bn_ref[0:1, :]) * inv
    inside = (lax.broadcasted_iota(jnp.int32, (n_tok, 1), 0) < length).astype(F32)
    dfilt = inv * (
        dnorm_ref[...] * (1.0 + vi(6)) - inside / bn_ref[2:3, :] * (plain + xhat * tilted)
    )
    gin = gin_ref[...]
    sig = sigmoid(gsig_ref[...])
    taps = vi_ref.shape[0] - 9
    pad_store(pad_m, gin * sig * inside)
    pad_store(pad_d, dfilt)
    run_taps(pad_d, vi_ref, [8 + taps - 1 - e for e in range(taps)], dmix)
    wide = n_tok + 8
    for i in range(width // LANES):
        for s in range(8):
            moved = pad_d[16 - s:16 - s + wide, blk(i)]
            for q in range(4):
                e = 8 * q + s - 1
                if 0 <= e < taps:
                    gi_ref[8 + e:9 + e, blk(i)] = rows_sum(
                        moved * pad_m[8 * q:8 * q + wide, blk(i)]
                    )
    dm = dmix[...] * inside
    dgi = (dm * sig).astype(BF16)
    dgs = (dm * gin * sig * (1.0 - sig)).astype(BF16)
    dgi_ref[...] = dgi
    dgs_ref[...] = dgs
    wait_weights(wb, sem)
    s2 = s2_ref[...]
    n2_ref[...] = ln(s2, vm(6), vm(7)).astype(BF16)
    dx, gain, shift = ln_back(s2, vm(6), nt(dgi, wb[5]) + nt(dgs, wb[6]))
    gm_ref[6:7, :] = gain
    gm_ref[7:8, :] = shift
    ds2 = ds3_ref[...] + dx
    dla = ds2.astype(BF16)
    dla_ref[...] = dla
    dctx = nn(dla, wb[3]).astype(BF16)
    row = lax.broadcasted_iota(jnp.int32, (n_tok, n_tok), 0)
    col = lax.broadcasted_iota(jnp.int32, (n_tok, n_tok), 1)
    flip = (row + col == n_tok - 1).astype(F32).astype(BF16)
    for i in range(width // LANES):
        qub, qvb, kb, vb = (r[:, blk(i)] for r in (qu_ref, qv_ref, k_ref, v_ref))
        rb = rel_ref[:, blk(i)]
        dcb = dctx[:, blk(i)]
        got = []
        for h in range(2):
            mask = head_mask(h)
            probs = probs_ref[2 * i + h]
            dprobs = nt(jnp.where(mask, dcb, 0), vb)
            dvh = tn(probs.astype(BF16), dcb)
            ds = probs * (dprobs - jnp.sum(probs * dprobs, axis=-1, keepdims=True))
            ds = (ds.astype(BF16).astype(F32) * HEAD_DIM ** (-0.5)).astype(BF16)
            turned = jnp.concatenate([nn(flip, ds), jnp.zeros((n_tok, n_tok), F32)], axis=1)
            turned = pltpu.roll(turned, 0, 1, stride=1, stride_axis=0).astype(BF16)
            dr = nn(flip, turned).astype(BF16)
            got.append((nn(ds, kb), nn(dr, rb), tn(ds, qub), dvh, tn(dr, qvb)))
        first = head_mask(0)
        dqu, dqv, dk, dv, drel = (jnp.where(first, a, b) for a, b in zip(*got))
        dq = (dqu + dqv).astype(BF16)
        dvb = dv.astype(BF16)
        dq_ref[:, blk(i)] = dq
        dk_ref[:, blk(i)] = dk.astype(BF16)
        dv_ref[:, blk(i)] = dvb
        drel_ref[:, blk(i)] = drel.astype(BF16)
        gi_ref[0:1, blk(i)] = rows_sum(dq.astype(F32))
        gi_ref[1:2, blk(i)] = rows_sum(dvb.astype(F32))
        gi_ref[2:3, blk(i)] = rows_sum(dqu)
        gi_ref[3:4, blk(i)] = rows_sum(dqv)
    gi_ref[4:5, :] = rows_sum(dgi.astype(F32))
    gi_ref[5:6, :] = rows_sum(dgs.astype(F32))
    gi_ref[6:8, :] = gi1_ref[0:2, :]
    gi_ref[8 + taps:40, :] = jnp.zeros((40 - 8 - taps, width), F32)
    gm_ref[0:3, :] = jnp.zeros((3, width), F32)
    gm_ref[8:16, :] = gm1_ref[...]
    s1 = s1_ref[...]
    n1_ref[...] = ln(s1, vm(3), vm(4)).astype(BF16)
    dn = nt(dq_ref[...], wb[0]) + nt(dk_ref[...], wb[1]) + nt(dv_ref[...], wb[2])
    dx, gain, shift = ln_back(s1, vm(3), dn)
    gm_ref[3:4, :] = gain
    gm_ref[4:5, :] = shift
    gm_ref[5:6, :] = rows_sum(dla.astype(F32))
    ds1 = ds2 + dx
    ds1_ref[...] = ds1
    dl_ref[...] = (0.5 * ds1).astype(BF16)


def b3_kernel(dims, fresh, meta, ds1_ref, xa_ref, xb_ref, before_ref, vm_ref, *refs):
    part_a, (dx_ref, n0_ref, db_ref, gm_ref, gf_ref, wa, sem) = refs[:PARTS_A], refs[PARTS_A:]
    if fresh:
        start_a(meta, part_a, wa, sem, ORDER_A, dims)
    vm = lambda r: vm_ref[r:r + 1, :]
    ds1 = ds1_ref[...]
    delta = (0.5 * ds1).astype(BF16)
    before = before_ref[...]
    slope = silu_slope(before)
    x = jnp.where(meta[3] == 1, xb_ref[...].astype(F32), xa_ref[...].astype(F32))
    n0_ref[...] = ln(x, vm(0), vm(1)).astype(BF16)
    wait_weights(wa, sem)
    db = (nn(delta, wa[1]) * slope).astype(BF16)
    db_ref[...] = db
    dx, gain, shift = ln_back(x, vm(0), nt(db, wa[0]))
    gm_ref[0:1, :] = gain
    gm_ref[1:2, :] = shift
    gm_ref[2:3, :] = rows_sum(delta.astype(F32))
    gm_ref[3:8, :] = jnp.zeros((5, gain.shape[1]), F32)
    gf_ref[...] = rows_sum(db.astype(F32))
    dx_ref[...] = (ds1 + dx).astype(BF16)


def back_kernel(dims, groups, meta, *refs):
    n_in = 2 + groups + 16 + PARTS_B
    ins, refs = refs[:n_in], refs[n_in:]
    (xa_ref, xb_ref, before_ref), part_a, refs = refs[:3], refs[3:3 + PARTS_A], refs[3 + PARTS_A:]
    mid, last, scratch, (wa, sem_a) = refs[:13], refs[13:18], refs[18:23], refs[23:]
    start_a(meta, part_a, wa, sem_a, ORDER_A, dims)
    b2_kernel(dims, groups, meta, *ins, *mid, *scratch)
    b3_kernel(dims, False, meta, mid[0], xa_ref, xb_ref, before_ref, ins[groups + 16], *part_a,
              *last, wa, sem_a)


def pieces_of(slots):
    out, top = [], slots
    while top > 1:
        out.append(range(top // 2, top))
        top //= 2
    return out + [range(0, 1)]


def w_kernel(dims, order, count, vectors, meta, *refs):
    slots, tensor, half = dims
    ins, refs = refs[:2 * count], refs[2 * count:]
    vecs, refs = refs[:vectors], refs[vectors:]
    outs, grad = refs[:-1], refs[-1]
    bits = bit_order(order, slots.bit_length() - 1)
    me, core = meta[0], meta[1]
    flat_rows = len(outs[0].shape) == 3
    cols = outs[0].shape[-1]
    rows = ins[0].shape[1] // (2 * half)
    mine = half * rows
    for i in range(count):
        part = ins[2 * i][:, pl.ds(pl.multiple_of(core * mine, mine), mine)]
        grad[i] = tn(part, ins[2 * i + 1][...])
    for out, piece in zip(outs, pieces_of(slots)):
        for at, slot in enumerate(piece):
            f = me ^ slot_mask(slot, bits)
            plane, t = f // tensor, lax.rem(f, tensor)
            row = pl.ds(pl.multiple_of(plane * rows, rows), rows)
            col = pl.ds(pl.multiple_of(t * cols, cols), cols)
            for i in range(count):
                block = grad[i, row, col].astype(BF16)
                if flat_rows:
                    out[at, i * rows:(i + 1) * rows, :] = block
                else:
                    out[at, i] = block
            if vectors:
                gm2_ref, gm0_ref, gi_ref, gf0_ref, gf1_ref = vecs
                width, hidden = gm2_ref.shape[1], gf0_ref.shape[1]
                offs = lane_offsets(core * half + plane, t, dims, width, hidden)
                model = gm2_ref[...] + jnp.concatenate(
                    [gm0_ref[...], jnp.zeros((8, width), F32)], axis=0)
                ff = jnp.concatenate(
                    [gf0_ref[...], gf1_ref[...], jnp.zeros((6, hidden), F32)], axis=0)
                moved = [
                    pltpu.roll(v, v.shape[1] - off, 1)[:, :LANES]
                    for v, off in ((model, offs[0]), (gi_ref[...], offs[1]), (ff, offs[2]))
                ]
                tail = jnp.concatenate([moved[1][32:40], moved[2]], axis=0)
                out[at, count * rows:count * rows + 16, :] = jnp.concatenate(
                    [moved[0], moved[1][0:16], moved[1][16:32], tail], axis=1).astype(BF16)


def vmem(*shape):
    return pl.BlockSpec(memory_space=pltpu.VMEM)


def call(kernel, ins, outs, scratch=(), any_from=None, flops=0, name=None):
    specs = [pl.BlockSpec(memory_space=pltpu.SMEM)]
    for i in range(1, len(ins)):
        away = i in any_from if isinstance(any_from, list) else any_from is not None and i >= any_from
        specs.append(pl.BlockSpec(memory_space=pl.ANY if away else pltpu.VMEM))
    nbytes = sum(a.size * a.dtype.itemsize for a in ins)
    return pl.pallas_call(
        kernel,
        out_shape=[jax.ShapeDtypeStruct(s, d) for s, d in outs],
        in_specs=specs,
        out_specs=[pl.BlockSpec(memory_space=pltpu.VMEM) for _ in outs],
        scratch_shapes=list(scratch),
        compiler_params=pltpu.CompilerParams(vmem_limit_bytes=VMEM_LIMIT),
        cost_estimate=pl.CostEstimate(flops=flops, bytes_accessed=nbytes, transcendentals=0),
        name=name,
    )(*ins)


def permute(value, pairs):
    return lax.ppermute(value, ("pipe", "dp", "tensor"), pairs)


def per_device(n, tensor, boundary, lengths, batch_of, mats, ffw, vec_model, vec_inner, vec_ff):
    half = n // 2
    slots = half * tensor
    nbits = slots.bit_length() - 1
    dims = (slots, tensor, half)
    core = lax.axis_index("pipe")
    d = lax.axis_index("dp")
    t = lax.axis_index("tensor")
    upper = d // half
    plane = lax.rem(d, half)
    me = plane * tensor + t
    is_upper = upper == 1

    def flat(c, dd, tt):
        return (c * n + dd) * tensor + tt

    everyone = [(c, dd, tt) for c in range(2) for dd in range(n) for tt in range(tensor)]

    def home(c, dd, tt):
        u = dd // half
        return (c, dd, tt) if c == u else (1 - c, dd + half if u == 0 else dd - half, tt)

    swap_pairs = [(flat(*e), flat(*home(*e))) for e in everyone]
    core_pairs = [(flat(c, dd, tt), flat(1 - c, dd, tt)) for c, dd, tt in everyone]

    def bit_pairs(b):
        out = []
        for c, dd, tt in everyone:
            f = ((dd % half) * tensor + tt) ^ (1 << b)
            out.append((flat(c, dd, tt), flat(c, dd // half * half + f // tensor, f % tensor)))
        return out

    def spread(held, bits):
        for b in bits:
            held = jnp.concatenate([held, permute(held, bit_pairs(b))], axis=0)
        return held

    def both_cores(pieces):
        return pieces + [permute(p, core_pairs) for p in pieces]

    def gather(block, order):
        bits = bit_order(order, nbits)
        held = spread(permute(block, swap_pairs)[None], bits[:-1])
        return both_cores([held, permute(held, bit_pairs(bits[-1]))])

    rows, fcols, mcols = ffw.shape[2], ffw.shape[3], mats.shape[3]
    ends = boundary[0]
    rows_here, width = ends.shape[1], ends.shape[2]
    length_all = rows_here * tensor
    side, micro = lax.rem(t, 2), t // 2
    first_is = batch_of[0] == 0

    there, back = [], []
    for k in range(2):
        pairs = []
        for h in range(2):
            for dd in range(n):
                for tt in range(tensor):
                    s = dd // half
                    j = (s ^ (tt & 1)) + 2 * k
                    pairs.append((flat(h, dd, tt), flat(j & 1, h * half + dd % half, tt ^ j)))
        there.append(pairs)
        back.append([(b, a) for a, b in pairs])

    def lanes(v):
        return jnp.pad(v[0], ((0, 0), (0, LANES - v.shape[2])))

    vec = jnp.concatenate([
        jnp.pad(lanes(vec_model), ((0, VEC_INNER - vec_model.shape[1]), (0, 0))),
        jnp.pad(lanes(vec_inner), ((0, VEC_FF - VEC_INNER - vec_inner.shape[1]), (0, 0))),
        jnp.pad(lanes(vec_ff), ((0, VEC_ROWS - VEC_FF - vec_ff.shape[1]), (0, 0)))], axis=0)
    vec = vec.reshape(4, 16, LANES).transpose(1, 0, 2).reshape(16, 4 * LANES)
    ordered = jnp.where(first_is, ends, ends[::-1])
    len_ordered = jnp.where(first_is, lengths, lengths[::-1]).astype(BF16)
    parcels = jnp.concatenate(
        [ordered, jnp.broadcast_to(len_ordered[:, None, None], (MB, 16, width))], axis=1)
    sends = jnp.where(micro == 0, parcels, parcels[::-1])
    arrived = jnp.stack([permute(sends[k], there[k]) for k in range(2)])
    others = permute(arrived, core_pairs)
    both = jnp.where(core == 0, jnp.stack([arrived, others], 1), jnp.stack([others, arrived], 1))
    both = jnp.where(lax.rem(t, 2) == 0, both, both[:, ::-1])
    both = jnp.where(micro == 0, both, both[::-1])
    x0 = both[:, :, :rows_here].reshape(length_all, width)
    my_length = both[0, 0, rows_here, 0].astype(jnp.int32)
    meta = jnp.stack([me, core, my_length, upper]).astype(jnp.int32)
    pos = jnp.asarray(sinusoid(length_all, width)).astype(BF16)

    a_all = gather(jnp.concatenate([ffw[0, 0:2].reshape(2 * rows, fcols), vec], axis=0), ORDER_A)
    b_all = gather(mats[0], ORDER_B)
    c_all = gather(ffw[0, 2:4].reshape(2 * rows, fcols), ORDER_C)

    hidden = fcols * tensor
    heads = width // HEAD_DIM
    L, D, H = length_all, width, hidden
    wa_s = pltpu.VMEM((2, D, H), BF16)
    wb_s = pltpu.VMEM((8, D, D), BF16)
    wct_s = pltpu.VMEM((1, D, D), BF16)
    sem_s = pltpu.SemaphoreType.DMA
    sems = pltpu.SemaphoreType.DMA((2,))
    pad_s = pltpu.VMEM((L + 32, D), F32)
    mat_flops = 2 * L * D * D

    vm, vi, vf = call(
        functools.partial(prep_kernel, dims, rows), [meta] + a_all,
        [((16, D), F32), ((40, D), F32), ((8, H), F32)],
        [pltpu.VMEM((2 * slots, 16, 4 * LANES), BF16), sem_s], 1, 0, "vectors",
    )

    def f1(xa, xb):
        return call(
            functools.partial(f1_kernel, dims),
            [meta, xa, xb, vm, vi, vf, pos] + a_all + b_all,
            [((L, D), F32), ((L, D), F32), ((8, D), F32), ((L, D), F32), ((L, H), F32),
             ((L, H), BF16)] + [((L, D), BF16)] * 4
            + [((2 * L, D), BF16), ((heads, L, L), F32), ((L, D), BF16), ((L, D), F32), ((L, D), F32)],
            [wa_s, wb_s, pad_s, sems], 7, 15 * mat_flops, "layer_front",
        )

    rear_out = [((L, D), BF16), ((L, D), F32), ((L, H), F32), ((L, D), F32), ((8, D), F32)]
    back_rear_out = [
        ((L, D), F32), ((L, D), F32), ((8, D), F32), ((L, D), BF16), ((L, H), BF16),
        ((L, D), BF16), ((L, H), BF16), ((L, D), BF16), ((L, D), BF16),
        ((8, D), F32), ((8, D), F32), ((1, H), F32)]
    back_front_out = ([((L, D), F32)] + [((L, D), BF16)] * 8
                      + [((2 * L, D), BF16), ((L, D), BF16), ((16, D), F32), ((40, D), F32)])
    back_first_out = [((L, D), BF16), ((L, D), BF16), ((L, H), BF16), ((8, D), F32), ((1, H), F32)]
    front_scratch = [wb_s, pad_s, pad_s, pltpu.VMEM((L, D), F32), sem_s]

    def f2(s2, filt, stats):
        ins = [meta, s2, filt] + stats + [vm, vi, vf]
        return call(
            functools.partial(f2_kernel, dims, len(stats)), ins + b_all + c_all, rear_out,
            [wct_s, wa_s, sems], len(ins), 9 * mat_flops, "layer_rear",
        )

    def turn(ga, s2, filt, stats):
        ins = [meta, ga, s2, filt] + stats + [vm, vi, vf]
        out = call(
            functools.partial(turn_kernel, dims, len(stats)), ins + b_all + c_all,
            rear_out + back_rear_out, [wct_s, wa_s, sems], len(ins), 18 * mat_flops, "layer_turn",
        )
        return out[:5], out[5:]

    def b1(ga, gb, s4, s3, before, filt, bn):
        return call(
            functools.partial(b1_kernel, dims, True),
            [meta, ga, gb, s4, s3, before, filt, bn, vm, vi] + b_all + c_all, back_rear_out,
            [wct_s, wa_s, sems], 10, 9 * mat_flops, "back_rear",
        )

    def b2(ds3, dnorm, sums, *rest):
        ins = [meta, ds3, dnorm] + sums + list(rest) + [vm, vi]
        return call(
            functools.partial(b2_kernel, dims, len(sums)), ins + b_all, back_front_out,
            front_scratch, len(ins), 16 * mat_flops, "back_front",
        )

    def b3(ds1, xa, xb, before):
        return call(
            functools.partial(b3_kernel, dims, True), [meta, ds1, xa, xb, before, vm] + a_all,
            back_first_out, [wa_s, sem_s], 6, 8 * mat_flops, "back_first",
        )

    def back_whole(ds3, dnorm, sums, rest, xa, xb, before):
        ins = [meta, ds3, dnorm] + sums + list(rest) + [vm, vi]
        away = list(range(len(ins), len(ins) + PARTS_B))
        whole = ins + b_all + [xa, xb, before] + a_all
        away += list(range(len(whole) - PARTS_A, len(whole)))
        return call(
            functools.partial(back_kernel, dims, len(sums)), whole,
            back_front_out + back_first_out, front_scratch + [wa_s, sem_s], away, 24 * mat_flops,
            "back_whole",
        )[len(back_front_out)]

    def w(order, pairs, cols, is_ff, vecs=()):
        count = len(pairs)
        if is_ff:
            shape = (count * rows + (16 if vecs else 0), cols)
        else:
            shape = (count, rows, cols)
        return call(
            functools.partial(w_kernel, dims, order, count, len(vecs)),
            [meta] + [a for pair in pairs for a in pair] + list(vecs),
            [((len(p),) + shape, BF16) for p in pieces_of(slots)],
            [pltpu.VMEM((count, half * rows, cols * tensor), F32)], None, 4 * mat_flops,
            "weight_grads",
        )

    norm_bits = [0] + list(range(tensor.bit_length() - 1, nbits))

    def mask_pairs(mask):
        out = []
        for c, dd, tt in everyone:
            f = ((dd % half) * tensor + tt) ^ mask
            out.append((flat(c, dd, tt), flat(c, dd // half * half + f // tensor, f % tensor)))
        return out

    def norm_group(value):
        held = value[None]
        for first in range(0, len(norm_bits), 2):
            masks = [0]
            for b in norm_bits[first:first + 2]:
                masks = masks + [m ^ (1 << b) for m in masks]
            parts = [held] + [permute(held, mask_pairs(m)) for m in masks[1:]]
            if first + 2 < len(norm_bits):
                held = jnp.concatenate(parts, axis=0)
        return parts

    up_pairs = [(flat(c, dd, tt), flat(c, dd + half, tt)) for c, dd, tt in everyone if dd < half]
    down_pairs = [(b, a) for a, b in up_pairs]

    def forward(xa, xb):
        front = f1(xa, xb)
        stats = norm_group(front[2])
        return front, f2(front[0], front[1], stats)

    _, rear = forward(x0, x0)
    middle = permute(rear[0], up_pairs)
    front = f1(x0, middle)
    (s2, filt, stats, s1, before0, a0, qu, qv, k, v, rel, probs, ctx, gin, gsig) = front
    rear, part1 = turn(x0, s2, filt, norm_group(stats))
    made, s3, before1, s4, bn = rear

    def rest(part):
        return [filt, bn, gin, gsig, s2, s1, qu, qv, k, v, rel, probs, part[9], part[10]]

    dx = back_whole(part1[0], part1[1], norm_group(part1[2]), rest(part1), x0, middle, before0)
    d_middle = permute(dx, down_pairs)
    part1 = b1(x0, d_middle, s4, s3, before1, filt, bn)
    sums = norm_group(part1[2])
    (_, _, _, n3, db1, dl3, a1, dlc, ac, _, _, gf1) = part1

    def round_of(sent, got, order):
        done = len(got)
        total = sent[done].astype(F32)
        size = total.shape[0]
        last = done == nbits
        for g in got:
            total = total + (g[0:1] if last else g[size:2 * size]).astype(F32)
        if last:
            return permute(total[0].astype(BF16), swap_pairs)
        bit = list(reversed(bit_order(order, nbits)))[done]
        return got + [permute(total.astype(BF16), bit_pairs(bit))]

    def scatter(sent, got, order):
        while len(got) <= nbits:
            more = round_of(sent, got, order)
            if len(got) == nbits:
                return more
            got = more

    pieces_c = w(2, [(n3, db1), (dl3, a1)], fcols, True)
    got_c = round_of(pieces_c, [], 2)
    part2 = b2(part1[0], part1[1], sums, *rest(part1))
    (ds1, n2, dgi, dgs, dla, n1, dq, dk, dv, drel, dl0, gm2, gi2) = part2
    got_c[0], n1 = lax.optimization_barrier((got_c[0], n1))
    got_c = round_of(pieces_c, got_c, 2)
    pieces_b = list(w(0, [(n1, dq), (n1, dk), (n1, dv), (dla, ctx), (pos, drel), (n2, dgi),
                          (n2, dgs), (dlc, ac)], mcols, False))
    got_b = round_of(pieces_b, [], 0)
    ds1, pieces_b[1] = lax.optimization_barrier((ds1, pieces_b[1]))
    dx, n0, db0, gm0, gf0 = b3(ds1, x0, middle, before0)
    got_c[1], n0 = lax.optimization_barrier((got_c[1], n0))
    got_c = round_of(pieces_c, got_c, 2)
    pieces_a = w(1, [(n0, db0), (dl0, a0)], fcols, True, (gm2, gm0, gi2, gf0, gf1))
    got_a = round_of(pieces_a, [], 1)
    grad_c = scatter(pieces_c, got_c, 2)
    got_a = round_of(pieces_a, got_a, 1)
    got_a[1], grad_c = lax.optimization_barrier((got_a[1], grad_c))
    grad_b = scatter(pieces_b, got_b, 0)
    grad_a = scatter(pieces_a, got_a, 1)

    stream = jnp.where(is_upper, made, dx).reshape(tensor, rows_here, width)
    pair = jnp.stack([
        permute(lax.dynamic_index_in_dim(stream, t ^ (core + 2 * k), 0, keepdims=False), back[k])
        for k in range(2)])
    pair = jnp.where(micro == 0, pair, pair[::-1])
    ends_out = jnp.where(first_is, pair, pair[::-1])[None]

    grad_a = grad_a.astype(F32)
    gv = grad_a[2 * rows:]
    small = vec_model.shape[2]
    gvi = jnp.concatenate([gv[:, LANES:LANES + small], gv[:, 2 * LANES:2 * LANES + small],
                           gv[:8, 3 * LANES:3 * LANES + small]], axis=0)
    grad_f = jnp.concatenate([grad_a[:2 * rows].reshape(2, rows, fcols),
                              grad_c.astype(F32).reshape(2, rows, fcols)], axis=0)
    grad_m = grad_b.astype(F32)
    return (
        ends_out,
        grad_m[None],
        grad_f[None],
        gv[:vec_model.shape[1], :small][None],
        gvi[:vec_inner.shape[1]][None],
        gv[8:8 + vec_ff.shape[1], 3 * LANES:3 * LANES + vec_ff.shape[2]][None],
    )


def solution(mesh):
    return jax.shard_map(
        functools.partial(per_device, mesh.shape["dp"], mesh.shape["tensor"]),
        mesh=mesh,
        in_specs=(
            P("pipe", "dp", "tensor", None),
            P("dp"),
            P("dp"),
            P("pipe", None, "dp", "tensor"),
            P("pipe", None, "dp", "tensor"),
            P("pipe", None, ("dp", "tensor")),
            P("pipe", None, ("tensor", "dp")),
            P("pipe", None, ("tensor", "dp")),
        ),
        out_specs=(
            P("pipe", "dp", "tensor", None),
            P("pipe", None, "dp", "tensor"),
            P("pipe", None, "dp", "tensor"),
            P("pipe", None, ("dp", "tensor")),
            P("pipe", None, ("tensor", "dp")),
            P("pipe", None, ("tensor", "dp")),
        ),
        check_vma=False,
    )
```

```python
import functools

import jax
import jax.numpy as jnp
import numpy as np
from jax import lax
from jax.experimental import pallas as pl
from jax.experimental.pallas import tpu as pltpu
from jax.sharding import PartitionSpec as P

HEAD_DIM = 64
MB = 2
EPSILON = 1e-05
HUGE_NEG = -1000000000.0
F32 = jnp.float32
BF16 = jnp.bfloat16
LANES = 128
VMEM_LIMIT = 28 * 1024 * 1024

ORDER_A = 0
ORDER_B = 1
ORDER_C = 2
PARTS_A = 4
PARTS_B = 4
PARTS_C = 4


def sinusoid(length, width):
    place = (length - 1 - np.arange(2 * length - 1)).astype(np.float32)
    index = np.arange(width // 2).astype(np.float32)
    rate = np.exp(index * np.float32(-2.0 * np.log(10000.0) / width)).astype(np.float32)
    angle = (place[:, None] * rate[None, :]).astype(np.float64)
    table = np.stack([np.sin(angle), np.cos(angle)], axis=-1).reshape(2 * length - 1, width)
    return np.pad(table, ((0, 1), (0, 0))).astype(np.float32)


def nn(a, b):
    return lax.dot_general(a, b, (((1,), (0,)), ((), ())), preferred_element_type=F32)


def nt(a, b):
    return lax.dot_general(a, b, (((1,), (1,)), ((), ())), preferred_element_type=F32)


def tn(a, b):
    return lax.dot_general(a, b, (((0,), (0,)), ((), ())), preferred_element_type=F32)


def ln_parts(v):
    centre = v - jnp.mean(v, axis=-1, keepdims=True)
    rstd = lax.rsqrt(jnp.mean(centre * centre, axis=-1, keepdims=True) + EPSILON)
    return centre * rstd, rstd


def ln(v, gain, shift):
    xhat, _ = ln_parts(v)
    return xhat * (1.0 + gain) + shift


def ln_back(v, gain, dy):
    xhat, rstd = ln_parts(v)
    g = dy * (1.0 + gain)
    dx = rstd * (
        g - jnp.mean(g, axis=-1, keepdims=True) - xhat * jnp.mean(g * xhat, axis=-1, keepdims=True)
    )
    return dx, rows_sum(dy * xhat), rows_sum(dy)


def rows_sum(v):
    return jnp.sum(v, axis=0, keepdims=True)


def sigmoid(v):
    return 1.0 / (1.0 + jnp.exp(-v))


def silu_slope(v):
    s = sigmoid(v)
    return s * (1.0 + v * (1.0 - s))


def bit_order(order, count):
    return [(order + k) % count for k in range(count)]


def slot_mask(slot, bits):
    out = 0
    for k, b in enumerate(bits):
        out |= ((slot >> k) & 1) << b
    return out


def owners(meta, srcs, order, dims):
    slots, tensor, half = dims
    bits = bit_order(order, slots.bit_length() - 1)
    me, core = meta[0], meta[1]
    out, own = [], len(srcs) // 2
    for side in range(2):
        slot = 0
        for src in srcs[side * own:(side + 1) * own]:
            for at in range(src.shape[0]):
                f = me ^ slot_mask(slot, bits)
                plane, t = f // tensor, lax.rem(f, tensor)
                out.append((src, at, (core if side == 0 else 1 - core) * half + plane, t))
                slot += 1
    return out


def start_a(meta, srcs, dst, sem, order, dims):
    cols = srcs[0].shape[-1]
    rows = dst.shape[1] // (2 * dims[2])
    for which, at, d, t in owners(meta, srcs, order, dims):
        col = pl.ds(pl.multiple_of(t * cols, cols), cols)
        row = pl.ds(pl.multiple_of(d * rows, rows), rows)
        for k in range(2):
            pltpu.make_async_copy(
                which.at[at, pl.ds(k * rows, rows)], dst.at[k, row, col], sem).start()


def start_b(meta, srcs, dst, sem, order, dims, which_mats):
    rows, cols = srcs[0].shape[-2:]
    for which, at, d, t in owners(meta, srcs, order, dims):
        col = pl.ds(pl.multiple_of(t * cols, cols), cols)
        row = pl.ds(pl.multiple_of(d * rows, rows), rows)
        pltpu.make_async_copy(
            which.at[at, pl.ds(*which_mats)], dst.at[:, row, col], sem).start()


def wait_weights(dst, sem):
    pltpu.make_async_copy(dst, dst, sem).wait()


def head_mask(h):
    lane = lax.broadcasted_iota(jnp.int32, (1, LANES), 1)
    return (lane // HEAD_DIM) == h


def blk(i):
    return slice(i * LANES, (i + 1) * LANES)


VEC_MODEL, VEC_INNER, VEC_FF, VEC_ROWS = 0, 16, 56, 64


def lane_offsets(d, t, dims, width, hidden):
    slots, tensor, half = dims
    n = 2 * half
    w_small, w_ff = width // (n * tensor), hidden // (n * tensor)
    return (d * tensor + t) * w_small, (t * n + d) * w_small, (t * n + d) * w_ff


def prep_kernel(dims, rows, meta, *refs):
    srcs, (vm_ref, vi_ref, vf_ref, held, sem) = refs[:PARTS_A], refs[PARTS_A:]
    where = owners(meta, srcs, ORDER_A, dims)
    for i, (which, at, d, t) in enumerate(where):
        pltpu.make_async_copy(which.at[at, pl.ds(2 * rows, 16)], held.at[i], sem).start()
    wait_weights(held, sem)
    width, hidden = vm_ref.shape[1], vf_ref.shape[1]
    totals = None
    for i, (which, at, d, t) in enumerate(where):
        got = held[i].astype(F32)
        pieces = [got[:, blk(k)] for k in range(4)]
        model, inner, ff = pieces[0], jnp.concatenate(pieces[1:3] + [pieces[3][0:8]], axis=0), pieces[3][8:16]
        offs = lane_offsets(d, t, dims, width, hidden)
        placed = []
        for value, off, full in ((model, offs[0], width), (inner, offs[1], width), (ff, offs[2], hidden)):
            value = jnp.concatenate([value, jnp.zeros((value.shape[0], full - LANES), F32)], axis=1)
            placed.append(pltpu.roll(value, off, 1))
        totals = placed if totals is None else [a + b for a, b in zip(totals, placed)]
    vm_ref[...], vi_ref[...], vf_ref[...] = totals


def f1_kernel(dims, ready, meta, xa_ref, xb_ref, vm_ref, vi_ref, vf_ref, pos_ref, *refs):
    part_a, part_b, refs = refs[:PARTS_A], refs[PARTS_A:PARTS_A + PARTS_B], refs[PARTS_A + PARTS_B:]
    (s2_ref, filt_ref, stat_ref, s1_ref, before_ref, act_ref, qu_ref, qv_ref, k_ref, v_ref,
     rel_ref, probs_ref, ctx_ref, gi_ref, gs_ref, wa, wb, pad, sems) = refs
    start_a(meta, part_a, wa, sems.at[0], ORDER_A, dims)
    start_b(meta, part_b, wb, sems.at[1], ORDER_B, dims, (0, 8))
    length = meta[2]
    n_tok = xa_ref.shape[0]
    vm = lambda r: vm_ref[r:r + 1, :]
    vi = lambda r: vi_ref[r:r + 1, :]
    x = jnp.where(meta[3] == 1, xb_ref[...].astype(F32), xa_ref[...].astype(F32))
    wait_weights(wa, sems.at[0])
    n0 = ln(x, vm(0), vm(1)).astype(BF16)
    before = nn(n0, wa[0]) + vf_ref[0:1, :]
    before_ref[...] = before
    active = (before * sigmoid(before)).astype(BF16)
    act_ref[...] = active
    s1 = x + 0.5 * (nt(active, wa[1]) + vm(2))
    s1_ref[...] = s1
    wait_weights(wb, sems.at[1])
    rel_ref[...] = pos_ref[...] if ready else nn(pos_ref[...], wb[4]).astype(BF16)
    n1 = ln(s1, vm(3), vm(4)).astype(BF16)
    q = nn(n1, wb[0]) + vi(0)
    qu_ref[...] = (q + vi(2)).astype(BF16)
    qv_ref[...] = (q + vi(3)).astype(BF16)
    k_ref[...] = nn(n1, wb[1]).astype(BF16)
    v_ref[...] = (nn(n1, wb[2]) + vi(1)).astype(BF16)
    keep = lax.broadcasted_iota(jnp.int32, (1, n_tok), 1) < length
    for i in range(qu_ref.shape[1] // LANES):
        qub, qvb, kb, vb = (r[:, blk(i)] for r in (qu_ref, qv_ref, k_ref, v_ref))
        rb = rel_ref[:, blk(i)]
        halves = []
        for h in range(2):
            mask = head_mask(h)
            direct = nt(jnp.where(mask, qub, 0), kb)
            table = nt(jnp.where(mask, qvb, 0), rb)
            shifted = pltpu.roll(table, n_tok + 1, 1, stride=1, stride_axis=0)[:, :n_tok]
            scores = jnp.where(keep, (direct + shifted) * HEAD_DIM ** (-0.5), HUGE_NEG)
            e = jnp.exp(scores - jnp.max(scores, axis=-1, keepdims=True))
            probs = e / jnp.sum(e, axis=-1, keepdims=True)
            probs_ref[2 * i + h] = probs
            halves.append(nn(probs.astype(BF16), vb))
        ctx_ref[:, blk(i)] = jnp.where(head_mask(0), halves[0], halves[1]).astype(BF16)
    s2 = s1 + nt(ctx_ref[...], wb[3]) + vm(5)
    s2_ref[...] = s2
    n2 = ln(s2, vm(6), vm(7)).astype(BF16)
    gi = nn(n2, wb[5]) + vi(4)
    gs = nn(n2, wb[6]) + vi(5)
    gi_ref[...] = gi
    gs_ref[...] = gs
    inside = (lax.broadcasted_iota(jnp.int32, (n_tok, 1), 0) < length).astype(F32)
    mixed = gi * sigmoid(gs) * inside
    taps = vi_ref.shape[0] - 9
    pad_store(pad, mixed)
    run_taps(pad, vi_ref, [8 + k for k in range(taps)], filt_ref)
    f = filt_ref[...]
    count = length.astype(F32)
    total = rows_sum(inside * f)
    centre = (f - total / count) * inside
    stat_ref[0:1, :] = total
    stat_ref[1:2, :] = rows_sum(centre * centre)
    stat_ref[2:3, :] = jnp.full_like(total, 1.0) * count
    stat_ref[3:8, :] = jnp.zeros((5, total.shape[1]), F32)


def pad_store(pad, value):
    rows = value.shape[0]
    pad[0:16, :] = jnp.zeros((16, value.shape[1]), F32)
    pad[16:16 + rows, :] = value
    pad[16 + rows:32 + rows, :] = jnp.zeros((16, value.shape[1]), F32)


def run_taps(pad, vi_ref, rows, out_ref):
    n_tok = out_ref.shape[0]
    wide = n_tok + 8
    for i in range(out_ref.shape[1] // LANES):
        total = None
        for s in range(8):
            part = None
            for q in range(4):
                e = 8 * q + s - 1
                if 0 <= e < len(rows):
                    term = vi_ref[rows[e]:rows[e] + 1, blk(i)] * pad[8 * q:8 * q + wide, blk(i)]
                    part = term if part is None else part + term
            moved = part[s:s + n_tok]
            total = moved if total is None else total + moved
        out_ref[:, blk(i)] = total


def each_group(refs):
    return [(r, g) for r in refs for g in range(r.shape[0])]


def bn_combine(refs):
    groups = each_group(refs)
    total = sum(r[g, 0:1, :] for r, g in groups)
    count = sum(r[g, 2:3, :] for r, g in groups)
    mean = total / count
    m2 = 0.0
    for r, g in groups:
        n_g = r[g, 2:3, :]
        off = r[g, 0:1, :] / n_g - mean
        m2 = m2 + r[g, 1:2, :] + n_g * off * off
    return mean, lax.rsqrt(m2 / count + EPSILON), count


def f2_kernel(dims, groups, meta, s2_ref, filt_ref, *refs):
    stats, refs = refs[:groups], refs[groups:]
    vm_ref, vi_ref, vf_ref = refs[:3]
    part_b, part_c, refs = refs[3:3 + PARTS_B], refs[3 + PARTS_B:3 + PARTS_B + PARTS_C], refs[3 + PARTS_B + PARTS_C:]
    out_ref, s3_ref, before_ref, s4_ref, bn_ref, wct, wc, sems = refs
    start_b(meta, part_b, wct, sems.at[0], ORDER_B, dims, (7, 1))
    start_a(meta, part_c, wc, sems.at[1], ORDER_C, dims)
    vm = lambda r: vm_ref[r:r + 1, :]
    vi = lambda r: vi_ref[r:r + 1, :]
    mean, inv, count = bn_combine(stats)
    bn_ref[0:1, :] = mean
    bn_ref[1:2, :] = inv
    bn_ref[2:3, :] = count
    bn_ref[3:8, :] = jnp.zeros((5, mean.shape[1]), F32)
    normal = (filt_ref[...] - mean) * inv * (1.0 + vi(6)) + vi(7)
    active = (normal * sigmoid(normal)).astype(BF16)
    wait_weights(wct, sems.at[0])
    s3 = s2_ref[...] + nt(active, wct[0]) + vm(8)
    s3_ref[...] = s3
    n3 = ln(s3, vm(9), vm(10)).astype(BF16)
    wait_weights(wc, sems.at[1])
    before = nn(n3, wc[0]) + vf_ref[1:2, :]
    before_ref[...] = before
    act = (before * sigmoid(before)).astype(BF16)
    s4 = s3 + 0.5 * (nt(act, wc[1]) + vm(11))
    s4_ref[...] = s4
    out_ref[...] = ln(s4, vm(12), vm(13)).astype(BF16)


def b1_kernel(dims, fresh, meta, ga_ref, gb_ref, s4_ref, s3_ref, before_ref, filt_ref, bn_ref,
              vm_ref, vi_ref, *refs):
    part_b, part_c, refs = refs[:PARTS_B], refs[PARTS_B:PARTS_B + PARTS_C], refs[PARTS_B + PARTS_C:]
    (ds3_ref, dnorm_ref, sum_ref, n3_ref, db_ref, dl_ref, a_ref, dlc_ref, ac_ref,
     gm_ref, gi_ref, gf_ref, wct, wc, sems) = refs
    if fresh:
        start_a(meta, part_c, wc, sems.at[1], ORDER_C, dims)
        start_b(meta, part_b, wct, sems.at[0], ORDER_B, dims, (7, 1))
    vm = lambda r: vm_ref[r:r + 1, :]
    vi = lambda r: vi_ref[r:r + 1, :]
    g = jnp.where(meta[3] == 1, ga_ref[...].astype(F32), gb_ref[...].astype(F32))
    ds4, gain4, shift4 = ln_back(s4_ref[...], vm(12), g)
    delta = (0.5 * ds4).astype(BF16)
    dl_ref[...] = delta
    s3 = s3_ref[...]
    n3_ref[...] = ln(s3, vm(9), vm(10)).astype(BF16)
    before = before_ref[...]
    a_ref[...] = (before * sigmoid(before)).astype(BF16)
    if fresh:
        wait_weights(wc, sems.at[1])
    db = (nn(delta, wc[1]) * silu_slope(before)).astype(BF16)
    db_ref[...] = db
    dn = nt(db, wc[0])
    dx, gain3, shift3 = ln_back(s3, vm(9), dn)
    ds3 = ds4 + dx
    ds3_ref[...] = ds3
    dlc = ds3.astype(BF16)
    dlc_ref[...] = dlc
    xhat = (filt_ref[...] - bn_ref[0:1, :]) * bn_ref[1:2, :]
    normal = xhat * (1.0 + vi(6)) + vi(7)
    ac_ref[...] = (normal * sigmoid(normal)).astype(BF16)
    if fresh:
        wait_weights(wct, sems.at[0])
    dnorm = nn(dlc, wct[0]) * silu_slope(normal)
    dnorm_ref[...] = dnorm
    u6 = rows_sum(dnorm * xhat)
    u7 = rows_sum(dnorm)
    sum_ref[0:1, :] = u7 * (1.0 + vi(6))
    sum_ref[1:2, :] = u6 * (1.0 + vi(6))
    sum_ref[2:8, :] = jnp.zeros((6, u6.shape[1]), F32)
    gm_ref[0:1, :] = rows_sum(dlc.astype(F32))
    gm_ref[1:2, :] = gain3
    gm_ref[2:3, :] = shift3
    gm_ref[3:4, :] = rows_sum(delta.astype(F32))
    gm_ref[4:5, :] = gain4
    gm_ref[5:6, :] = shift4
    gm_ref[6:8, :] = jnp.zeros((2, u6.shape[1]), F32)
    gi_ref[0:1, :] = u6
    gi_ref[1:2, :] = u7
    gi_ref[2:8, :] = jnp.zeros((6, u6.shape[1]), F32)
    gf_ref[...] = rows_sum(db.astype(F32))


def turn_kernel(dims, groups, meta, ga_ref, s2_ref, filt_ref, *refs):
    stats, refs = refs[:groups], refs[groups:]
    n_in = 3 + PARTS_B + PARTS_C
    vm_ref, vi_ref, vf_ref, *weights = refs[:n_in]
    refs = refs[n_in:]
    ahead, behind, (wct, wc, sems) = refs[:5], refs[5:17], refs[17:]
    f2_kernel(dims, groups, meta, s2_ref, filt_ref, *stats, vm_ref, vi_ref, vf_ref, *weights,
              *ahead, wct, wc, sems)
    _, s3_ref, before_ref, s4_ref, bn_ref = ahead
    b1_kernel(dims, False, meta, ga_ref, ga_ref, s4_ref, s3_ref, before_ref, filt_ref, bn_ref,
              vm_ref, vi_ref, *weights, *behind, wct, wc, sems)


def b2_kernel(dims, groups, meta, ds3_ref, dnorm_ref, *refs):
    sums, refs = refs[:groups], refs[groups:]
    (filt_ref, bn_ref, gin_ref, gsig_ref, s2_ref, s1_ref, qu_ref, qv_ref, k_ref, v_ref, rel_ref,
     probs_ref, gm1_ref, gi1_ref, vm_ref, vi_ref) = refs[:16]
    part_b, refs = refs[16:16 + PARTS_B], refs[16 + PARTS_B:]
    (ds1_ref, n2_ref, dgi_ref, dgs_ref, dla_ref, n1_ref, dq_ref, dk_ref, dv_ref, drel_ref,
     dl_ref, gm_ref, gi_ref, wb, pad_m, pad_d, dmix, sem) = refs
    start_b(meta, part_b, wb, sem, ORDER_B, dims, (0, 8))
    length = meta[2]
    n_tok, width = ds3_ref.shape
    vm = lambda r: vm_ref[r:r + 1, :]
    vi = lambda r: vi_ref[r:r + 1, :]
    plain = sum(r[g, 0:1, :] for r, g in each_group(sums))
    tilted = sum(r[g, 1:2, :] for r, g in each_group(sums))
    inv = bn_ref[1:2, :]
    xhat = (filt_ref[...] - bn_ref[0:1, :]) * inv
    inside = (lax.broadcasted_iota(jnp.int32, (n_tok, 1), 0) < length).astype(F32)
    dfilt = inv * (
        dnorm_ref[...] * (1.0 + vi(6)) - inside / bn_ref[2:3, :] * (plain + xhat * tilted)
    )
    gin = gin_ref[...]
    sig = sigmoid(gsig_ref[...])
    taps = vi_ref.shape[0] - 9
    pad_store(pad_m, gin * sig * inside)
    pad_store(pad_d, dfilt)
    run_taps(pad_d, vi_ref, [8 + taps - 1 - e for e in range(taps)], dmix)
    wide = n_tok + 8
    for i in range(width // LANES):
        for s in range(8):
            moved = pad_d[16 - s:16 - s + wide, blk(i)]
            for q in range(4):
                e = 8 * q + s - 1
                if 0 <= e < taps:
                    gi_ref[8 + e:9 + e, blk(i)] = rows_sum(
                        moved * pad_m[8 * q:8 * q + wide, blk(i)]
                    )
    dm = dmix[...] * inside
    dgi = (dm * sig).astype(BF16)
    dgs = (dm * gin * sig * (1.0 - sig)).astype(BF16)
    dgi_ref[...] = dgi
    dgs_ref[...] = dgs
    wait_weights(wb, sem)
    s2 = s2_ref[...]
    n2_ref[...] = ln(s2, vm(6), vm(7)).astype(BF16)
    dx, gain, shift = ln_back(s2, vm(6), nt(dgi, wb[5]) + nt(dgs, wb[6]))
    gm_ref[6:7, :] = gain
    gm_ref[7:8, :] = shift
    ds2 = ds3_ref[...] + dx
    dla = ds2.astype(BF16)
    dla_ref[...] = dla
    dctx = nn(dla, wb[3]).astype(BF16)
    row = lax.broadcasted_iota(jnp.int32, (n_tok, n_tok), 0)
    col = lax.broadcasted_iota(jnp.int32, (n_tok, n_tok), 1)
    flip = (row + col == n_tok - 1).astype(F32).astype(BF16)
    for i in range(width // LANES):
        qub, qvb, kb, vb = (r[:, blk(i)] for r in (qu_ref, qv_ref, k_ref, v_ref))
        rb = rel_ref[:, blk(i)]
        dcb = dctx[:, blk(i)]
        got = []
        for h in range(2):
            mask = head_mask(h)
            probs = probs_ref[2 * i + h]
            dprobs = nt(jnp.where(mask, dcb, 0), vb)
            dvh = tn(probs.astype(BF16), dcb)
            ds = probs * (dprobs - jnp.sum(probs * dprobs, axis=-1, keepdims=True))
            ds = (ds.astype(BF16).astype(F32) * HEAD_DIM ** (-0.5)).astype(BF16)
            turned = jnp.concatenate([nn(flip, ds), jnp.zeros((n_tok, n_tok), F32)], axis=1)
            turned = pltpu.roll(turned, 0, 1, stride=1, stride_axis=0).astype(BF16)
            dr = nn(flip, turned).astype(BF16)
            got.append((nn(ds, kb), nn(dr, rb), tn(ds, qub), dvh, tn(dr, qvb)))
        first = head_mask(0)
        dqu, dqv, dk, dv, drel = (jnp.where(first, a, b) for a, b in zip(*got))
        dq = (dqu + dqv).astype(BF16)
        dvb = dv.astype(BF16)
        dq_ref[:, blk(i)] = dq
        dk_ref[:, blk(i)] = dk.astype(BF16)
        dv_ref[:, blk(i)] = dvb
        drel_ref[:, blk(i)] = drel.astype(BF16)
        gi_ref[0:1, blk(i)] = rows_sum(dq.astype(F32))
        gi_ref[1:2, blk(i)] = rows_sum(dvb.astype(F32))
        gi_ref[2:3, blk(i)] = rows_sum(dqu)
        gi_ref[3:4, blk(i)] = rows_sum(dqv)
    gi_ref[4:5, :] = rows_sum(dgi.astype(F32))
    gi_ref[5:6, :] = rows_sum(dgs.astype(F32))
    gi_ref[6:8, :] = gi1_ref[0:2, :]
    gi_ref[8 + taps:40, :] = jnp.zeros((40 - 8 - taps, width), F32)
    gm_ref[0:3, :] = jnp.zeros((3, width), F32)
    gm_ref[8:16, :] = gm1_ref[...]
    s1 = s1_ref[...]
    n1_ref[...] = ln(s1, vm(3), vm(4)).astype(BF16)
    dn = nt(dq_ref[...], wb[0]) + nt(dk_ref[...], wb[1]) + nt(dv_ref[...], wb[2])
    dx, gain, shift = ln_back(s1, vm(3), dn)
    gm_ref[3:4, :] = gain
    gm_ref[4:5, :] = shift
    gm_ref[5:6, :] = rows_sum(dla.astype(F32))
    ds1 = ds2 + dx
    ds1_ref[...] = ds1
    dl_ref[...] = (0.5 * ds1).astype(BF16)


def b3_kernel(dims, fresh, meta, ds1_ref, xa_ref, xb_ref, before_ref, vm_ref, *refs):
    part_a, (dx_ref, n0_ref, db_ref, gm_ref, gf_ref, wa, sem) = refs[:PARTS_A], refs[PARTS_A:]
    if fresh:
        start_a(meta, part_a, wa, sem, ORDER_A, dims)
    vm = lambda r: vm_ref[r:r + 1, :]
    ds1 = ds1_ref[...]
    delta = (0.5 * ds1).astype(BF16)
    before = before_ref[...]
    slope = silu_slope(before)
    x = jnp.where(meta[3] == 1, xb_ref[...].astype(F32), xa_ref[...].astype(F32))
    n0_ref[...] = ln(x, vm(0), vm(1)).astype(BF16)
    wait_weights(wa, sem)
    db = (nn(delta, wa[1]) * slope).astype(BF16)
    db_ref[...] = db
    dx, gain, shift = ln_back(x, vm(0), nt(db, wa[0]))
    gm_ref[0:1, :] = gain
    gm_ref[1:2, :] = shift
    gm_ref[2:3, :] = rows_sum(delta.astype(F32))
    gm_ref[3:8, :] = jnp.zeros((5, gain.shape[1]), F32)
    gf_ref[...] = rows_sum(db.astype(F32))
    dx_ref[...] = (ds1 + dx).astype(BF16)


def back_kernel(dims, groups, meta, *refs):
    n_in = 2 + groups + 16 + PARTS_B
    ins, refs = refs[:n_in], refs[n_in:]
    (xa_ref, xb_ref, before_ref), part_a, refs = refs[:3], refs[3:3 + PARTS_A], refs[3 + PARTS_A:]
    mid, last, scratch, (wa, sem_a) = refs[:13], refs[13:18], refs[18:23], refs[23:]
    start_a(meta, part_a, wa, sem_a, ORDER_A, dims)
    b2_kernel(dims, groups, meta, *ins, *mid, *scratch)
    b3_kernel(dims, False, meta, mid[0], xa_ref, xb_ref, before_ref, ins[groups + 16], *part_a,
              *last, wa, sem_a)


def pieces_of(slots):
    out, top = [], slots
    while top > 1:
        out.append(range(top // 2, top))
        top //= 2
    return out + [range(0, 1)]


def w_kernel(dims, order, count, vectors, meta, *refs):
    slots, tensor, half = dims
    ins, refs = refs[:2 * count], refs[2 * count:]
    vecs, refs = refs[:vectors], refs[vectors:]
    outs, grad = refs[:-1], refs[-1]
    bits = bit_order(order, slots.bit_length() - 1)
    me, core = meta[0], meta[1]
    flat_rows = len(outs[0].shape) == 3
    cols = outs[0].shape[-1]
    rows = ins[0].shape[1] // (2 * half)
    mine = half * rows
    for i in range(count):
        part = ins[2 * i][:, pl.ds(pl.multiple_of(core * mine, mine), mine)]
        grad[i] = tn(part, ins[2 * i + 1][...])
    for out, piece in zip(outs, pieces_of(slots)):
        for at, slot in enumerate(piece):
            f = me ^ slot_mask(slot, bits)
            plane, t = f // tensor, lax.rem(f, tensor)
            row = pl.ds(pl.multiple_of(plane * rows, rows), rows)
            col = pl.ds(pl.multiple_of(t * cols, cols), cols)
            for i in range(count):
                block = grad[i, row, col].astype(BF16)
                if flat_rows:
                    out[at, i * rows:(i + 1) * rows, :] = block
                else:
                    out[at, i] = block
            if vectors:
                gm2_ref, gm0_ref, gi_ref, gf0_ref, gf1_ref = vecs
                width, hidden = gm2_ref.shape[1], gf0_ref.shape[1]
                offs = lane_offsets(core * half + plane, t, dims, width, hidden)
                model = gm2_ref[...] + jnp.concatenate(
                    [gm0_ref[...], jnp.zeros((8, width), F32)], axis=0)
                ff = jnp.concatenate(
                    [gf0_ref[...], gf1_ref[...], jnp.zeros((6, hidden), F32)], axis=0)
                moved = [
                    pltpu.roll(v, v.shape[1] - off, 1)[:, :LANES]
                    for v, off in ((model, offs[0]), (gi_ref[...], offs[1]), (ff, offs[2]))
                ]
                tail = jnp.concatenate([moved[1][32:40], moved[2]], axis=0)
                out[at, count * rows:count * rows + 16, :] = jnp.concatenate(
                    [moved[0], moved[1][0:16], moved[1][16:32], tail], axis=1).astype(BF16)


def vmem(*shape):
    return pl.BlockSpec(memory_space=pltpu.VMEM)


def call(kernel, ins, outs, scratch=(), any_from=None, flops=0, name=None):
    specs = [pl.BlockSpec(memory_space=pltpu.SMEM)]
    for i in range(1, len(ins)):
        away = i in any_from if isinstance(any_from, list) else any_from is not None and i >= any_from
        specs.append(pl.BlockSpec(memory_space=pl.ANY if away else pltpu.VMEM))
    nbytes = sum(a.size * a.dtype.itemsize for a in ins)
    return pl.pallas_call(
        kernel,
        out_shape=[jax.ShapeDtypeStruct(s, d) for s, d in outs],
        in_specs=specs,
        out_specs=[pl.BlockSpec(memory_space=pltpu.VMEM) for _ in outs],
        scratch_shapes=list(scratch),
        compiler_params=pltpu.CompilerParams(vmem_limit_bytes=VMEM_LIMIT),
        cost_estimate=pl.CostEstimate(flops=flops, bytes_accessed=nbytes, transcendentals=0),
        name=name,
    )(*ins)


def permute(value, pairs):
    return lax.ppermute(value, ("pipe", "dp", "tensor"), pairs)


def per_device(n, tensor, boundary, lengths, batch_of, mats, ffw, vec_model, vec_inner, vec_ff):
    half = n // 2
    slots = half * tensor
    nbits = slots.bit_length() - 1
    dims = (slots, tensor, half)
    core = lax.axis_index("pipe")
    d = lax.axis_index("dp")
    t = lax.axis_index("tensor")
    upper = d // half
    plane = lax.rem(d, half)
    me = plane * tensor + t
    is_upper = upper == 1

    def flat(c, dd, tt):
        return (c * n + dd) * tensor + tt

    everyone = [(c, dd, tt) for c in range(2) for dd in range(n) for tt in range(tensor)]

    def home(c, dd, tt):
        u = dd // half
        return (c, dd, tt) if c == u else (1 - c, dd + half if u == 0 else dd - half, tt)

    swap_pairs = [(flat(*e), flat(*home(*e))) for e in everyone]
    core_pairs = [(flat(c, dd, tt), flat(1 - c, dd, tt)) for c, dd, tt in everyone]

    def bit_pairs(b):
        out = []
        for c, dd, tt in everyone:
            f = ((dd % half) * tensor + tt) ^ (1 << b)
            out.append((flat(c, dd, tt), flat(c, dd // half * half + f // tensor, f % tensor)))
        return out

    def spread(held, bits):
        for b in bits:
            held = jnp.concatenate([held, permute(held, bit_pairs(b))], axis=0)
        return held

    def both_cores(pieces):
        return pieces + [permute(p, core_pairs) for p in pieces]

    def gather(block, order):
        bits = bit_order(order, nbits)
        held = spread(permute(block, swap_pairs)[None], bits[:-1])
        return both_cores([held, permute(held, bit_pairs(bits[-1]))])

    rows, fcols, mcols = ffw.shape[2], ffw.shape[3], mats.shape[3]
    ends = boundary[0]
    rows_here, width = ends.shape[1], ends.shape[2]
    length_all = rows_here * tensor
    side, micro = lax.rem(t, 2), t // 2
    first_is = batch_of[0] == 0

    there, back = [], []
    for k in range(2):
        pairs = []
        for h in range(2):
            for dd in range(n):
                for tt in range(tensor):
                    s = dd // half
                    j = (s ^ (tt & 1)) + 2 * k
                    pairs.append((flat(h, dd, tt), flat(j & 1, h * half + dd % half, tt ^ j)))
        there.append(pairs)
        back.append([(b, a) for a, b in pairs])

    def lanes(v):
        return jnp.pad(v[0], ((0, 0), (0, LANES - v.shape[2])))

    vec = jnp.concatenate([
        jnp.pad(lanes(vec_model), ((0, VEC_INNER - vec_model.shape[1]), (0, 0))),
        jnp.pad(lanes(vec_inner), ((0, VEC_FF - VEC_INNER - vec_inner.shape[1]), (0, 0))),
        jnp.pad(lanes(vec_ff), ((0, VEC_ROWS - VEC_FF - vec_ff.shape[1]), (0, 0)))], axis=0)
    vec = vec.reshape(4, 16, LANES).transpose(1, 0, 2).reshape(16, 4 * LANES)
    ordered = jnp.where(first_is, ends, ends[::-1])
    len_ordered = jnp.where(first_is, lengths, lengths[::-1]).astype(BF16)
    parcels = jnp.concatenate(
        [ordered, jnp.broadcast_to(len_ordered[:, None, None], (MB, 16, width))], axis=1)
    sends = jnp.where(micro == 0, parcels, parcels[::-1])
    arrived = jnp.stack([permute(sends[k], there[k]) for k in range(2)])
    others = permute(arrived, core_pairs)
    both = jnp.where(core == 0, jnp.stack([arrived, others], 1), jnp.stack([others, arrived], 1))
    both = jnp.where(lax.rem(t, 2) == 0, both, both[:, ::-1])
    both = jnp.where(micro == 0, both, both[::-1])
    x0 = both[:, :, :rows_here].reshape(length_all, width)
    my_length = both[0, 0, rows_here, 0].astype(jnp.int32)
    meta = jnp.stack([me, core, my_length, upper]).astype(jnp.int32)
    pos = jnp.asarray(sinusoid(length_all, width)).astype(BF16)

    a_all = gather(jnp.concatenate([ffw[0, 0:2].reshape(2 * rows, fcols), vec], axis=0), ORDER_A)
    b_all = gather(mats[0], ORDER_B)
    c_all = gather(ffw[0, 2:4].reshape(2 * rows, fcols), ORDER_C)

    hidden = fcols * tensor
    heads = width // HEAD_DIM
    L, D, H = length_all, width, hidden
    wa_s = pltpu.VMEM((2, D, H), BF16)
    wb_s = pltpu.VMEM((8, D, D), BF16)
    wct_s = pltpu.VMEM((1, D, D), BF16)
    sem_s = pltpu.SemaphoreType.DMA
    sems = pltpu.SemaphoreType.DMA((2,))
    pad_s = pltpu.VMEM((L + 32, D), F32)
    mat_flops = 2 * L * D * D

    vm, vi, vf = call(
        functools.partial(prep_kernel, dims, rows), [meta] + a_all,
        [((16, D), F32), ((40, D), F32), ((8, H), F32)],
        [pltpu.VMEM((2 * slots, 16, 4 * LANES), BF16), sem_s], 1, 0, "vectors",
    )

    def f1(xa, xb, place, ready):
        return call(
            functools.partial(f1_kernel, dims, ready),
            [meta, xa, xb, vm, vi, vf, place] + a_all + b_all,
            [((L, D), F32), ((L, D), F32), ((8, D), F32), ((L, D), F32), ((L, H), F32),
             ((L, H), BF16)] + [((L, D), BF16)] * 4
            + [((2 * L, D), BF16), ((heads, L, L), F32), ((L, D), BF16), ((L, D), F32), ((L, D), F32)],
            [wa_s, wb_s, pad_s, sems], 7, 15 * mat_flops, "layer_front",
        )

    rear_out = [((L, D), BF16), ((L, D), F32), ((L, H), F32), ((L, D), F32), ((8, D), F32)]
    back_rear_out = [
        ((L, D), F32), ((L, D), F32), ((8, D), F32), ((L, D), BF16), ((L, H), BF16),
        ((L, D), BF16), ((L, H), BF16), ((L, D), BF16), ((L, D), BF16),
        ((8, D), F32), ((8, D), F32), ((1, H), F32)]
    back_front_out = ([((L, D), F32)] + [((L, D), BF16)] * 8
                      + [((2 * L, D), BF16), ((L, D), BF16), ((16, D), F32), ((40, D), F32)])
    back_first_out = [((L, D), BF16), ((L, D), BF16), ((L, H), BF16), ((8, D), F32), ((1, H), F32)]
    front_scratch = [wb_s, pad_s, pad_s, pltpu.VMEM((L, D), F32), sem_s]

    def f2(s2, filt, stats):
        ins = [meta, s2, filt] + stats + [vm, vi, vf]
        return call(
            functools.partial(f2_kernel, dims, len(stats)), ins + b_all + c_all, rear_out,
            [wct_s, wa_s, sems], len(ins), 9 * mat_flops, "layer_rear",
        )

    def turn(ga, s2, filt, stats):
        ins = [meta, ga, s2, filt] + stats + [vm, vi, vf]
        out = call(
            functools.partial(turn_kernel, dims, len(stats)), ins + b_all + c_all,
            rear_out + back_rear_out, [wct_s, wa_s, sems], len(ins), 18 * mat_flops, "layer_turn",
        )
        return out[:5], out[5:]

    def b1(ga, gb, s4, s3, before, filt, bn):
        return call(
            functools.partial(b1_kernel, dims, True),
            [meta, ga, gb, s4, s3, before, filt, bn, vm, vi] + b_all + c_all, back_rear_out,
            [wct_s, wa_s, sems], 10, 9 * mat_flops, "back_rear",
        )

    def b2(ds3, dnorm, sums, *rest):
        ins = [meta, ds3, dnorm] + sums + list(rest) + [vm, vi]
        return call(
            functools.partial(b2_kernel, dims, len(sums)), ins + b_all, back_front_out,
            front_scratch, len(ins), 16 * mat_flops, "back_front",
        )

    def b3(ds1, xa, xb, before):
        return call(
            functools.partial(b3_kernel, dims, True), [meta, ds1, xa, xb, before, vm] + a_all,
            back_first_out, [wa_s, sem_s], 6, 8 * mat_flops, "back_first",
        )

    def back_whole(ds3, dnorm, sums, rest, xa, xb, before):
        ins = [meta, ds3, dnorm] + sums + list(rest) + [vm, vi]
        away = list(range(len(ins), len(ins) + PARTS_B))
        whole = ins + b_all + [xa, xb, before] + a_all
        away += list(range(len(whole) - PARTS_A, len(whole)))
        return call(
            functools.partial(back_kernel, dims, len(sums)), whole,
            back_front_out + back_first_out, front_scratch + [wa_s, sem_s], away, 24 * mat_flops,
            "back_whole",
        )[len(back_front_out)]

    def w(order, pairs, cols, is_ff, vecs=()):
        count = len(pairs)
        if is_ff:
            shape = (count * rows + (16 if vecs else 0), cols)
        else:
            shape = (count, rows, cols)
        return call(
            functools.partial(w_kernel, dims, order, count, len(vecs)),
            [meta] + [a for pair in pairs for a in pair] + list(vecs),
            [((len(p),) + shape, BF16) for p in pieces_of(slots)],
            [pltpu.VMEM((count, half * rows, cols * tensor), F32)], None, 4 * mat_flops,
            "weight_grads",
        )

    norm_bits = [0] + list(range(tensor.bit_length() - 1, nbits))

    def mask_pairs(mask):
        out = []
        for c, dd, tt in everyone:
            f = ((dd % half) * tensor + tt) ^ mask
            out.append((flat(c, dd, tt), flat(c, dd // half * half + f // tensor, f % tensor)))
        return out

    def norm_group(value):
        held = value[None]
        for first in range(0, len(norm_bits), 2):
            masks = [0]
            for b in norm_bits[first:first + 2]:
                masks = masks + [m ^ (1 << b) for m in masks]
            parts = [held] + [permute(held, mask_pairs(m)) for m in masks[1:]]
            if first + 2 < len(norm_bits):
                held = jnp.concatenate(parts, axis=0)
        return parts

    up_pairs = [(flat(c, dd, tt), flat(c, dd + half, tt)) for c, dd, tt in everyone if dd < half]
    down_pairs = [(b, a) for a, b in up_pairs]

    def forward(xa, xb):
        front = f1(xa, xb, pos, False)
        stats = norm_group(front[2])
        return front, f2(front[0], front[1], stats)

    front, rear = forward(x0, x0)
    middle = permute(rear[0], up_pairs)
    front = f1(x0, middle, front[10], True)
    (s2, filt, stats, s1, before0, a0, qu, qv, k, v, rel, probs, ctx, gin, gsig) = front
    rear, part1 = turn(x0, s2, filt, norm_group(stats))
    made, s3, before1, s4, bn = rear

    def rest(part):
        return [filt, bn, gin, gsig, s2, s1, qu, qv, k, v, rel, probs, part[9], part[10]]

    dx = back_whole(part1[0], part1[1], norm_group(part1[2]), rest(part1), x0, middle, before0)
    d_middle = permute(dx, down_pairs)
    part1 = b1(x0, d_middle, s4, s3, before1, filt, bn)
    sums = norm_group(part1[2])
    (_, _, _, n3, db1, dl3, a1, dlc, ac, _, _, gf1) = part1

    def round_of(sent, got, order):
        done = len(got)
        total = sent[done].astype(F32)
        size = total.shape[0]
        last = done == nbits
        for g in got:
            total = total + (g[0:1] if last else g[size:2 * size]).astype(F32)
        if last:
            return permute(total[0].astype(BF16), swap_pairs)
        bit = list(reversed(bit_order(order, nbits)))[done]
        return got + [permute(total.astype(BF16), bit_pairs(bit))]

    def scatter(sent, got, order):
        while len(got) <= nbits:
            more = round_of(sent, got, order)
            if len(got) == nbits:
                return more
            got = more

    pieces_c = w(2, [(n3, db1), (dl3, a1)], fcols, True)
    got_c = round_of(pieces_c, [], 2)
    part2 = b2(part1[0], part1[1], sums, *rest(part1))
    (ds1, n2, dgi, dgs, dla, n1, dq, dk, dv, drel, dl0, gm2, gi2) = part2
    got_c[0], n1 = lax.optimization_barrier((got_c[0], n1))
    got_c = round_of(pieces_c, got_c, 2)
    pieces_b = list(w(0, [(n1, dq), (n1, dk), (n1, dv), (dla, ctx), (pos, drel), (n2, dgi),
                          (n2, dgs), (dlc, ac)], mcols, False))
    got_b = round_of(pieces_b, [], 0)
    ds1, pieces_b[1] = lax.optimization_barrier((ds1, pieces_b[1]))
    dx, n0, db0, gm0, gf0 = b3(ds1, x0, middle, before0)
    got_c[1], n0 = lax.optimization_barrier((got_c[1], n0))
    got_c = round_of(pieces_c, got_c, 2)
    pieces_a = w(1, [(n0, db0), (dl0, a0)], fcols, True, (gm2, gm0, gi2, gf0, gf1))
    got_a = round_of(pieces_a, [], 1)
    grad_c = scatter(pieces_c, got_c, 2)
    got_a = round_of(pieces_a, got_a, 1)
    got_a[1], grad_c = lax.optimization_barrier((got_a[1], grad_c))
    grad_b = scatter(pieces_b, got_b, 0)
    grad_a = scatter(pieces_a, got_a, 1)

    stream = jnp.where(is_upper, made, dx).reshape(tensor, rows_here, width)
    pair = jnp.stack([
        permute(lax.dynamic_index_in_dim(stream, t ^ (core + 2 * k), 0, keepdims=False), back[k])
        for k in range(2)])
    pair = jnp.where(micro == 0, pair, pair[::-1])
    ends_out = jnp.where(first_is, pair, pair[::-1])[None]

    grad_a = grad_a.astype(F32)
    gv = grad_a[2 * rows:]
    small = vec_model.shape[2]
    gvi = jnp.concatenate([gv[:, LANES:LANES + small], gv[:, 2 * LANES:2 * LANES + small],
                           gv[:8, 3 * LANES:3 * LANES + small]], axis=0)
    grad_f = jnp.concatenate([grad_a[:2 * rows].reshape(2, rows, fcols),
                              grad_c.astype(F32).reshape(2, rows, fcols)], axis=0)
    grad_m = grad_b.astype(F32)
    return (
        ends_out,
        grad_m[None],
        grad_f[None],
        gv[:vec_model.shape[1], :small][None],
        gvi[:vec_inner.shape[1]][None],
        gv[8:8 + vec_ff.shape[1], 3 * LANES:3 * LANES + vec_ff.shape[2]][None],
    )


def solution(mesh):
    return jax.shard_map(
        functools.partial(per_device, mesh.shape["dp"], mesh.shape["tensor"]),
        mesh=mesh,
        in_specs=(
            P("pipe", "dp", "tensor", None),
            P("dp"),
            P("dp"),
            P("pipe", None, "dp", "tensor"),
            P("pipe", None, "dp", "tensor"),
            P("pipe", None, ("dp", "tensor")),
            P("pipe", None, ("tensor", "dp")),
            P("pipe", None, ("tensor", "dp")),
        ),
        out_specs=(
            P("pipe", "dp", "tensor", None),
            P("pipe", None, "dp", "tensor"),
            P("pipe", None, "dp", "tensor"),
            P("pipe", None, ("dp", "tensor")),
            P("pipe", None, ("tensor", "dp")),
            P("pipe", None, ("tensor", "dp")),
        ),
        check_vma=False,
    )
```
